32 devices in a mesh: dp: 16 (over z, x, core), seq: 2 (over y).
Axes of the slice: x: 2, y: 2, z: 4, core: 2. Of those that a mesh axis runs over, the one named last changes fastest.
Arguments:
- tokens: bfloat16 [64, 1024, 768], P('dp', 'seq'), may hold values from -6 to 6
- weight_qkv: float32 [768, 2304], P('dp'), may hold values from -0.3125 to 0.3125
- bias_qv: float32 [1536], P('dp'), may hold values from -3 to 3
- weight_out: float32 [768, 768], P('dp'), may hold values from -0.4375 to 0.4375
- bias_out: float32 [768], P('dp'), may hold values from -3 to 3
- gain_attn: float32 [768], P('dp'), may hold values from 0.25 to 1.75
- shift_attn: float32 [768], P('dp'), may hold values from -3 to 3
- weight_in: float32 [768, 3072], P('dp'), may hold values from -0.21875 to 0.21875
- bias_in: float32 [3072], P('dp'), may hold values from -3 to 3
- weight_ffo: float32 [3072, 768], P('dp'), may hold values from -0.109375 to 0.109375
- bias_ffo: float32 [768], P('dp'), may hold values from -3 to 3
- gain_ffn: float32 [768], P('dp'), may hold values from 0.25 to 1.75
- shift_ffn: float32 [768], P('dp'), may hold values from -3 to 3
- lengths: int32 [64, 8], P('dp'), may hold values from 0 to 512, as said below
- cotangent: bfloat16 [64, 1024, 768], P('dp', 'seq'), may hold values from -6 to 6
Outputs:
- output: bfloat16 [64, 1024, 768], P('dp', 'seq')
- input_grad: bfloat16 [64, 1024, 768], P('dp', 'seq')
- grad_weight_qkv: float32 [768, 2304], P('dp')
- grad_bias_qv: float32 [1536], P('dp')
- grad_weight_out: float32 [768, 768], P('dp')
- grad_bias_out: float32 [768], P('dp')
- grad_gain_attn: float32 [768], P('dp')
- grad_shift_attn: float32 [768], P('dp')
- grad_weight_in: float32 [768, 3072], P('dp')
- grad_bias_in: float32 [3072], P('dp')
- grad_weight_ffo: float32 [3072, 768], P('dp')
- grad_bias_ffo: float32 [768], P('dp')
- grad_gain_ffn: float32 [768], P('dp')
- grad_shift_ffn: float32 [768], P('dp')
The draws below stay inside these ranges and needn't reach their ends.
Inputs may be any that keep to these rules, and one draw needn't show every extreme that they name: Each row's lengths sum to 1024. In each aligned group of 4 rows one row, which one drawn from the seed, holds three passages of 256, 512 and 256 tokens with its other entries 0; every other row holds 8 passages of 1 or more and fewer than 256 tokens each.
All inputs are finite; a program needn't handle non-finite values.
Results may differ from the reference program's by a relative error of at most 0.02.
The reference program's roundings to bfloat16 on the way count: a program that leaves them out, or rounds other values in their place, can miss the bound.
Values may be sent and summed in bfloat16 or wider, within the bound.
No kernel may reach another device: no remote copies, remote signals or barrier semaphores. Data moves between devices by JAX's collectives and lax.ppermute only.
A program may use at most 448 MiB of HBM per device.

```python
import math
from functools import partial
import jax
import jax.numpy as jnp
from jax import lax

D = 768
H = 12
FF = 3072
HD = 64
ROW_LEN = 1024
NDOC = 8
ROWS_DEV = 4
ROWS = 64


def draw_lengths(key, part):
    key = jax.random.fold_in(key, 11)
    cut_key, pick_key = jax.random.split(key)
    half_len = ROW_LEN // 2
    quarter_len = ROW_LEN // 4
    cell_len = ROW_LEN // NDOC
    offsets = jax.random.randint(cut_key, (ROWS, NDOC - 1), 0, cell_len).astype(jnp.int32)
    anchors = (jnp.arange(1, NDOC, dtype=jnp.int32) * cell_len)[None, :]
    cuts = anchors + offsets
    bounds = jnp.concatenate([jnp.zeros((ROWS, 1), jnp.int32), cuts, jnp.full((ROWS, 1), ROW_LEN, jnp.int32)], axis=1)
    spans = bounds[:, 1:] - bounds[:, :-1]
    group_count = ROWS // 4
    chosen = jax.random.randint(pick_key, (group_count,), 0, 4).astype(jnp.int32)
    row_index = jnp.arange(ROWS, dtype=jnp.int32)
    single_row = row_index % 4 == chosen[row_index // 4]
    slot = jnp.arange(NDOC, dtype=jnp.int32)
    three = jnp.where(slot == 0, quarter_len, jnp.where(slot == 1, half_len, jnp.where(slot == 2, ROW_LEN - quarter_len - half_len, 0))).astype(jnp.int32)
    return jnp.where(single_row[:, None], three[None, :], spans).astype(jnp.int32)


def steps_of(stream_key, dims, cuts, low, high):
    factor_of = 1.0
    for axis_at, shards_of in cuts:
        heights = jax.random.uniform(jax.random.fold_in(jax.random.fold_in(stream_key, 6), axis_at), (shards_of,), jnp.float32, low / len(cuts), high / len(cuts))
        factor_of = factor_of * jnp.repeat(jnp.exp(heights), dims[axis_at] // shards_of).reshape((-1,) + (1,) * (len(dims) - 1 - axis_at))
    return factor_of


def noise(rng, dims, width, limit, shards=(), kind=jnp.bfloat16):
    values = jax.random.normal(rng, dims, jnp.float32) * width
    if len(shards) > 0:
        values = steps_of(rng, dims, shards, -0.22, 0.18) * values
    return jnp.clip(values, min=-limit, max=limit).astype(kind)


def setup_inputs(seed: int = 0) -> dict:
    arg_keys = jax.random.split(jax.random.key(seed), 16)
    return {
        "tokens": noise(arg_keys[0], (ROWS, ROW_LEN, D), 1.0, 6.0, ((0, 16), (1, 2))),
        "weight_qkv": noise(arg_keys[1], (D, 3 * D), (D // 2) ** -0.5, 0.3125, ((0, 16),), jnp.float32),
        "bias_qv": noise(arg_keys[2], (2 * D,), 0.5, 3.0, ((0, 16),), jnp.float32),
        "weight_out": noise(arg_keys[3], (D, D), (D // 4) ** -0.5, 0.4375, ((0, 16),), jnp.float32),
        "bias_out": noise(arg_keys[4], (D,), 0.5, 3.0, ((0, 16),), jnp.float32),
        "gain_attn": jnp.clip(1.0 + 0.15 * jax.random.normal(arg_keys[5], (D,), jnp.float32), 0.25, 1.75),
        "shift_attn": noise(arg_keys[6], (D,), 0.5, 3.0, ((0, 16),), jnp.float32),
        "weight_in": noise(arg_keys[7], (D, FF), D ** -0.5, 0.21875, ((0, 16),), jnp.float32),
        "bias_in": noise(arg_keys[8], (FF,), 0.5, 3.0, ((0, 16),), jnp.float32),
        "weight_ffo": noise(arg_keys[9], (FF, D), FF ** -0.5, 0.109375, ((0, 16),), jnp.float32),
        "bias_ffo": noise(arg_keys[10], (D,), 0.5, 3.0, ((0, 16),), jnp.float32),
        "gain_ffn": jnp.clip(1.0 + 0.15 * jax.random.normal(arg_keys[11], (D,), jnp.float32), 0.25, 1.75),
        "shift_ffn": noise(arg_keys[12], (D,), 0.5, 3.0, ((0, 16),), jnp.float32),
        "lengths": draw_lengths(jax.random.fold_in(arg_keys[15], 71), 0),
        "cotangent": noise(arg_keys[14], (ROWS, ROW_LEN, D), 1.0, 6.0, ((0, 16), (1, 2))),
    }


@jax.custom_vjp
def low(v):
    return lax.optimization_barrier(v.astype(jnp.bfloat16)).astype(jnp.float32)

@jax.custom_vjp
def low_back(v):
    return v

def low_keep(v):
    return (low(v), None)

def low_pass(kept, grad):
    return (grad,)

def back_keep(v):
    return (v, None)

def back_low(kept, grad):
    return (low(grad),)
low.defvjp(low_keep, low_pass)
low_back.defvjp(back_keep, back_low)
highest = lax.Precision.HIGHEST

def rounded(value):
    return low_back(low(value))

def layer_norm(values, gain, shift):
    centred = values - lax.optimization_barrier(jnp.mean(values, axis=-1, keepdims=True))
    spread = lax.optimization_barrier(jnp.mean(centred * centred, axis=-1, keepdims=True))
    return centred * lax.rsqrt(spread + 1e-06) * gain + shift

def attend_row(inputs):
    queries, keys_row, values_row, segment_row = inputs
    score_scale = 1.0 / math.sqrt(HD)
    scores = low_back(jnp.einsum('qhd,khd->hqk', queries, keys_row, precision=highest) * score_scale)
    allowed = segment_row[:, None] == segment_row[None, :]
    weights = jax.nn.softmax(jnp.where(allowed[None], scores, -1e+30), axis=-1)
    return jnp.einsum('hqk,khd->qhd', low(weights), values_row, precision=highest)

def layer_group(params, inputs):
    weight_qkv, bias_qv, weight_out, bias_out, gain_attn, shift_attn, weight_in, bias_in, weight_ffo, bias_ffo, gain_ffn, shift_ffn = params
    group_x, group_segments = inputs
    group_rows = group_x.shape[0]
    flat_rows = group_x.reshape(group_rows * ROW_LEN, D)
    qkv_bias = jnp.concatenate([bias_qv[:D], jnp.zeros((D,), bias_qv.dtype), bias_qv[D:]])
    projected = jnp.dot(flat_rows, weight_qkv, precision=highest) + qkv_bias
    shaped = (group_rows, ROW_LEN, H, HD)
    queries = rounded(projected[:, :D]).reshape(shaped)
    keys_all = rounded(projected[:, D:2 * D]).reshape(shaped)
    values_all = rounded(projected[:, 2 * D:]).reshape(shaped)
    attended = lax.map(jax.checkpoint(attend_row), (queries, keys_all, values_all, group_segments))
    attn_flat = rounded(attended.reshape(group_rows * ROW_LEN, D))
    branch = low_back(jnp.dot(attn_flat, weight_out, precision=highest) + bias_out)
    hidden = layer_norm(flat_rows + branch, gain_attn, shift_attn)
    pre_gelu = low_back(jnp.dot(low(hidden), weight_in, precision=highest) + bias_in)
    activated = jax.nn.gelu(pre_gelu, approximate=False)
    second = low_back(jnp.dot(low(activated), weight_ffo, precision=highest) + bias_ffo)
    return layer_norm(hidden + second, gain_ffn, shift_ffn).reshape(group_rows, ROW_LEN, D)

def reference(tokens, weight_qkv, bias_qv, weight_out, bias_out, gain_attn, shift_attn, weight_in, bias_in, weight_ffo, bias_ffo, gain_ffn, shift_ffn, lengths, cotangent):
    bounds = jnp.cumsum(lengths, axis=1)
    positions = jnp.arange(ROW_LEN, dtype=jnp.int32)
    segments = lax.optimization_barrier(jnp.sum((positions[None, :, None] >= bounds[:, None, :]).astype(jnp.int32), axis=2))
    grouped_segments = segments.reshape(ROWS // ROWS_DEV, ROWS_DEV, ROW_LEN)

    def forward(inputs, *params):
        lowered = tuple((low(param) for param in params))
        grouped = inputs.reshape(ROWS // ROWS_DEV, ROWS_DEV, ROW_LEN, D)
        result = lax.map(jax.checkpoint(partial(layer_group, lowered)), (grouped, grouped_segments))
        return result.reshape(ROWS, ROW_LEN, D)
    masters = (weight_qkv, bias_qv, weight_out, bias_out, gain_attn, shift_attn, weight_in, bias_in, weight_ffo, bias_ffo, gain_ffn, shift_ffn)
    result, pull = jax.vjp(forward, tokens.astype(jnp.float32), *masters)
    grads = pull(cotangent.astype(jnp.float32))
    return (result.astype(jnp.bfloat16), grads[0].astype(jnp.bfloat16), grads[1], grads[2], grads[3], grads[4], grads[5], grads[6], grads[7], grads[8], grads[9], grads[10], grads[11], grads[12])
```

```python
import functools
import math

import jax
import jax.numpy as jnp
from jax import lax
from jax.experimental import pallas as pl
from jax.experimental.pallas import tpu as pltpu
from jax.sharding import PartitionSpec as P

H = 12
HD = 64
PAIR = 2 * HD
LANES = 128
f32 = jnp.float32
bf16 = jnp.bfloat16
SCORE_SCALE = 1.0 / math.sqrt(HD)
EXP2_SCALE = SCORE_SCALE * math.log2(math.e)
MASKED = -1e30
VMEM_LIMIT = 60 << 20
BLOCK = 256
WINDOWS = (2, 3, 4, 5, 6)


def dot(a, b):
    return jnp.dot(a, b, preferred_element_type=f32)


def dot_nt(a, b):
    return lax.dot_general(a, b, (((1,), (1,)), ((), ())), preferred_element_type=f32)


def dot_tn(a, b):
    return lax.dot_general(a, b, (((0,), (0,)), ((), ())), preferred_element_type=f32)


def column_sum(values):
    return jnp.sum(values, axis=0, keepdims=True)


def shape_of(shape, dtype):
    return jax.ShapeDtypeStruct(shape, dtype)


def project_kernel(x_ref, w_ref, b_ref, out_ref, outT_ref):
    low = (dot(x_ref[...], w_ref[...]) + b_ref[0:1, :]).astype(bf16)
    out_ref[...] = low
    outT_ref[...] = low.T


def project(x, weight, bias, block):
    tokens, width = x.shape
    columns = weight.shape[1]
    return pl.pallas_call(
        project_kernel,
        grid=(tokens // block,),
        in_specs=[
            pl.BlockSpec((block, width), lambda i: (i, 0)),
            pl.BlockSpec((width, columns), lambda i: (0, 0), pipeline_mode=pl.Buffered(1)),
            pl.BlockSpec((8, columns), lambda i: (0, 0), pipeline_mode=pl.Buffered(1)),
        ],
        out_specs=[
            pl.BlockSpec((block, columns), lambda i: (i, 0)),
            pl.BlockSpec((columns, block), lambda i: (0, i)),
        ],
        out_shape=[shape_of((tokens, columns), bf16), shape_of((columns, tokens), bf16)],
        compiler_params=pltpu.CompilerParams(vmem_limit_bytes=VMEM_LIMIT),
        cost_estimate=pl.CostEstimate(
            flops=2 * tokens * width * columns,
            bytes_accessed=2 * (tokens * width + width * columns + 2 * tokens * columns),
            transcendentals=0,
        ),
        name="project",
    )(x, weight, bias)


def passage_range(bounds_ref, row, start, size, row_len):
    first = jnp.int32(0)
    last = jnp.int32(row_len)
    for j in range(bounds_ref.shape[1]):
        bound = bounds_ref[row, j]
        first = jnp.where(bound <= start, jnp.maximum(first, bound), first)
        last = jnp.where(bound >= start + size, jnp.minimum(last, bound), last)
    return first, last


def segments_at(bounds_ref, row, positions):
    count = jnp.zeros(positions.shape, jnp.int32)
    for j in range(bounds_ref.shape[1]):
        count = count + (positions >= bounds_ref[row, j]).astype(jnp.int32)
    return count


def with_window(first, last, row_len, body):
    first_tile = first // LANES
    needed = (last + LANES - 1) // LANES - first_tile
    below = 0
    for tiles in WINDOWS:

        @pl.when((needed > below) & (needed <= tiles))
        def _(tiles=tiles):
            start = jnp.minimum(first_tile, row_len // LANES - tiles)
            body(pl.multiple_of(start * LANES, LANES), tiles * LANES)

        below = tiles


def mask_bias(bounds_ref, row, sub_start, sub_len, lane_start, lane_len):
    down = segments_at(
        bounds_ref, row, sub_start + lax.broadcasted_iota(jnp.int32, (sub_len, LANES), 0)
    )
    across = segments_at(
        bounds_ref, row, lane_start + lax.broadcasted_iota(jnp.int32, (1, lane_len), 1)
    )
    down = jnp.concatenate([down] * (lane_len // LANES), axis=1)
    return jnp.where(down == across, 0.0, MASKED).astype(f32)


def head_rows(h):
    return slice(HD * h, HD * h + HD)


def pair_lanes(h):
    return slice(PAIR * (h // 2), PAIR * (h // 2) + PAIR)


def in_pair(h, rows):
    zero = jnp.zeros_like(rows)
    return jnp.concatenate([rows, zero] if h % 2 == 0 else [zero, rows], axis=0)


def attend_kernel(bounds_ref, k_ref, qT_ref, vT_ref, out_ref, outT_ref, log_ref, bias_ref):
    row = pl.program_id(0)
    row_len, width = k_ref.shape
    block = qT_ref.shape[1]
    heads = width // HD
    q_start = pl.program_id(1) * block
    first, last = passage_range(bounds_ref, row, q_start, block, row_len)

    def body(start, window):
        keys = pl.ds(start, window)
        bias_ref[:window, :] = mask_bias(bounds_ref, row, start, window, q_start, block)

        def score(h):
            return dot(k_ref[keys, pair_lanes(h)], in_pair(h, qT_ref[head_rows(h), :]))

        def weigh(scores):
            masked = scores + bias_ref[:window, :]
            best = jnp.max(masked, axis=0, keepdims=True)
            return best, jnp.exp2((masked - best) * EXP2_SCALE).astype(bf16)

        def attend(h, best, weights):
            values = jnp.concatenate(
                [vT_ref[head_rows(h), keys], jnp.ones((16, window), bf16)], axis=0
            )
            summed = dot(values, weights)
            total = summed[HD : HD + 1]
            outT_ref[head_rows(h), :] = (summed[:HD] * (1.0 / total)).astype(bf16)
            log_ref[h : h + 1, :] = best * EXP2_SCALE + jnp.log2(total)

        scores = [score(0), score(1)]
        held = None
        for h in range(0, heads, 2):
            now = scores
            if h + 2 < heads:
                scores = [score(h + 2), score(h + 3)]
            weighed = [weigh(s) for s in now]
            if held is not None:
                attend(h - 2, *held[0])
                attend(h - 1, *held[1])
            held = weighed
        attend(heads - 2, *held[0])
        attend(heads - 1, *held[1])

    with_window(first, last, row_len, body)
    out_ref[...] = outT_ref[...].T


def attend_rows(bounds, qkv, qkvT, block):
    rows = bounds.shape[0]
    tokens = qkv.shape[0]
    width = qkv.shape[1] // 3
    row_len = tokens // rows
    blocks = row_len // block
    return pl.pallas_call(
        attend_kernel,
        grid_spec=pltpu.PrefetchScalarGridSpec(
            num_scalar_prefetch=1,
            grid=(rows, blocks),
            in_specs=[
                pl.BlockSpec((row_len, width), lambda r, b, s: (r, 1)),
                pl.BlockSpec((width, block), lambda r, b, s: (0, r * blocks + b)),
                pl.BlockSpec((width, row_len), lambda r, b, s: (2, r)),
            ],
            out_specs=[
                pl.BlockSpec((block, width), lambda r, b, s: (r * blocks + b, 0)),
                pl.BlockSpec((width, block), lambda r, b, s: (0, r * blocks + b)),
                pl.BlockSpec((16, block), lambda r, b, s: (0, r * blocks + b)),
            ],
            scratch_shapes=[pltpu.VMEM((max(WINDOWS) * LANES, block), f32)],
        ),
        out_shape=[
            shape_of((tokens, width), bf16),
            shape_of((width, tokens), bf16),
            shape_of((16, tokens), f32),
        ],
        compiler_params=pltpu.CompilerParams(vmem_limit_bytes=VMEM_LIMIT),
        cost_estimate=pl.CostEstimate(
            flops=16 * tokens * row_len * width // 4,
            bytes_accessed=10 * tokens * width,
            transcendentals=0,
        ),
        name="attend",
    )(bounds, qkv, qkvT, qkvT)


def attend_back_kernel(
    bounds_ref, k_ref, kT_ref, v_ref, q_ref, qT_ref, do_ref, doT_ref, outT_ref, log_ref,
    dq_ref, dk_ref, dv_ref, sum_ref, bias_ref, dqT_ref, delta_ref,
):
    row = pl.program_id(0)
    at = pl.program_id(1)
    row_len, width = q_ref.shape
    block = k_ref.shape[0]
    heads = width // HD
    k_start = at * block

    @pl.when((row == 0) & (at == 0))
    def _():
        sum_ref[...] = jnp.zeros(sum_ref.shape, f32)

    @pl.when(at == 0)
    def _():
        dqT_ref[...] = jnp.zeros(dqT_ref.shape, f32)
        for h in range(heads):
            both = doT_ref[head_rows(h), :].astype(f32) * outT_ref[head_rows(h), :].astype(f32)
            delta_ref[h : h + 1, :] = column_sum(both)

    first, last = passage_range(bounds_ref, row, k_start, block, row_len)
    low_half = lax.broadcasted_iota(jnp.int32, (block, PAIR), 1) < HD

    def body(start, window):
        queries = pl.ds(start, window)
        bias_ref[:, :window] = mask_bias(bounds_ref, row, k_start, block, start, window)
        even = {}

        def products(h):
            lanes = pair_lanes(h)
            scores = dot(k_ref[:, lanes], in_pair(h, qT_ref[head_rows(h), queries]))
            grad_prob = dot(v_ref[:, lanes], in_pair(h, doT_ref[head_rows(h), queries]))
            return scores, grad_prob

        def weigh(h, scores, grad_prob):
            shift = bias_ref[:, :window] - log_ref[h : h + 1, queries]
            probs = jnp.exp2(scores * EXP2_SCALE + shift)
            grad_score = probs * (grad_prob - delta_ref[h : h + 1, queries])
            return probs.astype(bf16), grad_score.astype(bf16)

        def gather(h, probs, grad_score):
            lanes = pair_lanes(h)
            dv = dot(probs, do_ref[queries, lanes])
            dk = dot(grad_score, q_ref[queries, lanes])
            dqT_ref[head_rows(h), queries] += dot(kT_ref[head_rows(h), :], grad_score)
            if h % 2 == 0:
                even[0] = (dv, dk)
            else:
                dk_ref[:, lanes] = (jnp.where(low_half, even[0][1], dk) * SCORE_SCALE).astype(bf16)
                dv_ref[:, lanes] = jnp.where(low_half, even[0][0], dv).astype(bf16)

        made = products(0)
        held = None
        for h in range(heads):
            now = made
            if h + 1 < heads:
                made = products(h + 1)
            weighed = weigh(h, *now)
            if held is not None:
                gather(h - 1, *held)
            held = weighed
        gather(heads - 1, *held)

    with_window(first, last, row_len, body)
    sum_ref[1:2, :] += column_sum(dv_ref[...].astype(f32))

    @pl.when(at == pl.num_programs(1) - 1)
    def _():
        dq = (dqT_ref[...] * SCORE_SCALE).astype(bf16).T
        dq_ref[...] = dq
        sum_ref[0:1, :] += column_sum(dq.astype(f32))


def attend_rows_back(bounds, qkv, qkvT, do, doT, outT, log, block):
    rows = bounds.shape[0]
    tokens, width = do.shape
    row_len = tokens // rows
    blocks = row_len // block
    whole = pl.BlockSpec((row_len, width), lambda r, b, s: (r, 0))
    wholeT = pl.BlockSpec((width, row_len), lambda r, b, s: (0, r))
    part = pl.BlockSpec((block, width), lambda r, b, s: (r * blocks + b, 0))
    return pl.pallas_call(
        attend_back_kernel,
        grid_spec=pltpu.PrefetchScalarGridSpec(
            num_scalar_prefetch=1,
            grid=(rows, blocks),
            in_specs=[
                pl.BlockSpec((block, width), lambda r, b, s: (r * blocks + b, 1)),
                pl.BlockSpec((width, block), lambda r, b, s: (1, r * blocks + b)),
                pl.BlockSpec((block, width), lambda r, b, s: (r * blocks + b, 2)),
                whole,
                wholeT,
                whole,
                wholeT,
                wholeT,
                pl.BlockSpec((16, row_len), lambda r, b, s: (0, r)),
            ],
            out_specs=[whole, part, part, pl.BlockSpec((8, width), lambda r, b, s: (0, 0))],
            scratch_shapes=[
                pltpu.VMEM((block, max(WINDOWS) * LANES), f32),
                pltpu.VMEM((width, row_len), f32),
                pltpu.VMEM((16, row_len), f32),
            ],
        ),
        out_shape=[shape_of((tokens, width), bf16)] * 3 + [shape_of((8, width), f32)],
        compiler_params=pltpu.CompilerParams(vmem_limit_bytes=VMEM_LIMIT),
        cost_estimate=pl.CostEstimate(
            flops=40 * tokens * row_len * width // 4,
            bytes_accessed=22 * tokens * width,
            transcendentals=0,
        ),
        name="attend_back",
    )(bounds, qkv, qkvT, qkv, qkv, qkvT, do, doT, outT, log)


def gelu_and_slope(x):
    share = 0.5 + 0.5 * lax.erf(x * math.sqrt(0.5))
    density = jnp.exp(x * x * -0.5) * (1.0 / math.sqrt(2.0 * math.pi))
    return x * share, share + x * density


def normalise(values):
    centred = values - jnp.mean(values, axis=-1, keepdims=True)
    scale = lax.rsqrt(jnp.mean(centred * centred, axis=-1, keepdims=True) + 1e-06)
    return centred * scale, scale


def normalise_back(grad, normed, scale):
    along = jnp.mean(grad * normed, axis=-1, keepdims=True)
    return scale * (grad - jnp.mean(grad, axis=-1, keepdims=True) - normed * along)


def dense_kernel(
    attn_ref, x_ref, cot_ref, wo_ref, wi_ref, wf_ref, vec_ref, bi_ref,
    out_ref, act_ref, gp_ref, gs_ref, low_ref, gr1_ref, gb_ref, do_ref, doT_ref, sum_ref,
    sum_in_ref, slope_ref, *, chunk,
):
    width = x_ref.shape[1]
    inner = wi_ref.shape[1]
    bias_out, gain_a, shift_a, bias_ffo, gain_f, shift_f = [vec_ref[j : j + 1, :] for j in range(6)]

    @pl.when(pl.program_id(0) == 0)
    def _():
        sum_ref[...] = jnp.zeros(sum_ref.shape, f32)
        sum_in_ref[...] = jnp.zeros(sum_in_ref.shape, f32)

    branch = dot(attn_ref[...], wo_ref[...]) + bias_out
    normed_a, scale_a = normalise(x_ref[...].astype(f32) + branch)
    hidden = normed_a * gain_a + shift_a
    low = hidden.astype(bf16)
    low_ref[...] = low
    cuts = [slice(c * chunk, (c + 1) * chunk) for c in range(inner // chunk)]
    last = len(cuts) - 1

    second = None
    held = None
    made = dot(low, wi_ref[:, cuts[0]])
    for c, cut in enumerate(cuts):
        pre = made + bi_ref[0:1, cut]
        if c < last:
            made = dot(low, wi_ref[:, cuts[c + 1]])
        value, slope = gelu_and_slope(pre)
        value = value.astype(bf16)
        act_ref[:, cut] = value
        slope_ref[:, cut] = slope.astype(bf16)
        if held is not None:
            term = dot(held, wf_ref[cuts[c - 1], :])
            second = term if second is None else second + term
        held = value
    term = dot(held, wf_ref[cuts[last], :])
    second = term if second is None else second + term

    normed_f, scale_f = normalise(hidden + (second + bias_ffo))
    out_ref[...] = (normed_f * gain_f + shift_f).astype(bf16)
    cot = cot_ref[...].astype(f32)
    grad_r2 = normalise_back(cot * gain_f, normed_f, scale_f)
    grad_second = grad_r2.astype(bf16)
    gs_ref[...] = grad_second
    sum_ref[0:1, :] += column_sum(cot * normed_f)
    sum_ref[1:2, :] += column_sum(cot)
    sum_ref[2:3, :] += column_sum(grad_second.astype(f32))

    grad_hidden = grad_r2
    held = None
    made = dot_nt(grad_second, wf_ref[cuts[0], :])
    for c, cut in enumerate(cuts):
        grad_act = made
        if c < last:
            made = dot_nt(grad_second, wf_ref[cuts[c + 1], :])
        grad_pre = (grad_act * slope_ref[:, cut].astype(f32)).astype(bf16)
        gp_ref[:, cut] = grad_pre
        sum_in_ref[0:1, cut] += column_sum(grad_pre.astype(f32))
        if held is not None:
            grad_hidden = grad_hidden + dot_nt(held, wi_ref[:, cuts[c - 1]])
        held = grad_pre
    grad_hidden = grad_hidden + dot_nt(held, wi_ref[:, cuts[last]])

    grad_r1 = normalise_back(grad_hidden * gain_a, normed_a, scale_a)
    gr1_ref[...] = grad_r1
    grad_branch = grad_r1.astype(bf16)
    gb_ref[...] = grad_branch
    sum_ref[3:4, :] += column_sum(grad_hidden * normed_a)
    sum_ref[4:5, :] += column_sum(grad_hidden)
    sum_ref[5:6, :] += column_sum(grad_branch.astype(f32))
    grad_attn = dot_nt(grad_branch, wo_ref[...]).astype(bf16)
    do_ref[...] = grad_attn
    doT_ref[...] = grad_attn.T


def dense(attn, x, cot, w_out, w_in, w_ffo, vectors, bias_in, block, chunk):
    tokens, width = x.shape
    inner = w_in.shape[1]
    narrow = pl.BlockSpec((block, width), lambda i: (i, 0))
    wide = pl.BlockSpec((block, inner), lambda i: (i, 0))

    def held(a):
        return pl.BlockSpec(a.shape, lambda i: (0, 0), pipeline_mode=pl.Buffered(1))

    return pl.pallas_call(
        functools.partial(dense_kernel, chunk=chunk),
        grid=(tokens // block,),
        in_specs=[narrow, narrow, narrow]
        + [held(a) for a in (w_out, w_in, w_ffo, vectors, bias_in)],
        out_specs=[
            narrow, wide, wide, narrow, narrow, narrow, narrow, narrow,
            pl.BlockSpec((width, block), lambda i: (0, i)),
            pl.BlockSpec((8, width), lambda i: (0, 0)),
            pl.BlockSpec((8, inner), lambda i: (0, 0)),
        ],
        out_shape=[
            shape_of((tokens, width), bf16),
            shape_of((tokens, inner), bf16),
            shape_of((tokens, inner), bf16),
            shape_of((tokens, width), bf16),
            shape_of((tokens, width), bf16),
            shape_of((tokens, width), f32),
            shape_of((tokens, width), bf16),
            shape_of((tokens, width), bf16),
            shape_of((width, tokens), bf16),
            shape_of((8, width), f32),
            shape_of((8, inner), f32),
        ],
        scratch_shapes=[pltpu.VMEM((block, inner), bf16)],
        compiler_params=pltpu.CompilerParams(vmem_limit_bytes=VMEM_LIMIT),
        cost_estimate=pl.CostEstimate(
            flops=2 * tokens * width * (2 * width + 4 * inner),
            bytes_accessed=tokens * (22 * width + 4 * inner) + 4 * width * inner,
            transcendentals=2 * tokens * inner,
        ),
        name="dense",
    )(attn, x, cot, w_out, w_in, w_ffo, vectors, bias_in)


def split_heads(values):
    return values.reshape(values.shape[0], values.shape[1], H, HD)


def gathered_probs(queries, keys, allowed):
    scores = jnp.einsum("rqhd,rkhd->rhqk", queries, keys, preferred_element_type=f32)
    return jax.nn.softmax(jnp.where(allowed, scores * SCORE_SCALE, MASKED), axis=-1)


def attend_gathered(bounds, qkv, rows, seq_index):
    width = qkv.shape[1] // 3
    parts = qkv.reshape(rows, -1, 3 * width)
    tok_seq = parts.shape[1]
    whole = lax.all_gather(parts[:, :, width:], "seq", axis=1, tiled=True)
    row_len = whole.shape[1]
    queries = split_heads(parts[:, :, :width])
    keys = split_heads(whole[:, :, :width])
    values = split_heads(whole[:, :, width:])
    positions = jnp.arange(row_len, dtype=jnp.int32)
    segments = jnp.sum((positions[None, :, None] >= bounds[:, None, :]).astype(jnp.int32), axis=2)
    mine = lax.dynamic_slice_in_dim(segments, seq_index * tok_seq, tok_seq, 1)
    allowed = mine[:, None, :, None] == segments[:, None, None, :]
    probs = gathered_probs(queries, keys, allowed)
    attended = jnp.einsum(
        "rhqk,rkhd->rqhd", probs.astype(bf16), values, preferred_element_type=f32
    )
    return attended.astype(bf16).reshape(-1, width), (queries, keys, values, allowed)


def attend_gathered_back(saved, attn, do):
    queries, keys, values, allowed = saved
    rows, tok_seq = queries.shape[:2]
    width = attn.shape[1]
    probs = gathered_probs(queries, keys, allowed)
    do = do.reshape(rows, tok_seq, H, HD)
    delta = jnp.sum(do.astype(f32) * attn.reshape(do.shape).astype(f32), axis=-1)
    grad_prob = jnp.einsum("rqhd,rkhd->rhqk", do, values, preferred_element_type=f32)
    grad_score = (probs * (grad_prob - delta.transpose(0, 2, 1)[..., None])).astype(bf16)
    dq = jnp.einsum("rhqk,rkhd->rqhd", grad_score, keys, preferred_element_type=f32) * SCORE_SCALE
    dk = (
        jnp.einsum("rhqk,rqhd->rkhd", grad_score, queries, preferred_element_type=f32)
        * SCORE_SCALE
    )
    dv = jnp.einsum("rhqk,rqhd->rkhd", probs.astype(bf16), do, preferred_element_type=f32)
    pair = jnp.concatenate([dk.reshape(rows, -1, width), dv.reshape(rows, -1, width)], axis=-1)
    pair = lax.psum_scatter(pair.astype(bf16), "seq", scatter_dimension=1, tiled=True)
    pair = pair.reshape(-1, 2 * width)
    dq = dq.astype(bf16).reshape(-1, width)
    dk, dv = pair[:, :width], pair[:, width:]
    sums = jnp.stack([jnp.sum(dq.astype(f32), axis=0), jnp.sum(dv.astype(f32), axis=0)])
    return dq, dk, dv, sums


def rows_of(values, seq_index, seq_count):
    rows, part, width = values.shape
    mine = rows // seq_count
    whole = jnp.zeros((mine, part * seq_count, width), values.dtype)
    for step in range(seq_count):
        to = (seq_index + step) % seq_count
        source = (seq_index - step) % seq_count
        piece = lax.dynamic_slice_in_dim(values, to * mine, mine, 0)
        if step:
            piece = lax.ppermute(
                piece, "seq", [(s, (s + step) % seq_count) for s in range(seq_count)]
            )
        whole = lax.dynamic_update_slice_in_dim(whole, piece, source * part, 1)
    return whole


def parts_of(values, seq_index, seq_count):
    mine, row_len, width = values.shape
    part = row_len // seq_count
    parts = jnp.zeros((mine * seq_count, part, width), values.dtype)
    for step in range(seq_count):
        to = (seq_index + step) % seq_count
        source = (seq_index - step) % seq_count
        piece = lax.dynamic_slice_in_dim(values, to * part, part, 1)
        if step:
            piece = lax.ppermute(
                piece, "seq", [(s, (s + step) % seq_count) for s in range(seq_count)]
            )
        parts = lax.dynamic_update_slice_in_dim(parts, piece, source * mine, 0)
    return parts


def per_device(
    tokens,
    weight_qkv,
    bias_qv,
    weight_out,
    bias_out,
    gain_attn,
    shift_attn,
    weight_in,
    bias_in,
    weight_ffo,
    bias_ffo,
    gain_ffn,
    shift_ffn,
    lengths,
    cotangent,
):
    rows, tok_seq, width = tokens.shape
    seq_count = lax.axis_size("seq")
    seq_index = lax.axis_index("seq")
    whole_rows = rows % seq_count == 0
    inner = weight_in.shape[1]
    shard = weight_qkv.shape[0]
    token_count = rows * tok_seq

    small = (bias_qv, bias_out, gain_attn, shift_attn, bias_in, bias_ffo, gain_ffn, shift_ffn)
    small_cols = [v.shape[0] // shard for v in small]
    packed = jnp.concatenate([v.reshape(shard, -1) for v in small], axis=1)
    packed = jnp.pad(packed, ((0, 0), (0, LANES - packed.shape[1])))
    first = jnp.concatenate([weight_qkv, packed], axis=1).astype(bf16)
    first = lax.all_gather(first, "dp", axis=0, tiled=True)
    w_qkv = first[:, : 3 * width]
    vectors = []
    at = 3 * width
    for cols in small_cols:
        vectors.append(first[:, at : at + cols].astype(f32).reshape(-1))
        at += cols
    v_qv, v_out, v_ga, v_sa, v_in, v_ffo, v_gf, v_sf = vectors
    w_out = lax.all_gather(weight_out.astype(bf16), "dp", axis=0, tiled=True)
    w_in = lax.all_gather(weight_in.astype(bf16), "dp", axis=0, tiled=True)
    w_ffo = lax.all_gather(weight_ffo.astype(bf16), "dp", axis=0, tiled=True)
    qkv_bias = jnp.concatenate([v_qv[:width], jnp.zeros((width,), f32), v_qv[width:]])
    qkv_bias = jnp.broadcast_to(qkv_bias[None], (8, 3 * width))
    vec = jnp.stack([v_out, v_ga, v_sa, v_ffo, v_gf, v_sf, v_sf, v_sf])
    in_bias = jnp.broadcast_to(v_in[None], (8, inner))

    bounds = jnp.cumsum(lengths, axis=1)
    if whole_rows:
        mine = rows // seq_count
        bounds = lax.dynamic_slice_in_dim(bounds, seq_index * mine, mine, 0)
        x = rows_of(tokens, seq_index, seq_count).reshape(token_count, width)
        cot = rows_of(cotangent, seq_index, seq_count).reshape(token_count, width)
    else:
        x = tokens.reshape(token_count, width)
        cot = cotangent.reshape(token_count, width)

    qkv, qkvT = project(x, w_qkv, qkv_bias, BLOCK)
    if whole_rows:
        attn, attnT, log = attend_rows(bounds, qkv, qkvT, BLOCK)
    else:
        attn, saved = attend_gathered(bounds, qkv, rows, seq_index)
    out, act, gp, gs, low, gr1, gb, do, doT, sums, sums_in = dense(
        attn, x, cot, w_out, w_in, w_ffo, vec, in_bias, BLOCK, width
    )
    grad_w_ffo = dot_tn(act, gs).astype(bf16)
    grad_w_in = dot_tn(low, gp).astype(bf16)
    grad_w_out = dot_tn(attn, gb).astype(bf16)
    if whole_rows:
        dq, dk, dv, sums_qv = attend_rows_back(bounds, qkv, qkvT, do, doT, attnT, log, BLOCK)
    else:
        dq, dk, dv, sums_qv = attend_gathered_back(saved, attn, do)
    grad_qkv = jnp.concatenate([dq, dk, dv], axis=1)
    grad_w_qkv = dot_tn(x, grad_qkv).astype(bf16)
    grad_x = (gr1 + dot_nt(grad_qkv, w_qkv)).astype(bf16)

    if whole_rows:
        out = parts_of(out.reshape(mine, -1, width), seq_index, seq_count)
        grad_x = parts_of(grad_x.reshape(mine, -1, width), seq_index, seq_count)
    else:
        out = out.reshape(rows, tok_seq, width)
        grad_x = grad_x.reshape(rows, tok_seq, width)

    def scatter(values):
        return lax.psum_scatter(values, "dp", scatter_dimension=0, tiled=True)

    small_grads = (
        sums_qv[:2].reshape(-1), sums[5], sums[3], sums[4], sums_in[0], sums[2], sums[0], sums[1],
    )
    dp_count = lax.axis_size("dp")
    packed = jnp.concatenate([v.reshape(dp_count * shard, -1) for v in small_grads], axis=1)
    packed = jnp.pad(packed, ((0, 0), (0, LANES - packed.shape[1]))).astype(bf16)
    last = scatter(jnp.concatenate([grad_w_qkv, packed], axis=1))
    shared = lax.psum(
        (scatter(grad_w_ffo), scatter(grad_w_in), scatter(grad_w_out), last), "seq"
    )
    d_ffo, d_in, d_out, last = [v.astype(f32) for v in shared]
    d_small = []
    at = 3 * width
    for cols in small_cols:
        d_small.append(last[:, at : at + cols].reshape(-1))
        at += cols
    g_qv, g_bo, g_ga, g_sa, g_bi, g_bf, g_gf, g_sf = d_small
    return (
        out, grad_x, last[:, : 3 * width], g_qv, d_out, g_bo, g_ga, g_sa, d_in, g_bi, d_ffo,
        g_bf, g_gf, g_sf,
    )


def solution(mesh):
    by_token = P("dp", "seq", None)
    weight = P("dp", None)
    vector = P("dp")
    params = (
        weight, vector, weight, vector, vector, vector, weight, vector, weight, vector, vector,
        vector,
    )
    return jax.shard_map(
        per_device,
        mesh=mesh,
        in_specs=(by_token,) + params + (weight, by_token),
        out_specs=(by_token, by_token) + params,
        check_vma=False,
    )
```

```python
import functools
import math

import jax
import jax.numpy as jnp
from jax import lax
from jax.experimental import pallas as pl
from jax.experimental.pallas import tpu as pltpu
from jax.sharding import PartitionSpec as P

H = 12
HD = 64
PAIR = 2 * HD
LANES = 128
f32 = jnp.float32
bf16 = jnp.bfloat16
SCORE_SCALE = 1.0 / math.sqrt(HD)
EXP2_SCALE = SCORE_SCALE * math.log2(math.e)
MASKED = -1e30
VMEM_LIMIT = 60 << 20
BLOCK = 256
WINDOWS = (2, 3, 4, 5, 6)


def dot(a, b):
    return jnp.dot(a, b, preferred_element_type=f32)


def dot_nt(a, b):
    return lax.dot_general(a, b, (((1,), (1,)), ((), ())), preferred_element_type=f32)


def dot_tn(a, b):
    return lax.dot_general(a, b, (((0,), (0,)), ((), ())), preferred_element_type=f32)


def column_sum(values):
    return jnp.sum(values, axis=0, keepdims=True)


def shape_of(shape, dtype):
    return jax.ShapeDtypeStruct(shape, dtype)


def vector_rows(sizes):
    rows = []
    at = 0
    for size in sizes:
        rows.append(at)
        at += -(-size // LANES)
    return rows, at


def lower_kernel(*refs):
    w_qkv, w_in, w_ffo, w_out = refs[:4]
    small = refs[4:-3]
    first_ref, others_ref, block_ref = refs[-3:]
    columns = w_qkv.shape[1]
    shard, width = w_out.shape
    first_ref[:, :columns] = w_qkv[...].astype(bf16)
    block_ref[...] = jnp.zeros(block_ref.shape, f32)
    for ref, row in zip(small, vector_rows([r.shape[1] for r in small])[0]):
        size = ref.shape[1]
        for at in range(0, size, LANES):
            n = min(LANES, size - at)
            block_ref[row : row + 1, :n] = ref[:, at : at + n]
            row += 1
    first_ref[:, columns:] = block_ref[...].astype(bf16)
    chunks = w_in.shape[1] // width
    for c in range(chunks):
        others_ref[c * shard : (c + 1) * shard, :] = w_in[:, c * width : (c + 1) * width].astype(bf16)
    others_ref[chunks * shard : 2 * chunks * shard, :] = w_ffo[...].astype(bf16)
    others_ref[2 * chunks * shard :, :] = w_out[...].astype(bf16)


def lower(w_qkv, w_in, w_ffo, w_out, small):
    shard, columns = w_qkv.shape
    width = w_out.shape[1]
    chunks = w_in.shape[1] // width
    return pl.pallas_call(
        lower_kernel,
        out_shape=[
            shape_of((shard, columns + LANES), bf16),
            shape_of(((2 * chunks + 1) * shard, width), bf16),
        ],
        scratch_shapes=[pltpu.VMEM((shard, LANES), f32)],
        compiler_params=pltpu.CompilerParams(vmem_limit_bytes=VMEM_LIMIT),
        name="lower",
    )(w_qkv, w_in, w_ffo, w_out, *[v.reshape(1, -1) for v in small])


def spread_vector(block, row, size, shards):
    total = size * shards
    place = lax.broadcasted_iota(jnp.int32, (LANES, total), 1) % size
    lane = lax.broadcasted_iota(jnp.int32, (LANES, total), 0)
    found = jnp.zeros((shards, total), f32)
    for at in range(0, size, LANES):
        pick = jnp.where(place == lane + at, 1.0, 0.0).astype(bf16)
        found = found + dot(block[:, row + at // LANES, :].astype(bf16), pick)
    owner = lax.broadcasted_iota(jnp.int32, (shards, total), 0)
    mine = lax.broadcasted_iota(jnp.int32, (shards, total), 1) // size
    return column_sum(jnp.where(owner == mine, found, 0.0))


def gather_vector(vector, shards):
    total = vector.shape[1]
    size = total // shards
    place = lax.broadcasted_iota(jnp.int32, (total, LANES), 0) % size
    lane = lax.broadcasted_iota(jnp.int32, (total, LANES), 1)
    owner = lax.broadcasted_iota(jnp.int32, (shards, total), 0)
    mine = lax.broadcasted_iota(jnp.int32, (shards, total), 1) // size
    own = jnp.where(owner == mine, vector, 0.0).astype(bf16)
    return [
        dot(own, jnp.where(place == lane + at, 1.0, 0.0).astype(bf16))
        for at in range(0, size, LANES)
    ]


def project_kernel(place_ref, mine_ref, other_ref, *refs, shards, pieces):
    x_ref, out_ref, outT_ref, w_ref, vec_ref, bi_ref, bias_ref, sems = refs[len(pieces) :]
    width = x_ref.shape[1]
    columns = out_ref.shape[1]
    shard = width // shards

    @pl.when((pl.program_id(0) == 0) & (pl.program_id(1) == 0) & (pl.program_id(2) == 0))
    def _():
        copies = []
        for j, (ref, back) in enumerate(zip(refs, pieces)):
            start = jnp.int32(0) if back is None else piece_owner(place_ref[1], back, shards) * shard
            rows = pl.ds(pl.multiple_of(start, 16), ref.shape[0])
            copies.append(pltpu.make_async_copy(ref, w_ref.at[rows, :], sems.at[j]))
        for copy in copies:
            copy.start()
        for copy in copies:
            copy.wait()
        block = w_ref[:, columns:].astype(f32).reshape(shards, shard, LANES)
        inner = bi_ref.shape[1]
        totals = (2 * width, width, width, width, inner, width, width, width)
        sizes = [total // shards for total in totals]
        found = [
            spread_vector(block, row, size, shards)
            for row, size in zip(vector_rows(sizes)[0], sizes)
        ]
        bias_ref[0:1, :width] = found[0][:, :width]
        bias_ref[0:1, width : 2 * width] = jnp.zeros((1, width), f32)
        bias_ref[0:1, 2 * width :] = found[0][:, width:]
        bi_ref[0:1, :] = found[4]
        for j, v in enumerate(found[1:4] + found[5:]):
            vec_ref[j : j + 1, :] = v

    x = jnp.where(pl.program_id(1) == place_ref[0], mine_ref[...], other_ref[...])
    x_ref[...] = x
    low = (dot(x, w_ref[:, :columns]) + bias_ref[0:1, :]).astype(bf16)
    out_ref[...] = low
    outT_ref[...] = low.T


def halves(block_rows, blocks):
    def at(used, r, h, b):
        rest = jnp.where(h == 0, 0, blocks - 1)
        return (r * blocks + jnp.where(used, b, rest), 0)

    return (
        lambda r, h, b, s: at(h == s[0], r, h, b),
        lambda r, h, b, s: at(h != s[0], r, h, b),
    )


def project(place, mine, other, weight, inner, block):
    rows, half, width = mine.shape
    block = min(block, half)
    blocks = half // block
    columns = 3 * width
    tokens = 2 * rows * half
    shards = lax.axis_size("dp")
    mine_at, other_at = halves(block, blocks)

    def at(r, h, b, s):
        return ((r * 2 + h) * blocks + b, 0)

    return pl.pallas_call(
        functools.partial(project_kernel, shards=shards, pieces=[back for _, back in weight]),
        grid_spec=pltpu.PrefetchScalarGridSpec(
            num_scalar_prefetch=1,
            grid=(rows, 2, blocks),
            in_specs=[
                pl.BlockSpec((block, width), mine_at),
                pl.BlockSpec((block, width), other_at),
            ]
            + [pl.BlockSpec(memory_space=pl.ANY)] * len(weight),
            out_specs=[
                pl.BlockSpec((block, width), at),
                pl.BlockSpec((block, columns), at),
                pl.BlockSpec((columns, block), lambda *i: (0, at(*i)[0])),
                pl.BlockSpec((width, columns + LANES), lambda *_: (0, 0)),
                pl.BlockSpec((8, width), lambda *_: (0, 0)),
                pl.BlockSpec((8, inner), lambda *_: (0, 0)),
            ],
            scratch_shapes=[
                pltpu.VMEM((8, columns), f32),
                pltpu.SemaphoreType.DMA((len(weight),)),
            ],
        ),
        out_shape=[
            shape_of((tokens, width), bf16),
            shape_of((tokens, columns), bf16),
            shape_of((columns, tokens), bf16),
            shape_of((width, columns + LANES), bf16),
            shape_of((8, width), f32),
            shape_of((8, inner), f32),
        ],
        compiler_params=pltpu.CompilerParams(vmem_limit_bytes=VMEM_LIMIT),
        cost_estimate=pl.CostEstimate(
            flops=2 * tokens * width * columns,
            bytes_accessed=2 * (2 * tokens * width + 2 * width * columns + 2 * tokens * columns),
            transcendentals=0,
        ),
        name="project",
    )(place, mine.reshape(-1, width), other.reshape(-1, width), *[w for w, _ in weight])


def passage_range(bounds_ref, row, start, size, row_len):
    first = jnp.int32(0)
    last = jnp.int32(row_len)
    for j in range(bounds_ref.shape[1]):
        bound = bounds_ref[row, j]
        first = jnp.where(bound <= start, jnp.maximum(first, bound), first)
        last = jnp.where(bound >= start + size, jnp.minimum(last, bound), last)
    return first, last


def segments_at(bounds_ref, row, positions):
    count = jnp.zeros(positions.shape, jnp.int32)
    for j in range(bounds_ref.shape[1]):
        count = count + (positions >= bounds_ref[row, j]).astype(jnp.int32)
    return count


def with_window(first, last, row_len, body):
    first_tile = first // LANES
    needed = (last + LANES - 1) // LANES - first_tile
    below = 0
    for tiles in WINDOWS:

        @pl.when((needed > below) & (needed <= tiles))
        def _(tiles=tiles):
            start = jnp.minimum(first_tile, row_len // LANES - tiles)
            body(pl.multiple_of(start * LANES, LANES), tiles * LANES)

        below = tiles


def mask_bias(bounds_ref, row, sub_start, sub_len, lane_start, lane_len):
    down = segments_at(
        bounds_ref, row, sub_start + lax.broadcasted_iota(jnp.int32, (sub_len, LANES), 0)
    )
    across = segments_at(
        bounds_ref, row, lane_start + lax.broadcasted_iota(jnp.int32, (1, lane_len), 1)
    )
    down = jnp.concatenate([down] * (lane_len // LANES), axis=1)
    return jnp.where(down == across, 0.0, MASKED).astype(f32)


def head_rows(h):
    return slice(HD * h, HD * h + HD)


def pair_lanes(h):
    return slice(PAIR * (h // 2), PAIR * (h // 2) + PAIR)


def in_pair(h, rows):
    zero = jnp.zeros_like(rows)
    return jnp.concatenate([rows, zero] if h % 2 == 0 else [zero, rows], axis=0)


def attend_kernel(bounds_ref, k_ref, qT_ref, vT_ref, out_ref, outT_ref, log_ref, bias_ref):
    row = pl.program_id(0)
    row_len, width = k_ref.shape
    block = qT_ref.shape[1]
    heads = width // HD
    q_start = pl.program_id(1) * block
    first, last = passage_range(bounds_ref, row, q_start, block, row_len)

    def body(start, window):
        keys = pl.ds(start, window)
        bias_ref[:window, :] = mask_bias(bounds_ref, row, start, window, q_start, block)

        def score(h):
            return dot(k_ref[keys, pair_lanes(h)], in_pair(h, qT_ref[head_rows(h), :]))

        def weigh(scores):
            masked = scores + bias_ref[:window, :]
            best = jnp.max(masked, axis=0, keepdims=True)
            return best, jnp.exp2((masked - best) * EXP2_SCALE).astype(bf16)

        def attend(h, best, weights):
            values = jnp.concatenate(
                [vT_ref[head_rows(h), keys], jnp.ones((16, window), bf16)], axis=0
            )
            summed = dot(values, weights)
            total = summed[HD : HD + 1]
            outT_ref[head_rows(h), :] = (summed[:HD] * (1.0 / total)).astype(bf16)
            log_ref[h : h + 1, :] = best * EXP2_SCALE + jnp.log2(total)

        scores = [score(0), score(1)]
        held = None
        for h in range(0, heads, 2):
            now = scores
            if h + 2 < heads:
                scores = [score(h + 2), score(h + 3)]
            weighed = [weigh(s) for s in now]
            if held is not None:
                attend(h - 2, *held[0])
                attend(h - 1, *held[1])
            held = weighed
        attend(heads - 2, *held[0])
        attend(heads - 1, *held[1])

    with_window(first, last, row_len, body)
    out_ref[...] = outT_ref[...].T


def attend_rows(bounds, qkv, qkvT, block):
    rows = bounds.shape[0]
    tokens = qkv.shape[0]
    width = qkv.shape[1] // 3
    row_len = tokens // rows
    blocks = row_len // block
    return pl.pallas_call(
        attend_kernel,
        grid_spec=pltpu.PrefetchScalarGridSpec(
            num_scalar_prefetch=1,
            grid=(rows, blocks),
            in_specs=[
                pl.BlockSpec((row_len, width), lambda r, b, s: (r, 1)),
                pl.BlockSpec((width, block), lambda r, b, s: (0, r * blocks + b)),
                pl.BlockSpec((width, row_len), lambda r, b, s: (2, r)),
            ],
            out_specs=[
                pl.BlockSpec((block, width), lambda r, b, s: (r * blocks + b, 0)),
                pl.BlockSpec((width, block), lambda r, b, s: (0, r * blocks + b)),
                pl.BlockSpec((16, block), lambda r, b, s: (0, r * blocks + b)),
            ],
            scratch_shapes=[pltpu.VMEM((max(WINDOWS) * LANES, block), f32)],
        ),
        out_shape=[
            shape_of((tokens, width), bf16),
            shape_of((width, tokens), bf16),
            shape_of((16, tokens), f32),
        ],
        compiler_params=pltpu.CompilerParams(vmem_limit_bytes=VMEM_LIMIT),
        cost_estimate=pl.CostEstimate(
            flops=16 * tokens * row_len * width // 4,
            bytes_accessed=10 * tokens * width,
            transcendentals=0,
        ),
        name="attend",
    )(bounds, qkv, qkvT, qkvT)


def attend_back_kernel(
    bounds_ref, k_ref, kT_ref, v_ref, q_ref, qT_ref, do_ref, doT_ref, outT_ref, log_ref,
    dq_ref, dk_ref, dv_ref, sum_ref, bias_ref, dqT_ref, delta_ref,
):
    row = pl.program_id(0)
    at = pl.program_id(1)
    row_len, width = q_ref.shape
    block = k_ref.shape[0]
    heads = width // HD
    k_start = at * block

    @pl.when((row == 0) & (at == 0))
    def _():
        sum_ref[...] = jnp.zeros(sum_ref.shape, f32)

    @pl.when(at == 0)
    def _():
        dqT_ref[...] = jnp.zeros(dqT_ref.shape, f32)
        for h in range(heads):
            both = doT_ref[head_rows(h), :].astype(f32) * outT_ref[head_rows(h), :].astype(f32)
            delta_ref[h : h + 1, :] = column_sum(both)

    first, last = passage_range(bounds_ref, row, k_start, block, row_len)
    low_half = lax.broadcasted_iota(jnp.int32, (block, PAIR), 1) < HD

    def body(start, window):
        queries = pl.ds(start, window)
        bias_ref[:, :window] = mask_bias(bounds_ref, row, k_start, block, start, window)
        even = {}

        def products(h):
            lanes = pair_lanes(h)
            scores = dot(k_ref[:, lanes], in_pair(h, qT_ref[head_rows(h), queries]))
            grad_prob = dot(v_ref[:, lanes], in_pair(h, doT_ref[head_rows(h), queries]))
            return scores, grad_prob

        def weigh(h, scores, grad_prob):
            shift = bias_ref[:, :window] - log_ref[h : h + 1, queries]
            probs = jnp.exp2(scores * EXP2_SCALE + shift)
            grad_score = probs * (grad_prob - delta_ref[h : h + 1, queries])
            return probs.astype(bf16), grad_score.astype(bf16)

        def gather(h, probs, grad_score):
            lanes = pair_lanes(h)
            dv = dot(probs, do_ref[queries, lanes])
            dk = dot(grad_score, q_ref[queries, lanes])
            dqT_ref[head_rows(h), queries] += dot(kT_ref[head_rows(h), :], grad_score)
            if h % 2 == 0:
                even[0] = (dv, dk)
            else:
                dk_ref[:, lanes] = (jnp.where(low_half, even[0][1], dk) * SCORE_SCALE).astype(bf16)
                dv_ref[:, lanes] = jnp.where(low_half, even[0][0], dv).astype(bf16)

        made = products(0)
        held = None
        for h in range(heads):
            now = made
            if h + 1 < heads:
                made = products(h + 1)
            weighed = weigh(h, *now)
            if held is not None:
                gather(h - 1, *held)
            held = weighed
        gather(heads - 1, *held)

    with_window(first, last, row_len, body)
    sum_ref[1:2, :] += column_sum(dv_ref[...].astype(f32))

    @pl.when(at == pl.num_programs(1) - 1)
    def _():
        dq = (dqT_ref[...] * SCORE_SCALE).astype(bf16).T
        dq_ref[...] = dq
        sum_ref[0:1, :] += column_sum(dq.astype(f32))


def attend_rows_back(bounds, qkv, qkvT, do, doT, outT, log, block):
    rows = bounds.shape[0]
    tokens, width = do.shape
    row_len = tokens // rows
    blocks = row_len // block
    whole = pl.BlockSpec((row_len, width), lambda r, b, s: (r, 0))
    wholeT = pl.BlockSpec((width, row_len), lambda r, b, s: (0, r))
    part = pl.BlockSpec((block, width), lambda r, b, s: (r * blocks + b, 0))
    return pl.pallas_call(
        attend_back_kernel,
        grid_spec=pltpu.PrefetchScalarGridSpec(
            num_scalar_prefetch=1,
            grid=(rows, blocks),
            in_specs=[
                pl.BlockSpec((block, width), lambda r, b, s: (r * blocks + b, 1)),
                pl.BlockSpec((width, block), lambda r, b, s: (1, r * blocks + b)),
                pl.BlockSpec((block, width), lambda r, b, s: (r * blocks + b, 2)),
                whole,
                wholeT,
                whole,
                wholeT,
                wholeT,
                pl.BlockSpec((16, row_len), lambda r, b, s: (0, r)),
            ],
            out_specs=[whole, part, part, pl.BlockSpec((8, width), lambda r, b, s: (0, 0))],
            scratch_shapes=[
                pltpu.VMEM((block, max(WINDOWS) * LANES), f32),
                pltpu.VMEM((width, row_len), f32),
                pltpu.VMEM((16, row_len), f32),
            ],
        ),
        out_shape=[shape_of((tokens, width), bf16)] * 3 + [shape_of((8, width), f32)],
        compiler_params=pltpu.CompilerParams(vmem_limit_bytes=VMEM_LIMIT),
        cost_estimate=pl.CostEstimate(
            flops=40 * tokens * row_len * width // 4,
            bytes_accessed=22 * tokens * width,
            transcendentals=0,
        ),
        name="attend_back",
    )(bounds, qkv, qkvT, qkv, qkv, qkvT, do, doT, outT, log)


def gelu_and_slope(x):
    share = 0.5 + 0.5 * lax.erf(x * math.sqrt(0.5))
    density = jnp.exp(x * x * -0.5) * (1.0 / math.sqrt(2.0 * math.pi))
    return x * share, share + x * density


def normalise(values):
    centred = values - jnp.mean(values, axis=-1, keepdims=True)
    scale = lax.rsqrt(jnp.mean(centred * centred, axis=-1, keepdims=True) + 1e-06)
    return centred * scale, scale


def normalise_back(grad, normed, scale):
    along = jnp.mean(grad * normed, axis=-1, keepdims=True)
    return scale * (grad - jnp.mean(grad, axis=-1, keepdims=True) - normed * along)


def dense_kernel(
    side_ref, attn_ref, x_ref, mine_ref, other_ref, wo_ref, wi_ref, wf_ref, vec_ref, bi_ref,
    out_ref, act_ref, gp_ref, gs_ref, low_ref, gr1_ref, gb_ref, do_ref, doT_ref, sum_ref,
    sum_in_ref, slope_ref,
):
    width = x_ref.shape[1]
    inner = bi_ref.shape[1]
    chunk = width
    groups, per_group = wi_ref.shape[:2]
    in_rows = per_group * chunk // inner
    ffo_groups = max(1, groups * chunk // inner)

    def w_out():
        return wo_ref[...].reshape(width, width)

    def w_in(c):
        return wi_ref[:, c * in_rows : (c + 1) * in_rows, :].reshape(width, chunk)

    def w_ffo(c):
        if groups == 1:
            return wf_ref[0, c * chunk : (c + 1) * chunk, :]
        return wf_ref[c * ffo_groups : (c + 1) * ffo_groups].reshape(chunk, width)

    bias_out, gain_a, shift_a, bias_ffo, gain_f, shift_f = [vec_ref[j : j + 1, :] for j in range(6)]

    @pl.when((pl.program_id(0) == 0) & (pl.program_id(1) == 0) & (pl.program_id(2) == 0))
    def _():
        sum_ref[...] = jnp.zeros(sum_ref.shape, f32)
        sum_in_ref[...] = jnp.zeros(sum_in_ref.shape, f32)

    branch = dot(attn_ref[...], w_out()) + bias_out
    normed_a, scale_a = normalise(x_ref[...].astype(f32) + branch)
    hidden = normed_a * gain_a + shift_a
    low = hidden.astype(bf16)
    low_ref[...] = low
    cuts = [slice(c * chunk, (c + 1) * chunk) for c in range(inner // chunk)]
    last = len(cuts) - 1

    second = None
    held = None
    made = dot(low, w_in(0))
    for c, cut in enumerate(cuts):
        pre = made + bi_ref[0:1, cut]
        if c < last:
            made = dot(low, w_in(c + 1))
        value, slope = gelu_and_slope(pre)
        value = value.astype(bf16)
        act_ref[:, cut] = value
        slope_ref[:, cut] = slope.astype(bf16)
        if held is not None:
            term = dot(held, w_ffo(c - 1))
            second = term if second is None else second + term
        held = value
    term = dot(held, w_ffo(last))
    second = term if second is None else second + term

    normed_f, scale_f = normalise(hidden + (second + bias_ffo))
    out_ref[...] = (normed_f * gain_f + shift_f).astype(bf16)
    cot = jnp.where(pl.program_id(1) == side_ref[0], mine_ref[...], other_ref[...]).astype(f32)
    grad_r2 = normalise_back(cot * gain_f, normed_f, scale_f)
    grad_second = grad_r2.astype(bf16)
    gs_ref[...] = grad_second
    sum_ref[0:1, :] += column_sum(cot * normed_f)
    sum_ref[1:2, :] += column_sum(cot)
    sum_ref[2:3, :] += column_sum(grad_second.astype(f32))

    grad_hidden = grad_r2
    held = None
    made = dot_nt(grad_second, w_ffo(0))
    for c, cut in enumerate(cuts):
        grad_act = made
        if c < last:
            made = dot_nt(grad_second, w_ffo(c + 1))
        grad_pre = (grad_act * slope_ref[:, cut].astype(f32)).astype(bf16)
        gp_ref[:, cut] = grad_pre
        sum_in_ref[0:1, cut] += column_sum(grad_pre.astype(f32))
        if held is not None:
            grad_hidden = grad_hidden + dot_nt(held, w_in(c - 1))
        held = grad_pre
    grad_hidden = grad_hidden + dot_nt(held, w_in(last))

    grad_r1 = normalise_back(grad_hidden * gain_a, normed_a, scale_a)
    gr1_ref[...] = grad_r1
    grad_branch = grad_r1.astype(bf16)
    gb_ref[...] = grad_branch
    sum_ref[3:4, :] += column_sum(grad_hidden * normed_a)
    sum_ref[4:5, :] += column_sum(grad_hidden)
    sum_ref[5:6, :] += column_sum(grad_branch.astype(f32))
    grad_attn = dot_nt(grad_branch, w_out()).astype(bf16)
    do_ref[...] = grad_attn
    doT_ref[...] = grad_attn.T


def dense(side, attn, x, mine, other, weights, vectors, bias_in, block):
    rows, half, width = mine.shape
    tokens = 2 * rows * half
    inner = bias_in.shape[1]
    block = min(block, half)
    blocks = half // block
    mine_at, other_at = halves(block, blocks)

    def at(r, h, b, s):
        return ((r * 2 + h) * blocks + b, 0)

    narrow = pl.BlockSpec((block, width), at)
    wide = pl.BlockSpec((block, inner), at)

    def held(shape, index):
        return pl.BlockSpec(shape, lambda *_: index, pipeline_mode=pl.Buffered(1))

    return pl.pallas_call(
        dense_kernel,
        grid_spec=pltpu.PrefetchScalarGridSpec(
            num_scalar_prefetch=1,
            grid=(rows, 2, blocks),
            in_specs=[
                narrow,
                narrow,
                pl.BlockSpec((block, width), mine_at),
                pl.BlockSpec((block, width), other_at),
            ]
            + [held(shape, index) for _, shape, index in weights]
            + [held(vectors.shape, (0, 0)), held(bias_in.shape, (0, 0))],
            out_specs=[
                narrow, wide, wide, narrow, narrow, narrow, narrow, narrow,
                pl.BlockSpec((width, block), lambda *i: (0, at(*i)[0])),
                pl.BlockSpec((8, width), lambda *_: (0, 0)),
                pl.BlockSpec((8, inner), lambda *_: (0, 0)),
            ],
            scratch_shapes=[pltpu.VMEM((block, inner), bf16)],
        ),
        out_shape=[
            shape_of((tokens, width), bf16),
            shape_of((tokens, inner), bf16),
            shape_of((tokens, inner), bf16),
            shape_of((tokens, width), bf16),
            shape_of((tokens, width), bf16),
            shape_of((tokens, width), f32),
            shape_of((tokens, width), bf16),
            shape_of((tokens, width), bf16),
            shape_of((width, tokens), bf16),
            shape_of((8, width), f32),
            shape_of((8, inner), f32),
        ],
        compiler_params=pltpu.CompilerParams(vmem_limit_bytes=VMEM_LIMIT),
        cost_estimate=pl.CostEstimate(
            flops=2 * tokens * width * (2 * width + 4 * inner),
            bytes_accessed=tokens * (22 * width + 4 * inner) + 4 * width * inner,
            transcendentals=2 * tokens * inner,
        ),
        name="dense",
    )(
        side, attn, x, mine.reshape(-1, width), other.reshape(-1, width),
        *[array for array, _, _ in weights], vectors, bias_in,
    )


def product_kernel(a_ref, b_ref, *rest):
    out_ref = rest[-1]
    out_ref[...] = dot_tn(a_ref[...], b_ref[...]).astype(bf16).reshape(out_ref.shape)


def product_into(buffer, shape, a, b, out_block, out_at, a_moves, steps):
    tokens = a.shape[0]
    a_cols = a.shape[1] // (steps if a_moves else 1)
    b_cols = b.shape[1] // (1 if a_moves else steps)
    moving = {"index_map": lambda i: (0, i)}
    still = {"index_map": lambda i: (0, 0), "pipeline_mode": pl.Buffered(1)}
    in_specs = [
        pl.BlockSpec((tokens, a_cols), **(moving if a_moves else still)),
        pl.BlockSpec((tokens, b_cols), **(still if a_moves else moving)),
    ]
    operands = [a, b]
    aliases = {}
    if buffer is not None:
        in_specs.append(pl.BlockSpec(memory_space=pl.ANY))
        operands.append(buffer)
        aliases = {2: 0}
    return pl.pallas_call(
        product_kernel,
        grid=(steps,),
        in_specs=in_specs,
        out_specs=pl.BlockSpec(out_block, out_at),
        out_shape=shape_of(shape, bf16),
        input_output_aliases=aliases,
        compiler_params=pltpu.CompilerParams(vmem_limit_bytes=VMEM_LIMIT),
        cost_estimate=pl.CostEstimate(
            flops=2 * tokens * a.shape[1] * b.shape[1],
            bytes_accessed=2 * (a.size + b.size + a.shape[1] * b.shape[1]),
            transcendentals=0,
        ),
        name="product",
    )(*operands)


def input_grad_kernel(dq_ref, dk_ref, dv_ref, gr1_ref, w_ref, out_ref):
    width = out_ref.shape[1]
    total = gr1_ref[...]
    for j, ref in enumerate((dq_ref, dk_ref, dv_ref)):
        total = total + dot_nt(ref[...], w_ref[:, j * width : (j + 1) * width])
    out_ref[...] = total.astype(bf16)


def input_grad(dq, dk, dv, grad_r1, weight, block):
    tokens, width = dq.shape
    block = min(block, tokens)
    part = pl.BlockSpec((block, width), lambda i: (i, 0))
    return pl.pallas_call(
        input_grad_kernel,
        grid=(tokens // block,),
        in_specs=[part] * 4
        + [pl.BlockSpec(weight.shape, lambda i: (0, 0), pipeline_mode=pl.Buffered(1))],
        out_specs=part,
        out_shape=shape_of((tokens, width), bf16),
        compiler_params=pltpu.CompilerParams(vmem_limit_bytes=VMEM_LIMIT),
        cost_estimate=pl.CostEstimate(
            flops=6 * tokens * width * width,
            bytes_accessed=12 * tokens * width + 6 * width * width,
            transcendentals=0,
        ),
        name="input_grad",
    )(dq, dk, dv, grad_r1, weight)


def split_heads(values):
    return values.reshape(values.shape[0], values.shape[1], H, HD)


def gathered_probs(queries, keys, allowed):
    scores = jnp.einsum("rqhd,rkhd->rhqk", queries, keys, preferred_element_type=f32)
    return jax.nn.softmax(jnp.where(allowed, scores * SCORE_SCALE, MASKED), axis=-1)


def attend_gathered(bounds, qkv, rows, seq_index):
    width = qkv.shape[1] // 3
    parts = qkv.reshape(rows, -1, 3 * width)
    tok_seq = parts.shape[1]
    whole = lax.all_gather(parts[:, :, width:], "seq", axis=1, tiled=True)
    row_len = whole.shape[1]
    queries = split_heads(parts[:, :, :width])
    keys = split_heads(whole[:, :, :width])
    values = split_heads(whole[:, :, width:])
    positions = jnp.arange(row_len, dtype=jnp.int32)
    segments = jnp.sum((positions[None, :, None] >= bounds[:, None, :]).astype(jnp.int32), axis=2)
    mine = lax.dynamic_slice_in_dim(segments, seq_index * tok_seq, tok_seq, 1)
    allowed = mine[:, None, :, None] == segments[:, None, None, :]
    probs = gathered_probs(queries, keys, allowed)
    attended = jnp.einsum(
        "rhqk,rkhd->rqhd", probs.astype(bf16), values, preferred_element_type=f32
    )
    return attended.astype(bf16).reshape(-1, width), (queries, keys, values, allowed)


def attend_gathered_back(saved, attn, do):
    queries, keys, values, allowed = saved
    rows, tok_seq = queries.shape[:2]
    width = attn.shape[1]
    probs = gathered_probs(queries, keys, allowed)
    do = do.reshape(rows, tok_seq, H, HD)
    delta = jnp.sum(do.astype(f32) * attn.reshape(do.shape).astype(f32), axis=-1)
    grad_prob = jnp.einsum("rqhd,rkhd->rhqk", do, values, preferred_element_type=f32)
    grad_score = (probs * (grad_prob - delta.transpose(0, 2, 1)[..., None])).astype(bf16)
    dq = jnp.einsum("rhqk,rkhd->rqhd", grad_score, keys, preferred_element_type=f32) * SCORE_SCALE
    dk = (
        jnp.einsum("rhqk,rqhd->rkhd", grad_score, queries, preferred_element_type=f32)
        * SCORE_SCALE
    )
    dv = jnp.einsum("rhqk,rqhd->rkhd", probs.astype(bf16), do, preferred_element_type=f32)
    pair = jnp.concatenate([dk.reshape(rows, -1, width), dv.reshape(rows, -1, width)], axis=-1)
    pair = lax.psum_scatter(pair.astype(bf16), "seq", scatter_dimension=1, tiled=True)
    pair = pair.reshape(-1, 2 * width)
    dq = dq.astype(bf16).reshape(-1, width)
    dk, dv = pair[:, :width], pair[:, width:]
    sums = jnp.stack([jnp.sum(dq.astype(f32), axis=0), jnp.sum(dv.astype(f32), axis=0)])
    return dq, dk, dv, sums


def collect_kernel(sums_qv_ref, sums_ref, sums_in_ref, *refs):
    out_ref = refs[-1]
    shards = out_ref.shape[0]
    qv = jnp.concatenate([sums_qv_ref[0:1, :], sums_qv_ref[1:2, :]], axis=1)
    rows = [sums_ref[j : j + 1, :] for j in range(6)]
    found = []
    for v in (qv, rows[5], rows[3], rows[4], sums_in_ref[0:1, :], rows[2], rows[0], rows[1]):
        found.extend(gather_vector(v, shards))
    out_ref[...] = jnp.zeros(out_ref.shape, bf16)
    for j, v in enumerate(found):
        out_ref[:, j : j + 1, :LANES] = v.astype(bf16).reshape(shards, 1, LANES)


def collect(buffer, sums_qv, sums, sums_in, shards):
    rows = buffer.shape[1]
    width = buffer.shape[2]
    whole = [pl.BlockSpec(v.shape, lambda i: (0, 0)) for v in (sums_qv, sums, sums_in)]
    return pl.pallas_call(
        collect_kernel,
        grid=(1,),
        in_specs=whole + [pl.BlockSpec(memory_space=pl.ANY)],
        out_specs=pl.BlockSpec((shards, 16, width), lambda i: (0, rows // 16 - 1, 0)),
        out_shape=shape_of(buffer.shape, bf16),
        input_output_aliases={3: 0},
        compiler_params=pltpu.CompilerParams(vmem_limit_bytes=VMEM_LIMIT),
        name="collect",
    )(sums_qv, sums, sums_in, buffer)


def swapped(values):
    return lax.ppermute(values, "seq", [(0, 1), (1, 0)])


def halves_of_rows(values, seq_index):
    mine = values.shape[0] // 2
    return (
        lax.dynamic_slice_in_dim(values, seq_index * mine, mine, 0),
        swapped(lax.dynamic_slice_in_dim(values, (1 - seq_index) * mine, mine, 0)),
    )


def rows_of_halves(values, seq_index):
    half = values.shape[1] // 2
    kept = lax.dynamic_slice_in_dim(values, seq_index * half, half, 1)
    came = swapped(lax.dynamic_slice_in_dim(values, (1 - seq_index) * half, half, 1))
    first = seq_index == 0
    return jnp.concatenate([jnp.where(first, kept, came), jnp.where(first, came, kept)], axis=0)


def coordinates(count):
    return ((2, 1), (count // 8, 2), (4, count // 4))


def turned(values, axis, size, stride, step):
    perm = []
    for i in range(lax.axis_size(axis)):
        at = (i // stride) % size
        perm.append((i, i + ((at + step) % size - at) * stride))
    return lax.ppermute(values, axis, perm)


def scatter_sum(values, axis):
    index = lax.axis_index(axis)
    rest = values
    for size, stride in coordinates(lax.axis_size(axis)):
        blocks = rest.reshape((-1, size) + values.shape[1:])
        here = (index // stride) % size
        total = lax.dynamic_index_in_dim(blocks, here, 1, False).astype(f32)
        for step in range(1, size):
            piece = lax.dynamic_index_in_dim(blocks, (here + step) % size, 1, False)
            total = total + turned(piece, axis, size, stride, step).astype(f32)
        rest = total.astype(values.dtype)
    return rest[0]


def gather_pieces(values, axis):
    pieces = [(values, (0, 0, 0))]
    for at, (size, stride) in reversed(list(enumerate(coordinates(lax.axis_size(axis))))):
        more = []
        for piece, back in pieces:
            for step in range(1, size):
                came = turned(piece, axis, size, stride, step)
                more.append((came, back[:at] + (step,) + back[at + 1 :]))
        pieces = pieces + more
    return pieces


def piece_owner(index, back, count):
    owner = jnp.int32(0)
    for (size, stride), step in zip(coordinates(count), back):
        owner = owner + lax.rem(lax.rem(index // stride, size) + (size - step), size) * stride
    return owner


def per_device(
    tokens,
    weight_qkv,
    bias_qv,
    weight_out,
    bias_out,
    gain_attn,
    shift_attn,
    weight_in,
    bias_in,
    weight_ffo,
    bias_ffo,
    gain_ffn,
    shift_ffn,
    lengths,
    cotangent,
):
    rows, tok_seq, width = tokens.shape
    seq_count = lax.axis_size("seq")
    seq_index = lax.axis_index("seq")
    shards = lax.axis_size("dp")
    shard = weight_qkv.shape[0]
    by_rows = seq_count == 2 and rows % 2 == 0 and shards % 8 == 0 and shard % 16 == 0
    inner = weight_in.shape[1]
    chunks = inner // width
    token_count = rows * tok_seq

    small = (bias_qv, bias_out, gain_attn, shift_attn, bias_in, bias_ffo, gain_ffn, shift_ffn)
    first, others = lower(weight_qkv, weight_in, weight_ffo, weight_out, small)
    if by_rows:
        first = gather_pieces(first, "dp")
    else:
        first = [(lax.all_gather(first, "dp", axis=0, tiled=True), None)]
    others = lax.all_gather(others[None], "dp", axis=0, tiled=True)
    if shard % 16 == 0:
        weights = (
            (others, (shards, shard, width), (0, 2 * chunks, 0)),
            (others, (shards, chunks * shard, width), (0, 0, 0)),
            (others, (shards, chunks * shard, width), (0, 1, 0)),
        )
    else:
        part = chunks * shard
        w_in = others[:, :part].reshape(shards, chunks, shard, width).transpose(1, 0, 2, 3)
        w_in = w_in.reshape(1, inner, width)
        w_ffo = others[:, part : 2 * part].reshape(1, inner, width)
        w_out = others[:, 2 * part :].reshape(1, width, width)
        weights = [(w, w.shape, (0, 0, 0)) for w in (w_out, w_in, w_ffo)]

    bounds = jnp.cumsum(lengths, axis=1)
    if by_rows:
        mine = rows // 2
        bounds = lax.dynamic_slice_in_dim(bounds, seq_index * mine, mine, 0)
        side = jnp.stack([seq_index, lax.axis_index("dp")]).astype(jnp.int32)
        x_halves = halves_of_rows(tokens, seq_index)
        cot_halves = halves_of_rows(cotangent, seq_index)
    else:
        side = jnp.zeros((2,), jnp.int32)
        x_halves = tokens.reshape(2, 1, -1, width)
        cot_halves = cotangent.reshape(2, 1, -1, width)

    x, qkv, qkvT, w_qkv, vec, in_bias = project(side, *x_halves, first, inner, BLOCK)
    if by_rows:
        attn, attnT, log = attend_rows(bounds, qkv, qkvT, BLOCK)
    else:
        attn, saved = attend_gathered(bounds, qkv, rows, seq_index)
    out, act, gp, gs, low, gr1, gb, do, doT, sums, sums_in = dense(
        side, attn, x, *cot_halves, weights, vec, in_bias, BLOCK
    )
    if by_rows:
        out = rows_of_halves(out.reshape(mine, -1, width), seq_index)
    else:
        out = out.reshape(rows, tok_seq, width)

    per_shard = (2 * chunks + 1) * shard
    if shard % 16 == 0:
        grads = product_into(
            None, (shards, per_shard, width), low, gp,
            (shards, shard, width), lambda i: (0, i, 0), False, chunks,
        )
        grads = product_into(
            grads, grads.shape, act, gs,
            (shards // chunks, chunks * shard, width), lambda i: (i, 1, 0), True, chunks,
        )
        grads = product_into(
            grads, grads.shape, attn, gb,
            (shards, shard, width), lambda i: (0, 2 * chunks, 0), False, 1,
        )
    else:
        g_in = dot_tn(low, gp).astype(bf16).reshape(shards, shard, chunks, width)
        g_in = g_in.transpose(0, 2, 1, 3).reshape(shards, chunks * shard, width)
        g_ffo = dot_tn(act, gs).astype(bf16).reshape(shards, chunks * shard, width)
        g_out = dot_tn(attn, gb).astype(bf16).reshape(shards, shard, width)
        grads = jnp.concatenate([g_in, g_ffo, g_out], axis=1)
    grads, do = lax.optimization_barrier((grads, do))
    reduced = lax.psum_scatter(grads, "dp", scatter_dimension=0, tiled=True)[0]

    if by_rows:
        dq, dk, dv, sums_qv = attend_rows_back(bounds, qkv, qkvT, do, doT, attnT, log, BLOCK)
    else:
        dq, dk, dv, sums_qv = attend_gathered_back(saved, attn, do)

    if by_rows:
        g_qkv = []
        for g in (dq, dk, dv):
            extra = 16 if g is dv else 0
            g_qkv.append(
                product_into(
                    None, (shards, shard + extra, width), x, g,
                    (shards, shard, width), lambda i: (0, 0, 0), False, 1,
                )
            )
        g_qkv[2] = collect(g_qkv[2], sums_qv, sums, sums_in, shards)
        g_qkv = [scatter_sum(g, "dp") for g in g_qkv]
    else:
        vectors = jnp.zeros((shards, 16, width), bf16)
        vectors = collect(vectors, sums_qv, sums, sums_in, shards)
        g_qkv = [dot_tn(x, g).astype(bf16).reshape(shards, shard, width) for g in (dq, dk, dv)]
        g_qkv[2] = jnp.concatenate([g_qkv[2], vectors], axis=1)
        g_qkv = [lax.psum_scatter(g, "dp", scatter_dimension=0, tiled=True)[0] for g in g_qkv]

    grad_x = input_grad(dq, dk, dv, gr1, w_qkv, BLOCK)
    if by_rows:
        grad_x = rows_of_halves(grad_x.reshape(mine, -1, width), seq_index)
    else:
        grad_x = grad_x.reshape(rows, tok_seq, width)

    def over_seq(values):
        if seq_count == 2:
            return values.astype(f32) + swapped(values).astype(f32)
        return lax.psum(values, "seq").astype(f32)

    reduced = over_seq(reduced)
    g_qkv = [over_seq(g) for g in g_qkv]
    vectors = g_qkv[2][shard:, :LANES]
    d_qkv = jnp.concatenate([g[:shard] for g in g_qkv], axis=1)
    d_in = reduced[: chunks * shard].reshape(chunks, shard, width).transpose(1, 0, 2)
    d_in = d_in.reshape(shard, inner)
    d_ffo = reduced[chunks * shard : 2 * chunks * shard]
    d_out = reduced[2 * chunks * shard :]
    sizes = [v.shape[0] for v in small]
    d_small = []
    for row, size in zip(vector_rows(sizes)[0], sizes):
        d_small.append(vectors[row : row - (-size // LANES)].reshape(-1)[:size])
    g_qv, g_bo, g_ga, g_sa, g_bi, g_bf, g_gf, g_sf = d_small
    return (
        out, grad_x, d_qkv, g_qv, d_out, g_bo, g_ga, g_sa, d_in, g_bi, d_ffo,
        g_bf, g_gf, g_sf,
    )


def solution(mesh):
    by_token = P("dp", "seq", None)
    weight = P("dp", None)
    vector = P("dp")
    params = (
        weight, vector, weight, vector, vector, vector, weight, vector, weight, vector, vector,
        vector,
    )
    return jax.shard_map(
        per_device,
        mesh=mesh,
        in_specs=(by_token,) + params + (weight, by_token),
        out_specs=(by_token, by_token) + params,
        check_vma=False,
    )
```

```python
import functools
import math

import jax
import jax.numpy as jnp
from jax import lax
from jax.experimental import pallas as pl
from jax.experimental.pallas import tpu as pltpu
from jax.sharding import PartitionSpec as P

H = 12
HD = 64
PAIR = 2 * HD
LANES = 128
f32 = jnp.float32
bf16 = jnp.bfloat16
SCORE_SCALE = 1.0 / math.sqrt(HD)
EXP2_SCALE = SCORE_SCALE * math.log2(math.e)
MASKED = -1e30
VMEM_LIMIT = 60 << 20
BLOCK = 256
COST = 4
GROUP = H
GROUP_ROWS = -(-GROUP // 8) * 8
WINDOWS = (2, 3, 4, 5, 6)


def dot(a, b):
    return jnp.dot(a, b, preferred_element_type=f32)


def dot_nt(a, b):
    return lax.dot_general(a, b, (((1,), (1,)), ((), ())), preferred_element_type=f32)


def dot_tn(a, b):
    return lax.dot_general(a, b, (((0,), (0,)), ((), ())), preferred_element_type=f32)


def column_sum(values):
    return jnp.sum(values, axis=0, keepdims=True)


def cost(flops, bytes_accessed, transcendentals=0):
    return pl.CostEstimate(
        flops=flops // COST, bytes_accessed=bytes_accessed // COST, transcendentals=transcendentals // COST
    )


def shape_of(shape, dtype):
    return jax.ShapeDtypeStruct(shape, dtype)


def vector_rows(sizes):
    rows = []
    at = 0
    for size in sizes:
        rows.append(at)
        at += -(-size // LANES)
    return rows, at


def lower_kernel(*refs):
    w_qkv, w_in, w_ffo, w_out = refs[:4]
    small = refs[4:-3]
    first_ref, others_ref, block_ref = refs[-3:]
    columns = w_qkv.shape[1]
    shard, width = w_out.shape
    first_ref[:, :columns] = w_qkv[...].astype(bf16)
    block_ref[...] = jnp.zeros(block_ref.shape, f32)
    for ref, row in zip(small, vector_rows([r.shape[1] for r in small])[0]):
        size = ref.shape[1]
        for at in range(0, size, LANES):
            n = min(LANES, size - at)
            block_ref[row : row + 1, :n] = ref[:, at : at + n]
            row += 1
    first_ref[:, columns:] = block_ref[...].astype(bf16)
    chunks = w_in.shape[1] // width
    for c in range(chunks):
        others_ref[c * shard : (c + 1) * shard, :] = w_in[:, c * width : (c + 1) * width].astype(bf16)
    others_ref[chunks * shard : 2 * chunks * shard, :] = w_ffo[...].astype(bf16)
    others_ref[2 * chunks * shard :, :] = w_out[...].astype(bf16)


def lower(w_qkv, w_in, w_ffo, w_out, small):
    shard, columns = w_qkv.shape
    width = w_out.shape[1]
    chunks = w_in.shape[1] // width
    return pl.pallas_call(
        lower_kernel,
        out_shape=[
            shape_of((shard, columns + LANES), bf16),
            shape_of(((2 * chunks + 1) * shard, width), bf16),
        ],
        scratch_shapes=[pltpu.VMEM((shard, LANES), f32)],
        compiler_params=pltpu.CompilerParams(vmem_limit_bytes=VMEM_LIMIT),
        name="lower",
    )(w_qkv, w_in, w_ffo, w_out, *[v.reshape(1, -1) for v in small])


def places(total, size):
    at = lax.broadcasted_iota(jnp.int32, (1, total), 1)
    return at % size, at // size


def picker(place, at):
    lane = lax.broadcasted_iota(jnp.int32, (LANES, place.shape[1]), 0)
    return jnp.where(place == lane + at, 1.0, 0.0).astype(bf16)


def spread_vector(block, row, size, shards):
    place, owner = places(size * shards, size)
    found = jnp.zeros((shards, size * shards), f32)
    for at in range(0, size, LANES):
        found = found + dot(block[:, row + at // LANES, :].astype(bf16), picker(place, at))
    index = lax.broadcasted_iota(jnp.int32, found.shape, 0)
    return column_sum(jnp.where(owner == index, found, 0.0))


def gather_vector(vector, shards):
    total = vector.shape[1]
    size = total // shards
    place, owner = places(total, size)
    index = lax.broadcasted_iota(jnp.int32, (shards, total), 0)
    own = jnp.where(owner == index, vector, 0.0).astype(bf16)
    return [dot_nt(own, picker(place, at)) for at in range(0, size, LANES)]


def project_kernel(place_ref, mine_ref, other_ref, *refs, shards, pieces):
    x_ref, out_ref, outT_ref, w_ref, vec_ref, bi_ref, bias_ref, sems = refs[len(pieces) :]
    width = x_ref.shape[1]
    columns = out_ref.shape[1]
    shard = width // shards

    @pl.when((pl.program_id(0) == 0) & (pl.program_id(1) == 0) & (pl.program_id(2) == 0))
    def _():
        copies = []
        for j, (ref, back) in enumerate(zip(refs, pieces)):
            start = jnp.int32(0) if back is None else piece_owner(place_ref[1], back, shards) * shard
            rows = pl.ds(pl.multiple_of(start, 16), ref.shape[0])
            copies.append(pltpu.make_async_copy(ref, w_ref.at[rows, :], sems.at[j]))
        for copy in copies:
            copy.start()
        for copy in copies:
            copy.wait()
        block = w_ref[:, columns:].astype(f32).reshape(shards, shard, LANES)
        inner = bi_ref.shape[1]
        totals = (2 * width, width, width, width, inner, width, width, width)
        sizes = [total // shards for total in totals]
        found = [
            spread_vector(block, row, size, shards)
            for row, size in zip(vector_rows(sizes)[0], sizes)
        ]
        bias_ref[0:1, :width] = found[0][:, :width]
        bias_ref[0:1, width : 2 * width] = jnp.zeros((1, width), f32)
        bias_ref[0:1, 2 * width :] = found[0][:, width:]
        bi_ref[0:1, :] = found[4]
        for j, v in enumerate(found[1:4] + found[5:]):
            vec_ref[j : j + 1, :] = v

    x = jnp.where(pl.program_id(1) == place_ref[0], mine_ref[...], other_ref[...])
    x_ref[...] = x
    low = (dot(x, w_ref[:, :columns]) + bias_ref[0:1, :]).astype(bf16)
    out_ref[...] = low
    outT_ref[...] = low.T


def halves(mine, other, block):
    rows, half, _ = other.shape
    blocks = half // block
    skip = rows if mine.shape[0] > rows else 0

    def at(used, r, h, b):
        rest = jnp.where(h == 0, 0, blocks - 1)
        return (r * blocks + jnp.where(used, b, rest), 0)

    return (
        lambda r, h, b, s: at(h == s[0], r + s[0] * skip, h, b),
        lambda r, h, b, s: at(h != s[0], r, h, b),
    )


def project(place, mine, other, weight, inner, block):
    rows, half, width = other.shape
    block = min(block, half)
    blocks = half // block
    columns = 3 * width
    tokens = 2 * rows * half
    shards = lax.axis_size("dp")
    mine_at, other_at = halves(mine, other, block)

    def at(r, h, b, s):
        return ((r * 2 + h) * blocks + b, 0)

    return pl.pallas_call(
        functools.partial(project_kernel, shards=shards, pieces=[back for _, back in weight]),
        grid_spec=pltpu.PrefetchScalarGridSpec(
            num_scalar_prefetch=1,
            grid=(rows, 2, blocks),
            in_specs=[
                pl.BlockSpec((block, width), mine_at),
                pl.BlockSpec((block, width), other_at),
            ]
            + [pl.BlockSpec(memory_space=pl.ANY)] * len(weight),
            out_specs=[
                pl.BlockSpec((block, width), at),
                pl.BlockSpec((block, columns), at),
                pl.BlockSpec((columns, block), lambda *i: (0, at(*i)[0])),
                pl.BlockSpec((width, columns + LANES), lambda *_: (0, 0)),
                pl.BlockSpec((8, width), lambda *_: (0, 0)),
                pl.BlockSpec((8, inner), lambda *_: (0, 0)),
            ],
            scratch_shapes=[
                pltpu.VMEM((8, columns), f32),
                pltpu.SemaphoreType.DMA((len(weight),)),
            ],
        ),
        out_shape=[
            shape_of((tokens, width), bf16),
            shape_of((tokens, columns), bf16),
            shape_of((columns, tokens), bf16),
            shape_of((width, columns + LANES), bf16),
            shape_of((8, width), f32),
            shape_of((8, inner), f32),
        ],
        compiler_params=pltpu.CompilerParams(vmem_limit_bytes=VMEM_LIMIT),
        cost_estimate=cost(
            flops=2 * tokens * width * columns,
            bytes_accessed=2 * (2 * tokens * width + 2 * width * columns + 2 * tokens * columns),
            transcendentals=0,
        ),
        name="project",
    )(place, mine.reshape(-1, width), other.reshape(-1, width), *[w for w, _ in weight])


def passage_range(bounds_ref, row, start, size, row_len):
    first = jnp.int32(0)
    last = jnp.int32(row_len)
    for j in range(bounds_ref.shape[1]):
        bound = bounds_ref[row, j]
        first = jnp.where(bound <= start, jnp.maximum(first, bound), first)
        last = jnp.where(bound >= start + size, jnp.minimum(last, bound), last)
    return first, last


def segments_at(bounds_ref, row, positions):
    count = jnp.zeros(positions.shape, jnp.int32)
    for j in range(bounds_ref.shape[1]):
        count = count + (positions >= bounds_ref[row, j]).astype(jnp.int32)
    return count


def with_window(first, last, row_len, body):
    first_tile = first // LANES
    needed = (last + LANES - 1) // LANES - first_tile
    below = 0
    for tiles in WINDOWS:

        @pl.when((needed > below) & (needed <= tiles))
        def _(tiles=tiles):
            start = jnp.minimum(first_tile, row_len // LANES - tiles)
            body(pl.multiple_of(start * LANES, LANES), tiles * LANES)

        below = tiles


def mask_bias(bounds_ref, row, sub_start, sub_len, lane_start, lane_len):
    down = segments_at(
        bounds_ref, row, sub_start + lax.broadcasted_iota(jnp.int32, (sub_len, LANES), 0)
    )
    across = segments_at(
        bounds_ref, row, lane_start + lax.broadcasted_iota(jnp.int32, (1, lane_len), 1)
    )
    down = jnp.concatenate([down] * (lane_len // LANES), axis=1)
    return jnp.where(down == across, 0.0, MASKED).astype(f32)


def head_rows(h):
    return slice(HD * h, HD * h + HD)


def pair_lanes(h):
    return slice(PAIR * (h // 2), PAIR * (h // 2) + PAIR)


def log_row(h):
    return GROUP_ROWS * (h // GROUP) + h % GROUP


def in_pair(h, rows):
    zero = jnp.zeros_like(rows)
    return jnp.concatenate([rows, zero] if h % 2 == 0 else [zero, rows], axis=0)


def attend_kernel(bounds_ref, k_ref, qT_ref, vT_ref, outT_ref, log_ref, bias_ref):
    row = pl.program_id(0)
    row_len, width = k_ref.shape
    block = qT_ref.shape[1]
    heads = width // HD
    q_start = pl.program_id(1) * block
    first, last = passage_range(bounds_ref, row, q_start, block, row_len)

    def body(start, window):
        keys = pl.ds(start, window)
        bias_ref[:window, :] = mask_bias(bounds_ref, row, start, window, q_start, block)

        def score(h):
            return dot(k_ref[keys, pair_lanes(h)], in_pair(h, qT_ref[head_rows(h), :]))

        def weigh(scores):
            masked = scores + bias_ref[:window, :]
            best = jnp.max(masked, axis=0, keepdims=True)
            return best, jnp.exp2((masked - best) * EXP2_SCALE).astype(bf16)

        def attend(h, best, weights):
            values = jnp.concatenate(
                [vT_ref[head_rows(h), keys], jnp.ones((16, window), bf16)], axis=0
            )
            summed = dot(values, weights)
            total = summed[HD : HD + 1]
            outT_ref[head_rows(h), :] = (summed[:HD] * (1.0 / total)).astype(bf16)
            at = log_row(h)
            log_ref[at : at + 1, :] = best * EXP2_SCALE + jnp.log2(total)

        scores = [score(0), score(1)]
        held = None
        for h in range(0, heads, 2):
            now = scores
            if h + 2 < heads:
                scores = [score(h + 2), score(h + 3)]
            weighed = [weigh(s) for s in now]
            if held is not None:
                attend(h - 2, *held[0])
                attend(h - 1, *held[1])
            held = weighed
        attend(heads - 2, *held[0])
        attend(heads - 1, *held[1])

    with_window(first, last, row_len, body)


def attend_rows(bounds, qkv, qkvT, block):
    rows = bounds.shape[0]
    tokens = qkv.shape[0]
    width = qkv.shape[1] // 3
    row_len = tokens // rows
    blocks = row_len // block
    return pl.pallas_call(
        attend_kernel,
        grid_spec=pltpu.PrefetchScalarGridSpec(
            num_scalar_prefetch=1,
            grid=(rows, blocks),
            in_specs=[
                pl.BlockSpec((row_len, width), lambda r, b, s: (r, 1)),
                pl.BlockSpec((width, block), lambda r, b, s: (0, r * blocks + b)),
                pl.BlockSpec((width, row_len), lambda r, b, s: (2, r)),
            ],
            out_specs=[
                pl.BlockSpec((width, block), lambda r, b, s: (0, r * blocks + b)),
                pl.BlockSpec((H // GROUP * GROUP_ROWS, block), lambda r, b, s: (0, r * blocks + b)),
            ],
            scratch_shapes=[pltpu.VMEM((max(WINDOWS) * LANES, block), f32)],
        ),
        out_shape=[
            shape_of((width, tokens), bf16),
            shape_of((H // GROUP * GROUP_ROWS, tokens), f32),
        ],
        compiler_params=pltpu.CompilerParams(vmem_limit_bytes=VMEM_LIMIT),
        cost_estimate=cost(
            flops=16 * tokens * row_len * width // 4,
            bytes_accessed=10 * tokens * width,
            transcendentals=0,
        ),
        name="attend",
    )(bounds, qkv, qkvT, qkvT)


def attend_back_kernel(
    bounds_ref, k_ref, kT_ref, v_ref, q_ref, qT_ref, do_ref, doT_ref, outT_ref, log_ref,
    grad_ref, sum_ref, bias_ref, dqT_ref, delta_ref,
):
    row = pl.program_id(1)
    at = pl.program_id(2)
    row_len, width = q_ref.shape
    block = k_ref.shape[0]
    heads = width // HD
    k_start = at * block
    keys = pl.ds(pl.multiple_of(k_start, block), block)

    @pl.when((row == 0) & (at == 0))
    def _():
        sum_ref[...] = jnp.zeros(sum_ref.shape, f32)

    @pl.when(at == 0)
    def _():
        dqT_ref[...] = jnp.zeros(dqT_ref.shape, f32)
        for h in range(heads):
            both = doT_ref[head_rows(h), :].astype(f32) * outT_ref[head_rows(h), :].astype(f32)
            delta_ref[h : h + 1, :] = column_sum(both)

    first, last = passage_range(bounds_ref, row, k_start, block, row_len)
    low_half = lax.broadcasted_iota(jnp.int32, (block, PAIR), 1) < HD

    def body(start, window):
        queries = pl.ds(start, window)
        bias_ref[:, :window] = mask_bias(bounds_ref, row, k_start, block, start, window)
        even = {}

        def products(h):
            lanes = pair_lanes(h)
            scores = dot(k_ref[:, lanes], in_pair(h, qT_ref[head_rows(h), queries]))
            grad_prob = dot(v_ref[:, lanes], in_pair(h, doT_ref[head_rows(h), queries]))
            return scores, grad_prob

        def weigh(h, scores, grad_prob):
            shift = bias_ref[:, :window] - log_ref[h : h + 1, queries]
            probs = jnp.exp2(scores * EXP2_SCALE + shift)
            grad_score = probs * (grad_prob - delta_ref[h : h + 1, queries])
            return probs.astype(bf16), grad_score.astype(bf16)

        def gather(h, probs, grad_score):
            lanes = pair_lanes(h)
            dv = dot(probs, do_ref[queries, lanes])
            dk = dot(grad_score, q_ref[queries, lanes])
            dqT_ref[head_rows(h), queries] += dot(kT_ref[head_rows(h), :], grad_score)
            if h % 2 == 0:
                even[0] = (dv, dk)
            else:
                dk = jnp.where(low_half, even[0][1], dk) * SCORE_SCALE
                dv = jnp.where(low_half, even[0][0], dv)
                for part, value in ((1, dk), (2, dv)):
                    at_lanes = slice(part * width + lanes.start, part * width + lanes.stop)
                    grad_ref[keys, at_lanes] = value.astype(bf16)

        made = products(0)
        held = None
        for h in range(heads):
            now = made
            if h + 1 < heads:
                made = products(h + 1)
            weighed = weigh(h, *now)
            if held is not None:
                gather(h - 1, *held)
            held = weighed
        gather(heads - 1, *held)

    with_window(first, last, row_len, body)

    @pl.when(at == pl.num_programs(2) - 1)
    def _():
        grad_ref[:, :width] = (dqT_ref[...] * SCORE_SCALE).astype(bf16).T
        sum_ref[0:1, :] += column_sum(grad_ref[:, :width].astype(f32))
        sum_ref[1:2, :] += column_sum(grad_ref[:, 2 * width :].astype(f32))


def attend_rows_back(bounds, qkv, qkvT, do, doT, outT, log, first, count, block):
    rows = bounds.shape[0]
    tokens = do.shape[0]
    width = GROUP * HD
    groups = H // GROUP
    row_len = tokens // rows
    blocks = row_len // block
    whole = pl.BlockSpec((row_len, width), lambda g, r, b, s: (r, first + g))
    wholeT = pl.BlockSpec((width, row_len), lambda g, r, b, s: (first + g, r))

    def part(j):
        return lambda g, r, b, s: (r * blocks + b, j * groups + first + g)

    def partT(j):
        return lambda g, r, b, s: (j * groups + first + g, r * blocks + b)

    return pl.pallas_call(
        attend_back_kernel,
        grid_spec=pltpu.PrefetchScalarGridSpec(
            num_scalar_prefetch=1,
            grid=(count, rows, blocks),
            in_specs=[
                pl.BlockSpec((block, width), part(1)),
                pl.BlockSpec((width, block), partT(1)),
                pl.BlockSpec((block, width), part(2)),
                whole,
                wholeT,
                whole,
                wholeT,
                wholeT,
                pl.BlockSpec((GROUP_ROWS, row_len), lambda g, r, b, s: (first + g, r)),
            ],
            out_specs=[
                pl.BlockSpec((row_len, 3 * width), lambda g, r, b, s: (r, g)),
                pl.BlockSpec((8, width), lambda g, r, b, s: (0, g)),
            ],
            scratch_shapes=[
                pltpu.VMEM((block, max(WINDOWS) * LANES), f32),
                pltpu.VMEM((width, row_len), f32),
                pltpu.VMEM((GROUP_ROWS, row_len), f32),
            ],
        ),
        out_shape=[
            shape_of((tokens, 3 * width * count), bf16),
            shape_of((8, width * count), f32),
        ],
        compiler_params=pltpu.CompilerParams(vmem_limit_bytes=VMEM_LIMIT),
        cost_estimate=cost(
            flops=40 * tokens * row_len * width * count // 4,
            bytes_accessed=22 * tokens * width * count,
            transcendentals=0,
        ),
        name="attend_back",
    )(bounds, qkv, qkvT, qkv, qkv, qkvT, do, doT, outT, log)


def gelu_and_slope(x):
    share = 0.5 + 0.5 * lax.erf(x * math.sqrt(0.5))
    density = jnp.exp(x * x * -0.5) * (1.0 / math.sqrt(2.0 * math.pi))
    return x * share, share + x * density


def normalise(values):
    centred = values - jnp.mean(values, axis=-1, keepdims=True)
    scale = lax.rsqrt(jnp.mean(centred * centred, axis=-1, keepdims=True) + 1e-06)
    return centred * scale, scale


def normalise_back(grad, normed, scale):
    along = jnp.mean(grad * normed, axis=-1, keepdims=True)
    return scale * (grad - jnp.mean(grad, axis=-1, keepdims=True) - normed * along)


class Weights:
    def __init__(self, width, inner, w_out=None, w_in=None, w_ffo=None):
        self.width = width
        self.inner = inner
        self.refs = (w_out, w_in, w_ffo)

    def out(self):
        return self.refs[0][...].reshape(self.width, self.width)

    def into(self, c):
        ref = self.refs[1]
        rows = ref.shape[1] * self.width // self.inner
        return ref[:, c * rows : (c + 1) * rows, :].reshape(self.width, self.width)

    def ffo(self, c):
        ref = self.refs[2]
        if ref.shape[0] == 1:
            return ref[0, c * self.width : (c + 1) * self.width, :]
        groups = ref.shape[0] * self.width // self.inner
        return ref[c * groups : (c + 1) * groups].reshape(self.width, self.width)


def dense_kernel(
    side_ref, attn_ref, x_ref, mine_ref, other_ref, wo_ref, wi_ref, wf_ref, vec_ref, bi_ref,
    keep_ref, send_ref, act_ref, gp_ref, gs_ref, low_ref, gr1_ref, gb_ref, do_ref, doT_ref, sum_ref,
    sum_in_ref, slope_ref,
):
    width = x_ref.shape[1]
    inner = bi_ref.shape[1]
    weights = Weights(width, inner, wo_ref, wi_ref, wf_ref)
    bias_out, gain_a, shift_a, bias_ffo, gain_f, shift_f = [vec_ref[j : j + 1, :] for j in range(6)]

    @pl.when((pl.program_id(0) == 0) & (pl.program_id(1) == 0) & (pl.program_id(2) == 0))
    def _():
        sum_ref[...] = jnp.zeros(sum_ref.shape, f32)
        sum_in_ref[...] = jnp.zeros(sum_in_ref.shape, f32)

    branch = dot_tn(attn_ref[...], weights.out()) + bias_out
    normed_a, scale_a = normalise(x_ref[...].astype(f32) + branch)
    hidden = normed_a * gain_a + shift_a
    low = hidden.astype(bf16)
    low_ref[...] = low
    cuts = [slice(c * width, (c + 1) * width) for c in range(inner // width)]
    last = len(cuts) - 1

    second = None
    held = None
    made = dot(low, weights.into(0))
    for c, cut in enumerate(cuts):
        pre = made + bi_ref[0:1, cut]
        if c < last:
            made = dot(low, weights.into(c + 1))
        value, slope = gelu_and_slope(pre)
        value = value.astype(bf16)
        act_ref[:, cut] = value
        slope_ref[:, cut] = slope.astype(bf16)
        if held is not None:
            term = dot(held, weights.ffo(c - 1))
            second = term if second is None else second + term
        held = value
    term = dot(held, weights.ffo(last))
    second = term if second is None else second + term

    normed_f, scale_f = normalise(hidden + (second + bias_ffo))
    out = (normed_f * gain_f + shift_f).astype(bf16)
    own = pl.program_id(1) == side_ref[0]

    @pl.when(own)
    def _():
        keep_ref[...] = out

    @pl.when(jnp.logical_not(own))
    def _():
        send_ref[...] = out

    cot = jnp.where(own, mine_ref[...], other_ref[...]).astype(f32)
    grad_r2 = normalise_back(cot * gain_f, normed_f, scale_f)
    grad_second = grad_r2.astype(bf16)
    gs_ref[...] = grad_second
    sum_ref[0:1, :] += column_sum(cot * normed_f)
    sum_ref[1:2, :] += column_sum(cot)
    sum_ref[2:3, :] += column_sum(grad_second.astype(f32))

    grad_hidden = grad_r2
    held = None
    made = dot_nt(grad_second, weights.ffo(0))
    for c, cut in enumerate(cuts):
        grad_act = made
        if c < last:
            made = dot_nt(grad_second, weights.ffo(c + 1))
        grad_pre = (grad_act * slope_ref[:, cut].astype(f32)).astype(bf16)
        gp_ref[:, cut] = grad_pre
        sum_in_ref[0:1, cut] += column_sum(grad_pre.astype(f32))
        if held is not None:
            grad_hidden = grad_hidden + dot_nt(held, weights.into(c - 1))
        held = grad_pre
    grad_hidden = grad_hidden + dot_nt(held, weights.into(last))

    grad_r1 = normalise_back(grad_hidden * gain_a, normed_a, scale_a)
    gr1_ref[...] = grad_r1
    grad_branch = grad_r1.astype(bf16)
    gb_ref[...] = grad_branch
    sum_ref[3:4, :] += column_sum(grad_hidden * normed_a)
    sum_ref[4:5, :] += column_sum(grad_hidden)
    sum_ref[5:6, :] += column_sum(grad_branch.astype(f32))
    grad_attn = dot_nt(grad_branch, weights.out()).astype(bf16)
    do_ref[...] = grad_attn
    doT_ref[...] = grad_attn.T


def held(shape, index):
    return pl.BlockSpec(shape, lambda *_: index, pipeline_mode=pl.Buffered(1))


def dense(side, attn, x, mine, other, weights, vectors, bias_in, block):
    rows, half, width = other.shape
    tokens = 2 * rows * half
    inner = bias_in.shape[1]
    block = min(block, half)
    blocks = half // block
    mine_at, other_at = halves(mine, other, block)

    def at(r, h, b, s):
        return ((r * 2 + h) * blocks + b, 0)

    narrow = pl.BlockSpec((block, width), at)
    wide = pl.BlockSpec((block, inner), at)

    return pl.pallas_call(
        dense_kernel,
        grid_spec=pltpu.PrefetchScalarGridSpec(
            num_scalar_prefetch=1,
            grid=(rows, 2, blocks),
            in_specs=[
                pl.BlockSpec((width, block), lambda *i: (0, at(*i)[0])),
                narrow,
                pl.BlockSpec((block, width), mine_at),
                pl.BlockSpec((block, width), other_at),
            ]
            + [held(shape, index) for _, shape, index in weights]
            + [held(vectors.shape, (0, 0)), held(bias_in.shape, (0, 0))],
            out_specs=[
                pl.BlockSpec((block, width), mine_at),
                pl.BlockSpec((block, width), other_at),
                wide, wide, narrow, narrow, narrow, narrow, narrow,
                pl.BlockSpec((width, block), lambda *i: (0, at(*i)[0])),
                pl.BlockSpec((8, width), lambda *_: (0, 0)),
                pl.BlockSpec((8, inner), lambda *_: (0, 0)),
            ],
            scratch_shapes=[pltpu.VMEM((block, inner), bf16)],
        ),
        out_shape=[
            shape_of((mine.shape[0] * half, width), bf16),
            shape_of((rows * half, width), bf16),
            shape_of((tokens, inner), bf16),
            shape_of((tokens, inner), bf16),
            shape_of((tokens, width), bf16),
            shape_of((tokens, width), bf16),
            shape_of((tokens, width), f32),
            shape_of((tokens, width), bf16),
            shape_of((tokens, width), bf16),
            shape_of((width, tokens), bf16),
            shape_of((8, width), f32),
            shape_of((8, inner), f32),
        ],
        compiler_params=pltpu.CompilerParams(vmem_limit_bytes=VMEM_LIMIT),
        cost_estimate=cost(
            flops=2 * tokens * width * (2 * width + 4 * inner),
            bytes_accessed=tokens * (22 * width + 4 * inner) + 4 * width * inner,
            transcendentals=2 * tokens * inner,
        ),
        name="dense",
    )(
        side, attn, x, mine.reshape(-1, width), other.reshape(-1, width),
        *[array for array, _, _ in weights], vectors, bias_in,
    )


def product_kernel(*refs, more, split):
    place_ref, a_ref, b_ref = refs[:3]
    steps = pl.num_programs(0)

    def write(x_ref, y_ref, times=dot_tn):
        made = times(x_ref[...], y_ref[...]).astype(bf16)
        if not split:
            refs[-1][...] = made.reshape(refs[-1].shape)
            return
        keep_ref, send_ref, held_ref = refs[-3:]
        held_ref[...] = made.reshape(held_ref.shape)
        core = lax.rem(place_ref[1], 2)
        keep_ref[...] = held_ref[:, core]
        send_ref[...] = held_ref[:, 1 - core]

    if more:
        pl.when(pl.program_id(0) < steps - 1)(lambda: write(a_ref, b_ref))
        pl.when(pl.program_id(0) == steps - 1)(lambda: write(*refs[3:5], dot))
    else:
        write(a_ref, b_ref)


def product(place, shape, a, b, out_block, out_at, a_moves, steps, more=(), split=False):
    tokens = a.shape[0]
    a_cols = a.shape[1] // (steps if a_moves else 1)
    b_cols = b.shape[1] // (1 if a_moves else steps)
    moving = {"index_map": lambda i, s: (0, jnp.minimum(i, steps - 1))}
    still = {"index_map": lambda i, s: (0, 0), "pipeline_mode": pl.Buffered(1)}
    in_specs = [
        pl.BlockSpec((tokens, a_cols), **(moving if a_moves else still)),
        pl.BlockSpec((tokens, b_cols), **(still if a_moves else moving)),
    ]
    in_specs += [pl.BlockSpec(v.shape, **still) for v in more]
    halved = [n // 2 if split else n for n in (shape[0], out_block[0])]
    out_specs = pl.BlockSpec((halved[1],) + out_block[1:], lambda i, s: out_at(i))
    out_shape = shape_of((halved[0],) + shape[1:], bf16)
    return pl.pallas_call(
        functools.partial(product_kernel, more=bool(more), split=split),
        grid_spec=pltpu.PrefetchScalarGridSpec(
            num_scalar_prefetch=1,
            grid=(steps + bool(more),),
            in_specs=in_specs,
            out_specs=[out_specs] * 2 if split else out_specs,
            scratch_shapes=(
                [pltpu.VMEM((out_block[0] // 2, 2) + out_block[1:], bf16)] if split else []
            ),
        ),
        out_shape=[out_shape] * 2 if split else out_shape,
        compiler_params=pltpu.CompilerParams(vmem_limit_bytes=VMEM_LIMIT),
        cost_estimate=cost(
            flops=2 * tokens * a.shape[1] * b.shape[1],
            bytes_accessed=2 * (a.size + b.size + a.shape[1] * b.shape[1]),
            transcendentals=0,
        ),
        name="product",
    )(place, a, b, *more)


def input_grad_kernel(side_ref, g_ref, gr1_ref, w_ref, keep_ref, send_ref):
    width = send_ref.shape[1]
    total = gr1_ref[...] + dot_nt(g_ref[...], w_ref[:, : 3 * width])
    low = total.astype(bf16)
    own = pl.program_id(1) == side_ref[0]

    @pl.when(own)
    def _():
        keep_ref[...] = low

    @pl.when(jnp.logical_not(own))
    def _():
        send_ref[...] = low


def input_grad(side, grad_qkv, grad_r1, weight, mine, other, block):
    rows, half, width = other.shape
    block = min(block, half)
    blocks = half // block
    mine_at, other_at = halves(mine, other, block)

    def at(r, h, b, s):
        return ((r * 2 + h) * blocks + b, 0)

    keep, send = pl.pallas_call(
        input_grad_kernel,
        grid_spec=pltpu.PrefetchScalarGridSpec(
            num_scalar_prefetch=1,
            grid=(rows, 2, blocks),
            in_specs=[
                pl.BlockSpec((block, grad_qkv.shape[1]), at),
                pl.BlockSpec((block, width), at),
                pl.BlockSpec(weight.shape, lambda *_: (0, 0), pipeline_mode=pl.Buffered(1)),
            ],
            out_specs=[
                pl.BlockSpec((block, width), mine_at),
                pl.BlockSpec((block, width), other_at),
            ],
        ),
        out_shape=[shape_of((v.shape[0] * half, width), bf16) for v in (mine, other)],
        compiler_params=pltpu.CompilerParams(vmem_limit_bytes=VMEM_LIMIT),
        cost_estimate=cost(
            flops=12 * rows * half * width * width,
            bytes_accessed=24 * rows * half * width + 6 * width * width,
            transcendentals=0,
        ),
        name="input_grad",
    )(side, grad_qkv, grad_r1, weight)
    return keep.reshape(mine.shape), send.reshape(other.shape)


def vector_block(sums_ref, sums_in_ref, sums_qv_ref, shards):
    qv = jnp.concatenate([sums_qv_ref[j : j + 1, :] for j in range(2)], axis=1)
    rows = [sums_ref[j : j + 1, :] for j in range(6)]
    found = []
    for v in (qv, rows[5], rows[3], rows[4], sums_in_ref[0:1, :], rows[2], rows[0], rows[1]):
        found.extend(gather_vector(v, shards))
    return [v.astype(bf16) for v in found]


def last_product_kernel(place_ref, a_ref, b_ref, *refs, shards):
    keep_ref, send_ref, held_ref = refs[-3:]
    at = pl.program_id(0)
    width = a_ref.shape[1]
    shard = width // shards
    core = lax.rem(place_ref[1], 2)
    made = dot_tn(a_ref[...], b_ref[...]).astype(bf16)
    held_ref[...] = made.reshape(held_ref.shape)
    rows = pl.ds(pl.multiple_of(at * shard, 16), shard)
    keep_ref[:, rows, :] = held_ref[:, core]
    send_ref[:, rows, :] = held_ref[:, 1 - core]

    @pl.when(at == pl.num_programs(0) - 1)
    def _():
        held_ref[:, :, :16, :] = jnp.zeros(held_ref[:, :, :16, :].shape, bf16)
        for j, v in enumerate(vector_block(*refs[:3], shards)):
            held_ref[:, :, j : j + 1, :LANES] = v.reshape(shards // 2, 2, 1, LANES)
        end = slice(keep_ref.shape[1] - 16, keep_ref.shape[1])
        keep_ref[:, end, :] = held_ref[:, core, :16]
        send_ref[:, end, :] = held_ref[:, 1 - core, :16]


def last_product(place, a, b, sums, shards):
    tokens, width = a.shape
    steps = b.shape[1] // width
    shard = width // shards
    out = (shards // 2, steps * shard + 16, width)
    return pl.pallas_call(
        functools.partial(last_product_kernel, shards=shards),
        grid_spec=pltpu.PrefetchScalarGridSpec(
            num_scalar_prefetch=1,
            grid=(steps,),
            in_specs=[
                pl.BlockSpec((tokens, width), lambda i, s: (0, 0), pipeline_mode=pl.Buffered(1)),
                pl.BlockSpec((tokens, width), lambda i, s: (0, i)),
            ]
            + [pl.BlockSpec(v.shape, lambda i, s: (0, 0)) for v in sums],
            out_specs=[pl.BlockSpec(out, lambda i, s: (0, 0, 0))] * 2,
            scratch_shapes=[pltpu.VMEM((shards // 2, 2, shard, width), bf16)],
        ),
        out_shape=[shape_of(out, bf16)] * 2,
        compiler_params=pltpu.CompilerParams(vmem_limit_bytes=VMEM_LIMIT),
        cost_estimate=cost(
            flops=2 * tokens * width * b.shape[1],
            bytes_accessed=2 * (a.size + b.size + width * b.shape[1]),
            transcendentals=0,
        ),
        name="last_product",
    )(place, a, b, *sums)


def split_heads(values):
    return values.reshape(values.shape[0], values.shape[1], H, HD)


def gathered_probs(queries, keys, allowed):
    scores = jnp.einsum("rqhd,rkhd->rhqk", queries, keys, preferred_element_type=f32)
    return jax.nn.softmax(jnp.where(allowed, scores * SCORE_SCALE, MASKED), axis=-1)


def attend_gathered(bounds, qkv, rows, seq_index):
    width = qkv.shape[1] // 3
    parts = qkv.reshape(rows, -1, 3 * width)
    tok_seq = parts.shape[1]
    whole = lax.all_gather(parts[:, :, width:], "seq", axis=1, tiled=True)
    row_len = whole.shape[1]
    queries = split_heads(parts[:, :, :width])
    keys = split_heads(whole[:, :, :width])
    values = split_heads(whole[:, :, width:])
    positions = jnp.arange(row_len, dtype=jnp.int32)
    segments = jnp.sum((positions[None, :, None] >= bounds[:, None, :]).astype(jnp.int32), axis=2)
    mine = lax.dynamic_slice_in_dim(segments, seq_index * tok_seq, tok_seq, 1)
    allowed = mine[:, None, :, None] == segments[:, None, None, :]
    probs = gathered_probs(queries, keys, allowed)
    attended = jnp.einsum(
        "rhqk,rkhd->rqhd", probs.astype(bf16), values, preferred_element_type=f32
    )
    return attended.astype(bf16).reshape(-1, width), (queries, keys, values, allowed)


def attend_gathered_back(saved, attn, do):
    queries, keys, values, allowed = saved
    rows, tok_seq = queries.shape[:2]
    width = attn.shape[1]
    probs = gathered_probs(queries, keys, allowed)
    do = do.reshape(rows, tok_seq, H, HD)
    delta = jnp.sum(do.astype(f32) * attn.reshape(do.shape).astype(f32), axis=-1)
    grad_prob = jnp.einsum("rqhd,rkhd->rhqk", do, values, preferred_element_type=f32)
    grad_score = (probs * (grad_prob - delta.transpose(0, 2, 1)[..., None])).astype(bf16)
    dq = jnp.einsum("rhqk,rkhd->rqhd", grad_score, keys, preferred_element_type=f32) * SCORE_SCALE
    dk = (
        jnp.einsum("rhqk,rqhd->rkhd", grad_score, queries, preferred_element_type=f32)
        * SCORE_SCALE
    )
    dv = jnp.einsum("rhqk,rqhd->rkhd", probs.astype(bf16), do, preferred_element_type=f32)
    pair = jnp.concatenate([dk.reshape(rows, -1, width), dv.reshape(rows, -1, width)], axis=-1)
    pair = lax.psum_scatter(pair.astype(bf16), "seq", scatter_dimension=1, tiled=True)
    pair = pair.reshape(-1, 2 * width)
    dq = dq.astype(bf16).reshape(-1, width)
    dk, dv = pair[:, :width], pair[:, width:]
    sums = jnp.stack([jnp.sum(dq.astype(f32), axis=0), jnp.sum(dv.astype(f32), axis=0)])
    return jnp.concatenate([dq, dk, dv], axis=1), jnp.pad(sums, ((0, 6), (0, 0)))


def swapped(values):
    return lax.ppermute(values, "seq", [(0, 1), (1, 0)])


def other_half(values, seq_index):
    rows = values.shape[0] // 2
    return swapped(lax.dynamic_slice_in_dim(values, (1 - seq_index) * rows, rows, 0))


def placed(values, came, seq_index, row=0):
    at = (1 - seq_index) * (values.shape[0] // 2) + row
    return lax.dynamic_update_slice_in_dim(values, came, at, 0)


def coordinates(count):
    return ((2, 1), (count // 8, 2), (4, count // 4))


def turned(values, axis, size, stride, step):
    perm = []
    for i in range(lax.axis_size(axis)):
        at = (i // stride) % size
        perm.append((i, i + ((at + step) % size - at) * stride))
    return lax.ppermute(values, axis, perm)


class StagedSum:
    def __init__(self, keep, send, axis):
        self.axis = axis
        self.sizes = coordinates(lax.axis_size(axis))
        self.index = lax.axis_index(axis)
        self.own = keep
        size, stride = self.sizes[0]
        self.came = [turned(send, axis, size, stride, 1)]

    def sum(self, pick):
        total = pick(self.own).astype(f32)
        for values in self.came:
            total = total + pick(values).astype(f32)
        return total.astype(bf16)

    def step(self, at):
        size, stride = self.sizes[at]
        here = (self.index // stride) % size

        def part(step):
            def pick(values):
                blocks = values.reshape((-1, size) + values.shape[1:])
                return lax.dynamic_index_in_dim(blocks, (here + step) % size, 1, False)

            return self.sum(pick)

        came = [
            turned(part(step), self.axis, size, stride, step) for step in range(1, size)
        ]
        self.own, self.came = part(0), came

    def result(self):
        return self.sum(lambda values: values[0])


def tied(*values):
    return lax.optimization_barrier(values)


def gather_pieces(values, axis):
    pieces = [(values, (0, 0, 0))]
    for at, (size, stride) in reversed(list(enumerate(coordinates(lax.axis_size(axis))))):
        more = []
        for piece, back in pieces:
            for step in range(1, size):
                came = turned(piece, axis, size, stride, step)
                more.append((came, back[:at] + (step,) + back[at + 1 :]))
        pieces = pieces + more
    return pieces


def piece_owner(index, back, count):
    owner = jnp.int32(0)
    for (size, stride), step in zip(coordinates(count), back):
        owner = owner + lax.rem(lax.rem(index // stride, size) + (size - step), size) * stride
    return owner


def per_device(
    tokens,
    weight_qkv,
    bias_qv,
    weight_out,
    bias_out,
    gain_attn,
    shift_attn,
    weight_in,
    bias_in,
    weight_ffo,
    bias_ffo,
    gain_ffn,
    shift_ffn,
    lengths,
    cotangent,
):
    rows, tok_seq, width = tokens.shape
    seq_count = lax.axis_size("seq")
    seq_index = lax.axis_index("seq")
    shards = lax.axis_size("dp")
    shard = weight_qkv.shape[0]
    by_rows = seq_count == 2 and rows % 2 == 0 and shards % 8 == 0 and shard % 16 == 0
    inner = weight_in.shape[1]
    chunks = inner // width
    token_count = rows * tok_seq

    small = (bias_qv, bias_out, gain_attn, shift_attn, bias_in, bias_ffo, gain_ffn, shift_ffn)
    first, others = lower(weight_qkv, weight_in, weight_ffo, weight_out, small)
    if by_rows:
        first = gather_pieces(first, "dp")
        backs = [back for _, back in first]
    else:
        first = [(lax.all_gather(first, "dp", axis=0, tiled=True), None)]
    others = lax.all_gather(others[None], "dp", axis=0, tiled=True)
    if shard % 16 == 0:
        weights = (
            (others, (shards, shard, width), (0, 2 * chunks, 0)),
            (others, (shards, chunks * shard, width), (0, 0, 0)),
            (others, (shards, chunks * shard, width), (0, 1, 0)),
        )
    else:
        part = chunks * shard
        w_in = others[:, :part].reshape(shards, chunks, shard, width).transpose(1, 0, 2, 3)
        w_in = w_in.reshape(1, inner, width)
        w_ffo = others[:, part : 2 * part].reshape(1, inner, width)
        w_out = others[:, 2 * part :].reshape(1, width, width)
        weights = [(w, w.shape, (0, 0, 0)) for w in (w_out, w_in, w_ffo)]

    bounds = jnp.cumsum(lengths, axis=1)
    if by_rows:
        mine = rows // 2
        bounds = lax.dynamic_slice_in_dim(bounds, seq_index * mine, mine, 0)
        side = jnp.stack([seq_index, lax.axis_index("dp")]).astype(jnp.int32)
        x_other = other_half(tokens, seq_index)
        first, x_other, held_cot = tied([w for w, _ in first], x_other, cotangent)
        x_halves = tokens, x_other
        first = list(zip(first, backs))
        cot_halves = cotangent, other_half(held_cot, seq_index)
    else:
        mine = 1
        side = jnp.zeros((2,), jnp.int32)
        x_halves = tokens.reshape(2, 1, -1, width)
        cot_halves = cotangent.reshape(2, 1, -1, width)
    half = x_halves[1].shape[1]

    x, qkv, qkvT, w_qkv, vec, in_bias = project(side, *x_halves, first, inner, BLOCK)
    if by_rows:
        attnT, log = attend_rows(bounds, qkv, qkvT, BLOCK)
    else:
        attn, saved = attend_gathered(bounds, qkv, rows, seq_index)
        attnT = attn.T
    out, out_other, act, gp, gs, low, gr1, gb, do, doT, sums, sums_in = dense(
        side, attnT, x, *cot_halves, weights, vec, in_bias, BLOCK
    )
    out = out.reshape(-1, half, width)
    out_other = out_other.reshape(-1, half, width)
    part = chunks * shard
    if by_rows:
        core_split = functools.partial(product, side, split=True)
        out_other = swapped(out_other)
        g_in = core_split(
            (shards, part + shard, width), low, gp, (shards, shard, width), lambda i: (0, i, 0),
            False, chunks, (attnT, gb),
        )
        *g_in, act = tied(*g_in, act)
        in_sum = StagedSum(*g_in, "dp")
        g_ffo = product(
            side, (shards, part, width), act, gs, (shards // chunks, part, width),
            lambda i: (i, 0, 0), True, chunks,
        )
    else:
        out = jnp.concatenate([out, out_other], axis=1).reshape(rows, tok_seq, width)
        g_ffo = dot_tn(act, gs).astype(bf16).reshape(shards, part, width)
        g_in = dot_tn(low, gp).astype(bf16).reshape(shards, shard, chunks, width)
        g_in = g_in.transpose(0, 2, 1, 3).reshape(shards, part, width)
        g_out = dot_tn(attn, gb).astype(bf16).reshape(shards, shard, width)
        g_in = jnp.concatenate([g_in, g_out], axis=1)
        g_in = lax.psum_scatter(g_in, "dp", scatter_dimension=0, tiled=True)[0]
    if by_rows:
        g_ffo, do, in_sum.came = tied(g_ffo, do, in_sum.came)
    g_ffo = lax.psum_scatter(g_ffo, "dp", scatter_dimension=0, tiled=True)[0]

    if by_rows:
        in_sum.step(1)
        g_x, sums_qv = attend_rows_back(bounds, qkv, qkvT, do, doT, attnT, log, 0, 1, BLOCK)
        g_x, out_other, in_sum.came = tied(g_x, out_other, in_sum.came)
        in_sum.step(2)
        g_qkv = last_product(side, x, g_x, (sums, sums_in, sums_qv), shards)
        g_qkv, gr1 = tied(g_qkv, gr1)
        grad_x, grad_other = input_grad(side, g_x, gr1, w_qkv, *x_halves, BLOCK)
        grad_other, g_qkv, in_sum.came = tied(grad_other, g_qkv, in_sum.came)
        qkv_sum = StagedSum(*g_qkv, "dp")
        qkv_sum.step(1)
        grad_other = [swapped(grad_other[r : r + 1]) for r in range(mine)]
        qkv_sum.came, grad_other[0] = tied(qkv_sum.came, grad_other[0])
        qkv_sum.step(2)
        g_in = in_sum.result()
        both = swapped(jnp.concatenate([g_in, g_ffo], axis=0))
        qkv_sum.came, both, grad_other = tied(qkv_sum.came, both, grad_other)
        g_qkv = qkv_sum.result()
        for r in range(mine):
            grad_x = placed(grad_x, grad_other[r], seq_index, r)
        out = placed(out, out_other, seq_index)
        g_in = g_in.astype(f32) + both[: part + shard].astype(f32)
        d_ffo = g_ffo.astype(f32) + both[part + shard :].astype(f32)
        g_qkv = g_qkv.astype(f32) + swapped(g_qkv).astype(f32)
    else:
        g_x, sums_qv = attend_gathered_back(saved, attn, do)
        vectors = []
        for v in (sums_qv[:2].reshape(-1), sums[5], sums[3], sums[4], sums_in[0], sums[2], sums[0], sums[1]):
            v = v.reshape(shards, -1)
            vectors.append(jnp.pad(v, ((0, 0), (0, -v.shape[1] % LANES))).reshape(shards, -1, LANES))
        vectors = jnp.concatenate(vectors, axis=1).astype(bf16)
        vectors = jnp.pad(vectors, ((0, 0), (0, 16 - vectors.shape[1]), (0, width - LANES)))
        g_qkv = dot_tn(x, g_x).astype(bf16).reshape(shards, shard, 3, width)
        g_qkv = g_qkv.transpose(0, 2, 1, 3).reshape(shards, 3 * shard, width)
        g_qkv = jnp.concatenate([g_qkv, vectors], axis=1)
        g_qkv = lax.psum_scatter(g_qkv, "dp", scatter_dimension=0, tiled=True)[0]
        grad_x, grad_other = input_grad(side, g_x, gr1, w_qkv, *x_halves, BLOCK)
        grad_x = jnp.concatenate([grad_x, grad_other], axis=1).reshape(rows, tok_seq, width)
        d_ffo, g_in, g_qkv = [lax.psum(v, "seq").astype(f32) for v in (g_ffo, g_in, g_qkv)]
    vectors = g_qkv[3 * shard :, :LANES]
    d_qkv = jnp.concatenate([g_qkv[j * shard : (j + 1) * shard] for j in range(3)], axis=1)
    d_out = g_in[part:]
    d_in = jnp.concatenate([g_in[c * shard : (c + 1) * shard] for c in range(chunks)], axis=1)
    sizes = [v.shape[0] for v in small]
    d_small = []
    for row, size in zip(vector_rows(sizes)[0], sizes):
        d_small.append(vectors[row : row - (-size // LANES)].reshape(-1)[:size])
    g_qv, g_bo, g_ga, g_sa, g_bi, g_bf, g_gf, g_sf = d_small
    return (
        out, grad_x, d_qkv, g_qv, d_out, g_bo, g_ga, g_sa, d_in, g_bi, d_ffo,
        g_bf, g_gf, g_sf,
    )


def solution(mesh):
    by_token = P("dp", "seq", None)
    weight = P("dp", None)
    vector = P("dp")
    params = (
        weight, vector, weight, vector, vector, vector, weight, vector, weight, vector, vector,
        vector,
    )
    return jax.shard_map(
        per_device,
        mesh=mesh,
        in_specs=(by_token,) + params + (weight, by_token),
        out_specs=(by_token, by_token) + params,
        check_vma=False,
    )
```

```python
import functools
import math

import jax
import jax.numpy as jnp
from jax import lax
from jax.experimental import pallas as pl
from jax.experimental.pallas import tpu as pltpu
from jax.sharding import PartitionSpec as P

H = 12
HD = 64
PAIR = 2 * HD
LANES = 128
f32 = jnp.float32
bf16 = jnp.bfloat16
SCORE_SCALE = 1.0 / math.sqrt(HD)
EXP2_SCALE = SCORE_SCALE * math.log2(math.e)
MASKED = -1e30
VMEM_LIMIT = 60 << 20
BLOCK = 256
COST = 4
GROUP = H
GROUP_ROWS = -(-GROUP // 8) * 8
WINDOWS = (2, 3, 4, 5, 6)


def dot(a, b):
    return jnp.dot(a, b, preferred_element_type=f32)


def dot_nt(a, b):
    return lax.dot_general(a, b, (((1,), (1,)), ((), ())), preferred_element_type=f32)


def dot_tn(a, b):
    return lax.dot_general(a, b, (((0,), (0,)), ((), ())), preferred_element_type=f32)


def column_sum(values):
    return jnp.sum(values, axis=0, keepdims=True)


def cost(flops, bytes_accessed, transcendentals=0):
    return pl.CostEstimate(
        flops=flops // COST, bytes_accessed=bytes_accessed // COST, transcendentals=transcendentals // COST
    )


def shape_of(shape, dtype):
    return jax.ShapeDtypeStruct(shape, dtype)


def vector_rows(sizes):
    rows = []
    at = 0
    for size in sizes:
        rows.append(at)
        at += -(-size // LANES)
    return rows, at


def lower_kernel(*refs):
    w_qkv, w_in, w_ffo, w_out = refs[:4]
    small = refs[4:-3]
    first_ref, others_ref, block_ref = refs[-3:]
    columns = w_qkv.shape[1]
    shard, width = w_out.shape
    first_ref[:, :columns] = w_qkv[...].astype(bf16)
    block_ref[...] = jnp.zeros(block_ref.shape, f32)
    for ref, row in zip(small, vector_rows([r.shape[1] for r in small])[0]):
        size = ref.shape[1]
        for at in range(0, size, LANES):
            n = min(LANES, size - at)
            block_ref[row : row + 1, :n] = ref[:, at : at + n]
            row += 1
    first_ref[:, columns:] = block_ref[...].astype(bf16)
    chunks = w_in.shape[1] // width
    for c in range(chunks):
        others_ref[c * shard : (c + 1) * shard, :] = w_in[:, c * width : (c + 1) * width].astype(bf16)
    others_ref[chunks * shard : 2 * chunks * shard, :] = w_ffo[...].astype(bf16)
    others_ref[2 * chunks * shard :, :] = w_out[...].astype(bf16)


def lower(w_qkv, w_in, w_ffo, w_out, small):
    shard, columns = w_qkv.shape
    width = w_out.shape[1]
    chunks = w_in.shape[1] // width
    return pl.pallas_call(
        lower_kernel,
        out_shape=[
            shape_of((shard, columns + LANES), bf16),
            shape_of(((2 * chunks + 1) * shard, width), bf16),
        ],
        scratch_shapes=[pltpu.VMEM((shard, LANES), f32)],
        compiler_params=pltpu.CompilerParams(vmem_limit_bytes=VMEM_LIMIT),
        name="lower",
    )(w_qkv, w_in, w_ffo, w_out, *[v.reshape(1, -1) for v in small])


def places(total, size):
    at = lax.broadcasted_iota(jnp.int32, (1, total), 1)
    return at % size, at // size


def picker(place, at):
    lane = lax.broadcasted_iota(jnp.int32, (LANES, place.shape[1]), 0)
    return jnp.where(place == lane + at, 1.0, 0.0).astype(bf16)


def spread_vector(block, row, size, shards):
    place, owner = places(size * shards, size)
    found = jnp.zeros((shards, size * shards), f32)
    for at in range(0, size, LANES):
        found = found + dot(block[:, row + at // LANES, :].astype(bf16), picker(place, at))
    index = lax.broadcasted_iota(jnp.int32, found.shape, 0)
    return column_sum(jnp.where(owner == index, found, 0.0))


def gather_vector(vector, shards):
    total = vector.shape[1]
    size = total // shards
    place, owner = places(total, size)
    index = lax.broadcasted_iota(jnp.int32, (shards, total), 0)
    own = jnp.where(owner == index, vector, 0.0).astype(bf16)
    return [dot_nt(own, picker(place, at)) for at in range(0, size, LANES)]


def project_kernel(place_ref, mine_ref, other_ref, *refs, shards, pieces):
    x_ref, out_ref, outT_ref, w_ref, vec_ref, bi_ref, bias_ref, sems = refs[len(pieces) :]
    width = x_ref.shape[1]
    columns = out_ref.shape[1]
    shard = width // shards

    @pl.when((pl.program_id(0) == 0) & (pl.program_id(1) == 0) & (pl.program_id(2) == 0))
    def _():
        copies = []
        for j, (ref, back) in enumerate(zip(refs, pieces)):
            start = jnp.int32(0) if back is None else piece_owner(place_ref[1], back, shards) * shard
            rows = pl.ds(pl.multiple_of(start, 16), ref.shape[0])
            copies.append(pltpu.make_async_copy(ref, w_ref.at[rows, :], sems.at[j]))
        for copy in copies:
            copy.start()
        for copy in copies:
            copy.wait()
        block = w_ref[:, columns:].astype(f32).reshape(shards, shard, LANES)
        inner = bi_ref.shape[1]
        totals = (2 * width, width, width, width, inner, width, width, width)
        sizes = [total // shards for total in totals]
        found = [
            spread_vector(block, row, size, shards)
            for row, size in zip(vector_rows(sizes)[0], sizes)
        ]
        bias_ref[0:1, :width] = found[0][:, :width]
        bias_ref[0:1, width : 2 * width] = jnp.zeros((1, width), f32)
        bias_ref[0:1, 2 * width :] = found[0][:, width:]
        bi_ref[0:1, :] = found[4]
        for j, v in enumerate(found[1:4] + found[5:]):
            vec_ref[j : j + 1, :] = v

    x = jnp.where(pl.program_id(1) == place_ref[0], mine_ref[...], other_ref[...])
    x_ref[...] = x
    low = (dot(x, w_ref[:, :columns]) + bias_ref[0:1, :]).astype(bf16)
    out_ref[...] = low
    outT_ref[...] = low.T


def halves(mine, other, block):
    rows, half, _ = other.shape
    blocks = half // block
    skip = rows if mine.shape[0] > rows else 0

    def at(used, r, h, b):
        rest = jnp.where(h == 0, 0, blocks - 1)
        return (r * blocks + jnp.where(used, b, rest), 0)

    return (
        lambda r, h, b, s: at(h == s[0], r + s[0] * skip, h, b),
        lambda r, h, b, s: at(h != s[0], r, h, b),
    )


def project(place, mine, other, weight, inner, block):
    rows, half, width = other.shape
    block = min(block, half)
    blocks = half // block
    columns = 3 * width
    tokens = 2 * rows * half
    shards = lax.axis_size("dp")
    mine_at, other_at = halves(mine, other, block)

    def at(r, h, b, s):
        return ((r * 2 + h) * blocks + b, 0)

    return pl.pallas_call(
        functools.partial(project_kernel, shards=shards, pieces=[back for _, back in weight]),
        grid_spec=pltpu.PrefetchScalarGridSpec(
            num_scalar_prefetch=1,
            grid=(rows, 2, blocks),
            in_specs=[
                pl.BlockSpec((block, width), mine_at),
                pl.BlockSpec((block, width), other_at),
            ]
            + [pl.BlockSpec(memory_space=pl.ANY)] * len(weight),
            out_specs=[
                pl.BlockSpec((block, width), at),
                pl.BlockSpec((block, columns), at),
                pl.BlockSpec((columns, block), lambda *i: (0, at(*i)[0])),
                pl.BlockSpec((width, columns + LANES), lambda *_: (0, 0)),
                pl.BlockSpec((8, width), lambda *_: (0, 0)),
                pl.BlockSpec((8, inner), lambda *_: (0, 0)),
            ],
            scratch_shapes=[
                pltpu.VMEM((8, columns), f32),
                pltpu.SemaphoreType.DMA((len(weight),)),
            ],
        ),
        out_shape=[
            shape_of((tokens, width), bf16),
            shape_of((tokens, columns), bf16),
            shape_of((columns, tokens), bf16),
            shape_of((width, columns + LANES), bf16),
            shape_of((8, width), f32),
            shape_of((8, inner), f32),
        ],
        compiler_params=pltpu.CompilerParams(vmem_limit_bytes=VMEM_LIMIT),
        cost_estimate=cost(
            flops=2 * tokens * width * columns,
            bytes_accessed=2 * (2 * tokens * width + 2 * width * columns + 2 * tokens * columns),
            transcendentals=0,
        ),
        name="project",
    )(place, mine.reshape(-1, width), other.reshape(-1, width), *[w for w, _ in weight])


def passage_range(bounds_ref, row, start, size, row_len):
    first = jnp.int32(0)
    last = jnp.int32(row_len)
    for j in range(bounds_ref.shape[1]):
        bound = bounds_ref[row, j]
        first = jnp.where(bound <= start, jnp.maximum(first, bound), first)
        last = jnp.where(bound >= start + size, jnp.minimum(last, bound), last)
    return first, last


def segments_at(bounds_ref, row, positions):
    count = jnp.zeros(positions.shape, jnp.int32)
    for j in range(bounds_ref.shape[1]):
        count = count + (positions >= bounds_ref[row, j]).astype(jnp.int32)
    return count


def with_window(first, last, row_len, body):
    first_tile = first // LANES
    needed = (last + LANES - 1) // LANES - first_tile
    below = 0
    for tiles in WINDOWS:

        @pl.when((needed > below) & (needed <= tiles))
        def _(tiles=tiles):
            start = jnp.minimum(first_tile, row_len // LANES - tiles)
            body(pl.multiple_of(start * LANES, LANES), tiles * LANES)

        below = tiles


def mask_bias(bounds_ref, row, sub_start, sub_len, lane_start, lane_len):
    down = segments_at(
        bounds_ref, row, sub_start + lax.broadcasted_iota(jnp.int32, (sub_len, LANES), 0)
    )
    across = segments_at(
        bounds_ref, row, lane_start + lax.broadcasted_iota(jnp.int32, (1, lane_len), 1)
    )
    down = jnp.concatenate([down] * (lane_len // LANES), axis=1)
    return jnp.where(down == across, 0.0, MASKED).astype(f32)


def head_rows(h):
    return slice(HD * h, HD * h + HD)


def pair_lanes(h):
    return slice(PAIR * (h // 2), PAIR * (h // 2) + PAIR)


def log_row(h):
    return GROUP_ROWS * (h // GROUP) + h % GROUP


def in_pair(h, rows):
    zero = jnp.zeros_like(rows)
    return jnp.concatenate([rows, zero] if h % 2 == 0 else [zero, rows], axis=0)


def attend_kernel(bounds_ref, k_ref, qT_ref, vT_ref, outT_ref, log_ref, bias_ref):
    row = pl.program_id(0)
    row_len, width = k_ref.shape
    block = qT_ref.shape[1]
    heads = width // HD
    q_start = pl.program_id(1) * block
    first, last = passage_range(bounds_ref, row, q_start, block, row_len)

    def body(start, window):
        keys = pl.ds(start, window)
        bias_ref[:window, :] = mask_bias(bounds_ref, row, start, window, q_start, block)

        def score(h):
            return dot(k_ref[keys, pair_lanes(h)], in_pair(h, qT_ref[head_rows(h), :]))

        def weigh(scores):
            masked = scores + bias_ref[:window, :]
            best = jnp.max(masked, axis=0, keepdims=True)
            return best, jnp.exp2((masked - best) * EXP2_SCALE).astype(bf16)

        def attend(h, best, weights):
            values = jnp.concatenate(
                [vT_ref[head_rows(h), keys], jnp.ones((16, window), bf16)], axis=0
            )
            summed = dot(values, weights)
            total = summed[HD : HD + 1]
            outT_ref[head_rows(h), :] = (summed[:HD] * (1.0 / total)).astype(bf16)
            at = log_row(h)
            log_ref[at : at + 1, :] = best * EXP2_SCALE + jnp.log2(total)

        scores = [score(0), score(1)]
        held = None
        for h in range(0, heads, 2):
            now = scores
            if h + 2 < heads:
                scores = [score(h + 2), score(h + 3)]
            weighed = [weigh(s) for s in now]
            if held is not None:
                attend(h - 2, *held[0])
                attend(h - 1, *held[1])
            held = weighed
        attend(heads - 2, *held[0])
        attend(heads - 1, *held[1])

    with_window(first, last, row_len, body)


def attend_rows(bounds, qkv, qkvT, block):
    rows = bounds.shape[0]
    tokens = qkv.shape[0]
    width = qkv.shape[1] // 3
    row_len = tokens // rows
    blocks = row_len // block
    return pl.pallas_call(
        attend_kernel,
        grid_spec=pltpu.PrefetchScalarGridSpec(
            num_scalar_prefetch=1,
            grid=(rows, blocks),
            in_specs=[
                pl.BlockSpec((row_len, width), lambda r, b, s: (r, 1)),
                pl.BlockSpec((width, block), lambda r, b, s: (0, r * blocks + b)),
                pl.BlockSpec((width, row_len), lambda r, b, s: (2, r)),
            ],
            out_specs=[
                pl.BlockSpec((width, block), lambda r, b, s: (0, r * blocks + b)),
                pl.BlockSpec((H // GROUP * GROUP_ROWS, block), lambda r, b, s: (0, r * blocks + b)),
            ],
            scratch_shapes=[pltpu.VMEM((max(WINDOWS) * LANES, block), f32)],
        ),
        out_shape=[
            shape_of((width, tokens), bf16),
            shape_of((H // GROUP * GROUP_ROWS, tokens), f32),
        ],
        compiler_params=pltpu.CompilerParams(vmem_limit_bytes=VMEM_LIMIT),
        cost_estimate=cost(
            flops=16 * tokens * row_len * width // 4,
            bytes_accessed=10 * tokens * width,
            transcendentals=0,
        ),
        name="attend",
    )(bounds, qkv, qkvT, qkvT)


def attend_back_kernel(
    bounds_ref, k_ref, kT_ref, v_ref, q_ref, qT_ref, do_ref, doT_ref, outT_ref, log_ref,
    grad_ref, sum_ref, bias_ref, dqT_ref, delta_ref,
):
    row = pl.program_id(1)
    at = pl.program_id(2)
    row_len, width = q_ref.shape
    block = k_ref.shape[0]
    heads = width // HD
    k_start = at * block
    keys = pl.ds(pl.multiple_of(k_start, block), block)

    @pl.when((row == 0) & (at == 0))
    def _():
        sum_ref[...] = jnp.zeros(sum_ref.shape, f32)

    @pl.when(at == 0)
    def _():
        dqT_ref[...] = jnp.zeros(dqT_ref.shape, f32)
        for h in range(heads):
            both = doT_ref[head_rows(h), :].astype(f32) * outT_ref[head_rows(h), :].astype(f32)
            delta_ref[h : h + 1, :] = column_sum(both)

    first, last = passage_range(bounds_ref, row, k_start, block, row_len)
    low_half = lax.broadcasted_iota(jnp.int32, (block, PAIR), 1) < HD

    def body(start, window):
        queries = pl.ds(start, window)
        bias_ref[:, :window] = mask_bias(bounds_ref, row, k_start, block, start, window)
        even = {}

        def products(h):
            lanes = pair_lanes(h)
            scores = dot(k_ref[:, lanes], in_pair(h, qT_ref[head_rows(h), queries]))
            grad_prob = dot(v_ref[:, lanes], in_pair(h, doT_ref[head_rows(h), queries]))
            return scores, grad_prob

        def weigh(h, scores, grad_prob):
            shift = bias_ref[:, :window] - log_ref[h : h + 1, queries]
            probs = jnp.exp2(scores * EXP2_SCALE + shift)
            grad_score = probs * (grad_prob - delta_ref[h : h + 1, queries])
            return probs.astype(bf16), grad_score.astype(bf16)

        def gather(h, probs, grad_score):
            lanes = pair_lanes(h)
            dv = dot(probs, do_ref[queries, lanes])
            dk = dot(grad_score, q_ref[queries, lanes])
            dqT_ref[head_rows(h), queries] += dot(kT_ref[head_rows(h), :], grad_score)
            if h % 2 == 0:
                even[0] = (dv, dk)
            else:
                dk = jnp.where(low_half, even[0][1], dk) * SCORE_SCALE
                dv = jnp.where(low_half, even[0][0], dv)
                for part, value in ((1, dk), (2, dv)):
                    at_lanes = slice(part * width + lanes.start, part * width + lanes.stop)
                    grad_ref[keys, at_lanes] = value.astype(bf16)

        made = products(0)
        held = None
        for h in range(heads):
            now = made
            if h + 1 < heads:
                made = products(h + 1)
            weighed = weigh(h, *now)
            if held is not None:
                gather(h - 1, *held)
            held = weighed
        gather(heads - 1, *held)

    with_window(first, last, row_len, body)

    @pl.when(at == pl.num_programs(2) - 1)
    def _():
        grad_ref[:, :width] = (dqT_ref[...] * SCORE_SCALE).astype(bf16).T
        sum_ref[0:1, :] += column_sum(grad_ref[:, :width].astype(f32))
        sum_ref[1:2, :] += column_sum(grad_ref[:, 2 * width :].astype(f32))


def attend_rows_back(bounds, qkv, qkvT, do, doT, outT, log, first, count, block):
    rows = bounds.shape[0]
    tokens = do.shape[0]
    width = GROUP * HD
    groups = H // GROUP
    row_len = tokens // rows
    blocks = row_len // block
    whole = pl.BlockSpec((row_len, width), lambda g, r, b, s: (r, first + g))
    wholeT = pl.BlockSpec((width, row_len), lambda g, r, b, s: (first + g, r))

    def part(j):
        return lambda g, r, b, s: (r * blocks + b, j * groups + first + g)

    def partT(j):
        return lambda g, r, b, s: (j * groups + first + g, r * blocks + b)

    return pl.pallas_call(
        attend_back_kernel,
        grid_spec=pltpu.PrefetchScalarGridSpec(
            num_scalar_prefetch=1,
            grid=(count, rows, blocks),
            in_specs=[
                pl.BlockSpec((block, width), part(1)),
                pl.BlockSpec((width, block), partT(1)),
                pl.BlockSpec((block, width), part(2)),
                whole,
                wholeT,
                whole,
                wholeT,
                wholeT,
                pl.BlockSpec((GROUP_ROWS, row_len), lambda g, r, b, s: (first + g, r)),
            ],
            out_specs=[
                pl.BlockSpec((row_len, 3 * width), lambda g, r, b, s: (r, g)),
                pl.BlockSpec((8, width), lambda g, r, b, s: (0, g)),
            ],
            scratch_shapes=[
                pltpu.VMEM((block, max(WINDOWS) * LANES), f32),
                pltpu.VMEM((width, row_len), f32),
                pltpu.VMEM((GROUP_ROWS, row_len), f32),
            ],
        ),
        out_shape=[
            shape_of((tokens, 3 * width * count), bf16),
            shape_of((8, width * count), f32),
        ],
        compiler_params=pltpu.CompilerParams(vmem_limit_bytes=VMEM_LIMIT),
        cost_estimate=cost(
            flops=40 * tokens * row_len * width * count // 4,
            bytes_accessed=22 * tokens * width * count,
            transcendentals=0,
        ),
        name="attend_back",
    )(bounds, qkv, qkvT, qkv, qkv, qkvT, do, doT, outT, log)


def gelu_and_slope(x):
    share = 0.5 + 0.5 * lax.erf(x * math.sqrt(0.5))
    density = jnp.exp(x * x * -0.5) * (1.0 / math.sqrt(2.0 * math.pi))
    return x * share, share + x * density


def normalise(values):
    centred = values - jnp.mean(values, axis=-1, keepdims=True)
    scale = lax.rsqrt(jnp.mean(centred * centred, axis=-1, keepdims=True) + 1e-06)
    return centred * scale, scale


def normalise_back(grad, normed, scale):
    along = jnp.mean(grad * normed, axis=-1, keepdims=True)
    return scale * (grad - jnp.mean(grad, axis=-1, keepdims=True) - normed * along)


class Weights:
    def __init__(self, width, inner, w_out=None, w_in=None, w_ffo=None):
        self.width = width
        self.inner = inner
        self.refs = (w_out, w_in, w_ffo)

    def out(self):
        return self.refs[0][...].reshape(self.width, self.width)

    def into(self, c):
        ref = self.refs[1]
        rows = ref.shape[1] * self.width // self.inner
        return ref[:, c * rows : (c + 1) * rows, :].reshape(self.width, self.width)

    def ffo(self, c):
        ref = self.refs[2]
        if ref.shape[0] == 1:
            return ref[0, c * self.width : (c + 1) * self.width, :]
        groups = ref.shape[0] * self.width // self.inner
        return ref[c * groups : (c + 1) * groups].reshape(self.width, self.width)


def dense_kernel(
    side_ref, attn_ref, x_ref, mine_ref, other_ref, wo_ref, wi_ref, wf_ref, vec_ref, bi_ref,
    keep_ref, send_ref, act_ref, gp_ref, gs_ref, low_ref, gr1_ref, gb_ref, do_ref, doT_ref, sum_ref,
    sum_in_ref, slope_ref,
):
    width = x_ref.shape[1]
    inner = bi_ref.shape[1]
    weights = Weights(width, inner, wo_ref, wi_ref, wf_ref)
    bias_out, gain_a, shift_a, bias_ffo, gain_f, shift_f = [vec_ref[j : j + 1, :] for j in range(6)]

    @pl.when((pl.program_id(0) == 0) & (pl.program_id(1) == 0) & (pl.program_id(2) == 0))
    def _():
        sum_ref[...] = jnp.zeros(sum_ref.shape, f32)
        sum_in_ref[...] = jnp.zeros(sum_in_ref.shape, f32)

    branch = dot_tn(attn_ref[...], weights.out()) + bias_out
    normed_a, scale_a = normalise(x_ref[...].astype(f32) + branch)
    hidden = normed_a * gain_a + shift_a
    low = hidden.astype(bf16)
    low_ref[...] = low
    cuts = [slice(c * width, (c + 1) * width) for c in range(inner // width)]
    last = len(cuts) - 1

    second = None
    held = None
    made = dot(low, weights.into(0))
    for c, cut in enumerate(cuts):
        pre = made + bi_ref[0:1, cut]
        if c < last:
            made = dot(low, weights.into(c + 1))
        value, slope = gelu_and_slope(pre)
        value = value.astype(bf16)
        act_ref[:, cut] = value
        slope_ref[:, cut] = slope.astype(bf16)
        if held is not None:
            term = dot(held, weights.ffo(c - 1))
            second = term if second is None else second + term
        held = value
    term = dot(held, weights.ffo(last))
    second = term if second is None else second + term

    normed_f, scale_f = normalise(hidden + (second + bias_ffo))
    out = (normed_f * gain_f + shift_f).astype(bf16)
    own = pl.program_id(1) == side_ref[0]

    @pl.when(own)
    def _():
        keep_ref[...] = out

    @pl.when(jnp.logical_not(own))
    def _():
        send_ref[...] = out

    cot = jnp.where(own, mine_ref[...], other_ref[...]).astype(f32)
    grad_r2 = normalise_back(cot * gain_f, normed_f, scale_f)
    grad_second = grad_r2.astype(bf16)
    gs_ref[...] = grad_second
    sum_ref[0:1, :] += column_sum(cot * normed_f)
    sum_ref[1:2, :] += column_sum(cot)
    sum_ref[2:3, :] += column_sum(grad_second.astype(f32))

    grad_hidden = grad_r2
    held = None
    made = dot_nt(grad_second, weights.ffo(0))
    for c, cut in enumerate(cuts):
        grad_act = made
        if c < last:
            made = dot_nt(grad_second, weights.ffo(c + 1))
        grad_pre = (grad_act * slope_ref[:, cut].astype(f32)).astype(bf16)
        gp_ref[:, cut] = grad_pre
        sum_in_ref[0:1, cut] += column_sum(grad_pre.astype(f32))
        if held is not None:
            grad_hidden = grad_hidden + dot_nt(held, weights.into(c - 1))
        held = grad_pre
    grad_hidden = grad_hidden + dot_nt(held, weights.into(last))

    grad_r1 = normalise_back(grad_hidden * gain_a, normed_a, scale_a)
    gr1_ref[...] = grad_r1
    grad_branch = grad_r1.astype(bf16)
    gb_ref[...] = grad_branch
    sum_ref[3:4, :] += column_sum(grad_hidden * normed_a)
    sum_ref[4:5, :] += column_sum(grad_hidden)
    sum_ref[5:6, :] += column_sum(grad_branch.astype(f32))
    grad_attn = dot_nt(grad_branch, weights.out()).astype(bf16)
    do_ref[...] = grad_attn
    doT_ref[...] = grad_attn.T


def held(shape, index):
    return pl.BlockSpec(shape, lambda *_: index, pipeline_mode=pl.Buffered(1))


def dense(side, attn, x, mine, other, weights, vectors, bias_in, block):
    rows, half, width = other.shape
    tokens = 2 * rows * half
    inner = bias_in.shape[1]
    block = min(block, half)
    blocks = half // block
    mine_at, other_at = halves(mine, other, block)

    def at(r, h, b, s):
        return ((r * 2 + h) * blocks + b, 0)

    narrow = pl.BlockSpec((block, width), at)
    wide = pl.BlockSpec((block, inner), at)

    return pl.pallas_call(
        dense_kernel,
        grid_spec=pltpu.PrefetchScalarGridSpec(
            num_scalar_prefetch=1,
            grid=(rows, 2, blocks),
            in_specs=[
                pl.BlockSpec((width, block), lambda *i: (0, at(*i)[0])),
                narrow,
                pl.BlockSpec((block, width), mine_at),
                pl.BlockSpec((block, width), other_at),
            ]
            + [held(shape, index) for _, shape, index in weights]
            + [held(vectors.shape, (0, 0)), held(bias_in.shape, (0, 0))],
            out_specs=[
                pl.BlockSpec((block, width), mine_at),
                pl.BlockSpec((block, width), other_at),
                wide, wide, narrow, narrow, narrow, narrow, narrow,
                pl.BlockSpec((width, block), lambda *i: (0, at(*i)[0])),
                pl.BlockSpec((8, width), lambda *_: (0, 0)),
                pl.BlockSpec((8, inner), lambda *_: (0, 0)),
            ],
            scratch_shapes=[pltpu.VMEM((block, inner), bf16)],
        ),
        out_shape=[
            shape_of((mine.shape[0] * half, width), bf16),
            shape_of((rows * half, width), bf16),
            shape_of((tokens, inner), bf16),
            shape_of((tokens, inner), bf16),
            shape_of((tokens, width), bf16),
            shape_of((tokens, width), bf16),
            shape_of((tokens, width), f32),
            shape_of((tokens, width), bf16),
            shape_of((tokens, width), bf16),
            shape_of((width, tokens), bf16),
            shape_of((8, width), f32),
            shape_of((8, inner), f32),
        ],
        compiler_params=pltpu.CompilerParams(vmem_limit_bytes=VMEM_LIMIT),
        cost_estimate=cost(
            flops=2 * tokens * width * (2 * width + 4 * inner),
            bytes_accessed=tokens * (22 * width + 4 * inner) + 4 * width * inner,
            transcendentals=2 * tokens * inner,
        ),
        name="dense",
    )(
        side, attn, x, mine.reshape(-1, width), other.reshape(-1, width),
        *[array for array, _, _ in weights], vectors, bias_in,
    )


def share(place_ref, blocks, keep, send):
    core = lax.rem(place_ref[1], 2)

    @pl.when(core == 0)
    def _():
        keep(blocks[:, 0])
        send(blocks[:, 1])

    @pl.when(core == 1)
    def _():
        keep(blocks[:, 1])
        send(blocks[:, 0])


def store(ref, *at):
    def body(value):
        ref[at if at else ...] = value

    return body


def split_product_kernel(place_ref, a_ref, b_ref, keep_ref, send_ref):
    made = dot_tn(a_ref[...], b_ref[...]).astype(bf16)
    made = made.reshape((keep_ref.shape[0], 2) + keep_ref.shape[1:])
    share(place_ref, made, store(keep_ref), store(send_ref))


def split_product(place, a, b, shards):
    tokens, width = a.shape
    steps = b.shape[1] // width
    shard = width // shards
    out = pl.BlockSpec((shards // 2, shard, width), lambda i, s: (0, i, 0))
    return pl.pallas_call(
        split_product_kernel,
        grid_spec=pltpu.PrefetchScalarGridSpec(
            num_scalar_prefetch=1,
            grid=(steps,),
            in_specs=[
                pl.BlockSpec((tokens, width), lambda i, s: (0, 0), pipeline_mode=pl.Buffered(1)),
                pl.BlockSpec((tokens, width), lambda i, s: (0, i)),
            ],
            out_specs=[out] * 2,
        ),
        out_shape=[shape_of((shards // 2, steps * shard, width), bf16)] * 2,
        compiler_params=pltpu.CompilerParams(vmem_limit_bytes=VMEM_LIMIT),
        cost_estimate=cost(
            flops=2 * tokens * width * b.shape[1],
            bytes_accessed=2 * (a.size + b.size + width * b.shape[1]),
        ),
        name="split_product",
    )(place, a, b)


def pair_product_kernel(a_ref, b_ref, cT_ref, d_ref, out_ref):
    groups, rows, width = out_ref.shape
    first = a_ref.shape[1] // groups
    made = dot_tn(a_ref[...], b_ref[...]).astype(bf16)
    out_ref[:, :first, :] = made.reshape(groups, first, width)
    made = dot(cT_ref[...], d_ref[...]).astype(bf16)
    out_ref[:, first:, :] = made.reshape(groups, rows - first, width)


def pair_product(a, b, cT, d, shards):
    tokens, width = b.shape
    steps = a.shape[1] // width
    rows = (a.shape[1] + cT.shape[0]) // shards
    still = {"index_map": lambda i: (0, 0), "pipeline_mode": pl.Buffered(1)}
    return pl.pallas_call(
        pair_product_kernel,
        grid=(steps,),
        in_specs=[
            pl.BlockSpec((tokens, width), lambda i: (0, i)),
            pl.BlockSpec((tokens, width), **still),
            pl.BlockSpec((cT.shape[0] // steps, tokens), lambda i: (i, 0)),
            pl.BlockSpec((tokens, width), **still),
        ],
        out_specs=pl.BlockSpec((shards // steps, rows, width), lambda i: (i, 0, 0)),
        out_shape=shape_of((shards, rows, width), bf16),
        compiler_params=pltpu.CompilerParams(vmem_limit_bytes=VMEM_LIMIT),
        cost_estimate=cost(
            flops=2 * tokens * width * (a.shape[1] + cT.shape[0]),
            bytes_accessed=2 * (a.size + b.size + cT.size + d.size + shards * rows * width),
        ),
        name="pair_product",
    )(a, b, cT, d)


def input_grad_kernel(side_ref, g_ref, gr1_ref, w_ref, keep_ref, send_ref):
    width = send_ref.shape[1]
    total = gr1_ref[...] + dot_nt(g_ref[...], w_ref[:, : 3 * width])
    low = total.astype(bf16)
    own = pl.program_id(1) == side_ref[0]

    @pl.when(own)
    def _():
        keep_ref[...] = low

    @pl.when(jnp.logical_not(own))
    def _():
        send_ref[...] = low


def input_grad(side, grad_qkv, grad_r1, weight, mine, other, block):
    rows, half, width = other.shape
    block = min(block, half)
    blocks = half // block
    mine_at, other_at = halves(mine, other, block)

    def at(r, h, b, s):
        return ((r * 2 + h) * blocks + b, 0)

    keep, send = pl.pallas_call(
        input_grad_kernel,
        grid_spec=pltpu.PrefetchScalarGridSpec(
            num_scalar_prefetch=1,
            grid=(rows, 2, blocks),
            in_specs=[
                pl.BlockSpec((block, grad_qkv.shape[1]), at),
                pl.BlockSpec((block, width), at),
                pl.BlockSpec(weight.shape, lambda *_: (0, 0), pipeline_mode=pl.Buffered(1)),
            ],
            out_specs=[
                pl.BlockSpec((block, width), mine_at),
                pl.BlockSpec((block, width), other_at),
            ],
        ),
        out_shape=[shape_of((v.shape[0] * half, width), bf16) for v in (mine, other)],
        compiler_params=pltpu.CompilerParams(vmem_limit_bytes=VMEM_LIMIT),
        cost_estimate=cost(
            flops=12 * rows * half * width * width,
            bytes_accessed=24 * rows * half * width + 6 * width * width,
            transcendentals=0,
        ),
        name="input_grad",
    )(side, grad_qkv, grad_r1, weight)
    return keep.reshape(mine.shape), send.reshape(other.shape)


def vector_block(sums_ref, sums_in_ref, sums_qv_ref, shards):
    qv = jnp.concatenate([sums_qv_ref[j : j + 1, :] for j in range(2)], axis=1)
    rows = [sums_ref[j : j + 1, :] for j in range(6)]
    found = []
    for v in (qv, rows[5], rows[3], rows[4], sums_in_ref[0:1, :], rows[2], rows[0], rows[1]):
        found.extend(gather_vector(v, shards))
    return [v.astype(bf16) for v in found]


def last_product_kernel(place_ref, a_ref, b_ref, *refs, shards):
    keep_ref, send_ref = refs[-2:]
    at = pl.program_id(0)
    width = a_ref.shape[1]
    shard = width // shards
    made = dot_tn(a_ref[...], b_ref[...]).astype(bf16)
    here = (slice(None), pl.ds(pl.multiple_of(at * shard, 16), shard), slice(None))
    made = made.reshape(shards // 2, 2, shard, width)
    share(place_ref, made, store(keep_ref, *here), store(send_ref, *here))

    @pl.when(at == pl.num_programs(0) - 1)
    def _():
        end = keep_ref.shape[1] - 16
        for ref in (keep_ref, send_ref):
            ref[:, end:, :] = jnp.zeros((shards // 2, 16, width), bf16)
        for j, v in enumerate(vector_block(*refs[:3], shards)):
            here = (slice(None), slice(end + j, end + j + 1), slice(0, LANES))
            v = v.reshape(shards // 2, 2, 1, LANES)
            share(place_ref, v, store(keep_ref, *here), store(send_ref, *here))


def last_product(place, a, b, sums, shards):
    tokens, width = a.shape
    steps = b.shape[1] // width
    shard = width // shards
    out = (shards // 2, steps * shard + 16, width)
    return pl.pallas_call(
        functools.partial(last_product_kernel, shards=shards),
        grid_spec=pltpu.PrefetchScalarGridSpec(
            num_scalar_prefetch=1,
            grid=(steps,),
            in_specs=[
                pl.BlockSpec((tokens, width), lambda i, s: (0, 0), pipeline_mode=pl.Buffered(1)),
                pl.BlockSpec((tokens, width), lambda i, s: (0, i)),
            ]
            + [pl.BlockSpec(v.shape, lambda i, s: (0, 0)) for v in sums],
            out_specs=[pl.BlockSpec(out, lambda i, s: (0, 0, 0))] * 2,
        ),
        out_shape=[shape_of(out, bf16)] * 2,
        compiler_params=pltpu.CompilerParams(vmem_limit_bytes=VMEM_LIMIT),
        cost_estimate=cost(
            flops=2 * tokens * width * b.shape[1],
            bytes_accessed=2 * (a.size + b.size + width * b.shape[1]),
            transcendentals=0,
        ),
        name="last_product",
    )(place, a, b, *sums)


def split_heads(values):
    return values.reshape(values.shape[0], values.shape[1], H, HD)


def gathered_probs(queries, keys, allowed):
    scores = jnp.einsum("rqhd,rkhd->rhqk", queries, keys, preferred_element_type=f32)
    return jax.nn.softmax(jnp.where(allowed, scores * SCORE_SCALE, MASKED), axis=-1)


def attend_gathered(bounds, qkv, rows, seq_index):
    width = qkv.shape[1] // 3
    parts = qkv.reshape(rows, -1, 3 * width)
    tok_seq = parts.shape[1]
    whole = lax.all_gather(parts[:, :, width:], "seq", axis=1, tiled=True)
    row_len = whole.shape[1]
    queries = split_heads(parts[:, :, :width])
    keys = split_heads(whole[:, :, :width])
    values = split_heads(whole[:, :, width:])
    positions = jnp.arange(row_len, dtype=jnp.int32)
    segments = jnp.sum((positions[None, :, None] >= bounds[:, None, :]).astype(jnp.int32), axis=2)
    mine = lax.dynamic_slice_in_dim(segments, seq_index * tok_seq, tok_seq, 1)
    allowed = mine[:, None, :, None] == segments[:, None, None, :]
    probs = gathered_probs(queries, keys, allowed)
    attended = jnp.einsum(
        "rhqk,rkhd->rqhd", probs.astype(bf16), values, preferred_element_type=f32
    )
    return attended.astype(bf16).reshape(-1, width), (queries, keys, values, allowed)


def attend_gathered_back(saved, attn, do):
    queries, keys, values, allowed = saved
    rows, tok_seq = queries.shape[:2]
    width = attn.shape[1]
    probs = gathered_probs(queries, keys, allowed)
    do = do.reshape(rows, tok_seq, H, HD)
    delta = jnp.sum(do.astype(f32) * attn.reshape(do.shape).astype(f32), axis=-1)
    grad_prob = jnp.einsum("rqhd,rkhd->rhqk", do, values, preferred_element_type=f32)
    grad_score = (probs * (grad_prob - delta.transpose(0, 2, 1)[..., None])).astype(bf16)
    dq = jnp.einsum("rhqk,rkhd->rqhd", grad_score, keys, preferred_element_type=f32) * SCORE_SCALE
    dk = (
        jnp.einsum("rhqk,rqhd->rkhd", grad_score, queries, preferred_element_type=f32)
        * SCORE_SCALE
    )
    dv = jnp.einsum("rhqk,rqhd->rkhd", probs.astype(bf16), do, preferred_element_type=f32)
    pair = jnp.concatenate([dk.reshape(rows, -1, width), dv.reshape(rows, -1, width)], axis=-1)
    pair = lax.psum_scatter(pair.astype(bf16), "seq", scatter_dimension=1, tiled=True)
    pair = pair.reshape(-1, 2 * width)
    dq = dq.astype(bf16).reshape(-1, width)
    dk, dv = pair[:, :width], pair[:, width:]
    sums = jnp.stack([jnp.sum(dq.astype(f32), axis=0), jnp.sum(dv.astype(f32), axis=0)])
    return jnp.concatenate([dq, dk, dv], axis=1), jnp.pad(sums, ((0, 6), (0, 0)))


def swapped(values):
    return lax.ppermute(values, "seq", [(0, 1), (1, 0)])


def other_half(values, seq_index):
    rows = values.shape[0] // 2
    return swapped(lax.dynamic_slice_in_dim(values, (1 - seq_index) * rows, rows, 0))


def placed(values, came, seq_index, row=0):
    at = (1 - seq_index) * (values.shape[0] // 2) + row
    return lax.dynamic_update_slice_in_dim(values, came, at, 0)


def coordinates(count):
    return ((2, 1), (count // 8, 2), (4, count // 4))


def turned(values, axis, size, stride, step):
    perm = []
    for i in range(lax.axis_size(axis)):
        at = (i // stride) % size
        perm.append((i, i + ((at + step) % size - at) * stride))
    return lax.ppermute(values, axis, perm)


class StagedSum:
    def __init__(self, keep, send, axis):
        self.axis = axis
        self.sizes = coordinates(lax.axis_size(axis))
        self.index = lax.axis_index(axis)
        self.own = keep
        size, stride = self.sizes[0]
        self.came = [turned(send, axis, size, stride, 1)]

    def sum(self, pick):
        total = pick(self.own).astype(f32)
        for values in self.came:
            total = total + pick(values).astype(f32)
        return total.astype(bf16)

    def step(self, at):
        size, stride = self.sizes[at]
        here = (self.index // stride) % size

        def part(step):
            def pick(values):
                blocks = values.reshape((-1, size) + values.shape[1:])
                return lax.dynamic_index_in_dim(blocks, (here + step) % size, 1, False)

            return self.sum(pick)

        came = [
            turned(part(step), self.axis, size, stride, step) for step in range(1, size)
        ]
        self.own, self.came = part(0), came

    def result(self):
        return self.sum(lambda values: values[0])


def tied(*values):
    return lax.optimization_barrier(values)


def gather_pieces(values, axis):
    pieces = [(values, (0, 0, 0))]
    for at, (size, stride) in reversed(list(enumerate(coordinates(lax.axis_size(axis))))):
        more = []
        for piece, back in pieces:
            for step in range(1, size):
                came = turned(piece, axis, size, stride, step)
                more.append((came, back[:at] + (step,) + back[at + 1 :]))
        pieces = pieces + more
    return pieces


def piece_owner(index, back, count):
    owner = jnp.int32(0)
    for (size, stride), step in zip(coordinates(count), back):
        owner = owner + lax.rem(lax.rem(index // stride, size) + (size - step), size) * stride
    return owner


def per_device(
    tokens,
    weight_qkv,
    bias_qv,
    weight_out,
    bias_out,
    gain_attn,
    shift_attn,
    weight_in,
    bias_in,
    weight_ffo,
    bias_ffo,
    gain_ffn,
    shift_ffn,
    lengths,
    cotangent,
):
    rows, tok_seq, width = tokens.shape
    seq_count = lax.axis_size("seq")
    seq_index = lax.axis_index("seq")
    shards = lax.axis_size("dp")
    shard = weight_qkv.shape[0]
    by_rows = seq_count == 2 and rows % 2 == 0 and shards % 8 == 0 and shard % 16 == 0
    inner = weight_in.shape[1]
    chunks = inner // width
    token_count = rows * tok_seq

    small = (bias_qv, bias_out, gain_attn, shift_attn, bias_in, bias_ffo, gain_ffn, shift_ffn)
    first, others = lower(weight_qkv, weight_in, weight_ffo, weight_out, small)
    if by_rows:
        first = gather_pieces(first, "dp")
        backs = [back for _, back in first]
    else:
        first = [(lax.all_gather(first, "dp", axis=0, tiled=True), None)]
    others = lax.all_gather(others[None], "dp", axis=0, tiled=True)
    if shard % 16 == 0:
        weights = (
            (others, (shards, shard, width), (0, 2 * chunks, 0)),
            (others, (shards, chunks * shard, width), (0, 0, 0)),
            (others, (shards, chunks * shard, width), (0, 1, 0)),
        )
    else:
        part = chunks * shard
        w_in = others[:, :part].reshape(shards, chunks, shard, width).transpose(1, 0, 2, 3)
        w_in = w_in.reshape(1, inner, width)
        w_ffo = others[:, part : 2 * part].reshape(1, inner, width)
        w_out = others[:, 2 * part :].reshape(1, width, width)
        weights = [(w, w.shape, (0, 0, 0)) for w in (w_out, w_in, w_ffo)]

    bounds = jnp.cumsum(lengths, axis=1)
    if by_rows:
        mine = rows // 2
        bounds = lax.dynamic_slice_in_dim(bounds, seq_index * mine, mine, 0)
        side = jnp.stack([seq_index, lax.axis_index("dp")]).astype(jnp.int32)
        x_other = other_half(tokens, seq_index)
        first, x_other, held_cot = tied([w for w, _ in first], x_other, cotangent)
        x_halves = tokens, x_other
        first = list(zip(first, backs))
        cot_halves = cotangent, other_half(held_cot, seq_index)
    else:
        mine = 1
        side = jnp.zeros((2,), jnp.int32)
        x_halves = tokens.reshape(2, 1, -1, width)
        cot_halves = cotangent.reshape(2, 1, -1, width)
    half = x_halves[1].shape[1]

    x, qkv, qkvT, w_qkv, vec, in_bias = project(side, *x_halves, first, inner, BLOCK)
    if by_rows:
        attnT, log = attend_rows(bounds, qkv, qkvT, BLOCK)
    else:
        attn, saved = attend_gathered(bounds, qkv, rows, seq_index)
        attnT = attn.T
    out, out_other, act, gp, gs, low, gr1, gb, do, doT, sums, sums_in = dense(
        side, attnT, x, *cot_halves, weights, vec, in_bias, BLOCK
    )
    out = out.reshape(-1, half, width)
    out_other = out_other.reshape(-1, half, width)
    part = chunks * shard
    if by_rows:
        out_other = swapped(out_other)
        g_in = split_product(side, low, gp, shards)
        *g_in, act = tied(*g_in, act)
        in_sum = StagedSum(*g_in, "dp")
        g_ffo = pair_product(act, gs, attnT, gb, shards)
    else:
        out = jnp.concatenate([out, out_other], axis=1).reshape(rows, tok_seq, width)
        g_ffo = dot_tn(act, gs).astype(bf16).reshape(shards, part, width)
        g_in = dot_tn(low, gp).astype(bf16).reshape(shards, shard, chunks, width)
        g_in = g_in.transpose(0, 2, 1, 3).reshape(shards, part, width)
        g_out = dot_tn(attn, gb).astype(bf16).reshape(shards, shard, width)
        g_ffo = jnp.concatenate([g_ffo, g_out], axis=1)
        g_in = lax.psum_scatter(g_in, "dp", scatter_dimension=0, tiled=True)[0]
    if by_rows:
        g_ffo, do, in_sum.came = tied(g_ffo, do, in_sum.came)
    g_ffo = lax.psum_scatter(g_ffo, "dp", scatter_dimension=0, tiled=True)[0]

    if by_rows:
        in_sum.step(1)
        g_x, sums_qv = attend_rows_back(bounds, qkv, qkvT, do, doT, attnT, log, 0, 1, BLOCK)
        g_x, out_other, in_sum.came = tied(g_x, out_other, in_sum.came)
        in_sum.step(2)
        g_qkv = last_product(side, x, g_x, (sums, sums_in, sums_qv), shards)
        g_qkv, gr1 = tied(g_qkv, gr1)
        qkv_sum = StagedSum(*g_qkv, "dp")
        grad_x, grad_other = input_grad(side, g_x, gr1, w_qkv, *x_halves, BLOCK)
        grad_other, qkv_sum.came = tied(grad_other, qkv_sum.came)
        qkv_sum.step(1)
        grad_other = [swapped(grad_other[r : r + 1]) for r in range(mine)]
        qkv_sum.came, in_sum.came, grad_other[0] = tied(
            qkv_sum.came, in_sum.came, grad_other[0]
        )
        qkv_sum.step(2)
        g_in = in_sum.result()
        both = swapped(jnp.concatenate([g_in, g_ffo], axis=0))
        qkv_sum.came, both, grad_other = tied(qkv_sum.came, both, grad_other)
        g_qkv = qkv_sum.result()
        for r in range(mine):
            grad_x = placed(grad_x, grad_other[r], seq_index, r)
        out = placed(out, out_other, seq_index)
        g_in = g_in.astype(f32) + both[:part].astype(f32)
        g_ffo = g_ffo.astype(f32) + both[part:].astype(f32)
        g_qkv = g_qkv.astype(f32) + swapped(g_qkv).astype(f32)
    else:
        g_x, sums_qv = attend_gathered_back(saved, attn, do)
        vectors = []
        for v in (sums_qv[:2].reshape(-1), sums[5], sums[3], sums[4], sums_in[0], sums[2], sums[0], sums[1]):
            v = v.reshape(shards, -1)
            vectors.append(jnp.pad(v, ((0, 0), (0, -v.shape[1] % LANES))).reshape(shards, -1, LANES))
        vectors = jnp.concatenate(vectors, axis=1).astype(bf16)
        vectors = jnp.pad(vectors, ((0, 0), (0, 16 - vectors.shape[1]), (0, width - LANES)))
        g_qkv = dot_tn(x, g_x).astype(bf16).reshape(shards, shard, 3, width)
        g_qkv = g_qkv.transpose(0, 2, 1, 3).reshape(shards, 3 * shard, width)
        g_qkv = jnp.concatenate([g_qkv, vectors], axis=1)
        g_qkv = lax.psum_scatter(g_qkv, "dp", scatter_dimension=0, tiled=True)[0]
        grad_x, grad_other = input_grad(side, g_x, gr1, w_qkv, *x_halves, BLOCK)
        grad_x = jnp.concatenate([grad_x, grad_other], axis=1).reshape(rows, tok_seq, width)
        g_ffo, g_in, g_qkv = [lax.psum(v, "seq").astype(f32) for v in (g_ffo, g_in, g_qkv)]
    vectors = g_qkv[3 * shard :, :LANES]
    d_qkv = jnp.concatenate([g_qkv[j * shard : (j + 1) * shard] for j in range(3)], axis=1)
    d_ffo, d_out = g_ffo[:part], g_ffo[part:]
    d_in = jnp.concatenate([g_in[c * shard : (c + 1) * shard] for c in range(chunks)], axis=1)
    sizes = [v.shape[0] for v in small]
    d_small = []
    for row, size in zip(vector_rows(sizes)[0], sizes):
        d_small.append(vectors[row : row - (-size // LANES)].reshape(-1)[:size])
    g_qv, g_bo, g_ga, g_sa, g_bi, g_bf, g_gf, g_sf = d_small
    return (
        out, grad_x, d_qkv, g_qv, d_out, g_bo, g_ga, g_sa, d_in, g_bi, d_ffo,
        g_bf, g_gf, g_sf,
    )


def solution(mesh):
    by_token = P("dp", "seq", None)
    weight = P("dp", None)
    vector = P("dp")
    params = (
        weight, vector, weight, vector, vector, vector, weight, vector, weight, vector, vector,
        vector,
    )
    return jax.shard_map(
        per_device,
        mesh=mesh,
        in_specs=(by_token,) + params + (weight, by_token),
        out_specs=(by_token, by_token) + params,
        check_vma=False,
    )
```

```python
import functools
import math

import jax
import jax.numpy as jnp
from jax import lax
from jax.experimental import pallas as pl
from jax.experimental.pallas import tpu as pltpu
from jax.sharding import PartitionSpec as P

H = 12
HD = 64
PAIR = 2 * HD
LANES = 128
f32 = jnp.float32
bf16 = jnp.bfloat16
SCORE_SCALE = 1.0 / math.sqrt(HD)
EXP2_SCALE = SCORE_SCALE * math.log2(math.e)
MASKED = -1e30
VMEM_LIMIT = 60 << 20
BLOCK = 256
TALL = 512
COST = 4
GROUP = H
GROUP_ROWS = -(-GROUP // 8) * 8
WINDOWS = (2, 3, 4, 5, 6)


def dot(a, b):
    return jnp.dot(a, b, preferred_element_type=f32)


def dot_nt(a, b):
    return lax.dot_general(a, b, (((1,), (1,)), ((), ())), preferred_element_type=f32)


def dot_tn(a, b):
    return lax.dot_general(a, b, (((0,), (0,)), ((), ())), preferred_element_type=f32)


def column_sum(values):
    return jnp.sum(values, axis=0, keepdims=True)


def cost(flops, bytes_accessed, transcendentals=0):
    return pl.CostEstimate(
        flops=flops // COST, bytes_accessed=bytes_accessed // COST, transcendentals=transcendentals // COST
    )


def shape_of(shape, dtype):
    return jax.ShapeDtypeStruct(shape, dtype)


def vector_rows(sizes):
    rows = []
    at = 0
    for size in sizes:
        rows.append(at)
        at += -(-size // LANES)
    return rows, at


def lower_kernel(*refs):
    w_qkv, w_in, w_ffo, w_out = refs[:4]
    small = refs[4:-3]
    first_ref, others_ref, block_ref = refs[-3:]
    columns = w_qkv.shape[1]
    shard, width = w_out.shape
    first_ref[:, :columns] = w_qkv[...].astype(bf16)
    block_ref[...] = jnp.zeros(block_ref.shape, f32)
    for ref, row in zip(small, vector_rows([r.shape[1] for r in small])[0]):
        size = ref.shape[1]
        for at in range(0, size, LANES):
            n = min(LANES, size - at)
            block_ref[row : row + 1, :n] = ref[:, at : at + n]
            row += 1
    first_ref[:, columns:] = block_ref[...].astype(bf16)
    chunks = w_in.shape[1] // width
    for c in range(chunks):
        others_ref[c * shard : (c + 1) * shard, :] = w_in[:, c * width : (c + 1) * width].astype(bf16)
    others_ref[chunks * shard : 2 * chunks * shard, :] = w_ffo[...].astype(bf16)
    others_ref[2 * chunks * shard :, :] = w_out[...].astype(bf16)


def lower(w_qkv, w_in, w_ffo, w_out, small):
    shard, columns = w_qkv.shape
    width = w_out.shape[1]
    chunks = w_in.shape[1] // width
    return pl.pallas_call(
        lower_kernel,
        out_shape=[
            shape_of((shard, columns + LANES), bf16),
            shape_of(((2 * chunks + 1) * shard, width), bf16),
        ],
        scratch_shapes=[pltpu.VMEM((shard, LANES), f32)],
        compiler_params=pltpu.CompilerParams(vmem_limit_bytes=VMEM_LIMIT),
        name="lower",
    )(w_qkv, w_in, w_ffo, w_out, *[v.reshape(1, -1) for v in small])


def places(total, size):
    at = lax.broadcasted_iota(jnp.int32, (1, total), 1)
    return at % size, at // size


def picker(place, at):
    lane = lax.broadcasted_iota(jnp.int32, (LANES, place.shape[1]), 0)
    return jnp.where(place == lane + at, 1.0, 0.0).astype(bf16)


def spread_vector(block, row, size, shards):
    place, owner = places(size * shards, size)
    found = jnp.zeros((shards, size * shards), f32)
    for at in range(0, size, LANES):
        found = found + dot(block[:, row + at // LANES, :].astype(bf16), picker(place, at))
    index = lax.broadcasted_iota(jnp.int32, found.shape, 0)
    return column_sum(jnp.where(owner == index, found, 0.0))


def gather_vector(vector, shards):
    total = vector.shape[1]
    size = total // shards
    place, owner = places(total, size)
    index = lax.broadcasted_iota(jnp.int32, (shards, total), 0)
    own = jnp.where(owner == index, vector, 0.0).astype(bf16)
    return [dot_nt(own, picker(place, at)) for at in range(0, size, LANES)]


def project_kernel(place_ref, mine_ref, other_ref, *refs, shards, pieces):
    x_ref, out_ref, outT_ref, w_ref, vec_ref, bi_ref, bias_ref, sems = refs[len(pieces) :]
    width = x_ref.shape[1]
    columns = out_ref.shape[1]
    shard = width // shards

    @pl.when((pl.program_id(0) == 0) & (pl.program_id(1) == 0) & (pl.program_id(2) == 0))
    def _():
        copies = []
        for j, (ref, back) in enumerate(zip(refs, pieces)):
            start = jnp.int32(0) if back is None else piece_owner(place_ref[1], back, shards) * shard
            rows = pl.ds(pl.multiple_of(start, 16), ref.shape[0])
            copies.append(pltpu.make_async_copy(ref, w_ref.at[rows, :], sems.at[j]))
        for copy in copies:
            copy.start()
        for copy in copies:
            copy.wait()
        block = w_ref[:, columns:].astype(f32).reshape(shards, shard, LANES)
        inner = bi_ref.shape[1]
        totals = (2 * width, width, width, width, inner, width, width, width)
        sizes = [total // shards for total in totals]
        found = [
            spread_vector(block, row, size, shards)
            for row, size in zip(vector_rows(sizes)[0], sizes)
        ]
        bias_ref[0:1, :width] = found[0][:, :width]
        bias_ref[0:1, width : 2 * width] = jnp.zeros((1, width), f32)
        bias_ref[0:1, 2 * width :] = found[0][:, width:]
        bi_ref[0:1, :] = found[4]
        for j, v in enumerate(found[1:4] + found[5:]):
            vec_ref[j : j + 1, :] = v

    x = jnp.where(pl.program_id(1) == place_ref[0], mine_ref[...], other_ref[...])
    x_ref[...] = x
    cuts = [slice(at, at + width) for at in range(0, columns, width)]
    made = dot(x, w_ref[:, cuts[0]])
    for j, cut in enumerate(cuts):
        low = (made + bias_ref[0:1, cut]).astype(bf16)
        if j + 1 < len(cuts):
            made = dot(x, w_ref[:, cuts[j + 1]])
        out_ref[:, cut] = low
        outT_ref[cut, :] = low.T


def halves(mine, other, block):
    rows, half, _ = other.shape
    blocks = half // block
    skip = rows if mine.shape[0] > rows else 0

    def at(used, r, h, b):
        rest = jnp.where(h == 0, 0, blocks - 1)
        return (r * blocks + jnp.where(used, b, rest), 0)

    return (
        lambda r, h, b, s: at(h == s[0], r + s[0] * skip, h, b),
        lambda r, h, b, s: at(h != s[0], r, h, b),
    )


def project(place, mine, other, weight, inner, block):
    rows, half, width = other.shape
    block = min(block, half)
    blocks = half // block
    columns = 3 * width
    tokens = 2 * rows * half
    shards = lax.axis_size("dp")
    mine_at, other_at = halves(mine, other, block)

    def at(r, h, b, s):
        return ((r * 2 + h) * blocks + b, 0)

    return pl.pallas_call(
        functools.partial(project_kernel, shards=shards, pieces=[back for _, back in weight]),
        grid_spec=pltpu.PrefetchScalarGridSpec(
            num_scalar_prefetch=1,
            grid=(rows, 2, blocks),
            in_specs=[
                pl.BlockSpec((block, width), mine_at),
                pl.BlockSpec((block, width), other_at),
            ]
            + [pl.BlockSpec(memory_space=pl.ANY)] * len(weight),
            out_specs=[
                pl.BlockSpec((block, width), at),
                pl.BlockSpec((block, columns), at),
                pl.BlockSpec((columns, block), lambda *i: (0, at(*i)[0])),
                pl.BlockSpec((width, columns + LANES), lambda *_: (0, 0)),
                pl.BlockSpec((8, width), lambda *_: (0, 0)),
                pl.BlockSpec((8, inner), lambda *_: (0, 0)),
            ],
            scratch_shapes=[
                pltpu.VMEM((8, columns), f32),
                pltpu.SemaphoreType.DMA((len(weight),)),
            ],
        ),
        out_shape=[
            shape_of((tokens, width), bf16),
            shape_of((tokens, columns), bf16),
            shape_of((columns, tokens), bf16),
            shape_of((width, columns + LANES), bf16),
            shape_of((8, width), f32),
            shape_of((8, inner), f32),
        ],
        compiler_params=pltpu.CompilerParams(vmem_limit_bytes=VMEM_LIMIT),
        cost_estimate=cost(
            flops=2 * tokens * width * columns,
            bytes_accessed=2 * (2 * tokens * width + 2 * width * columns + 2 * tokens * columns),
            transcendentals=0,
        ),
        name="project",
    )(place, mine.reshape(-1, width), other.reshape(-1, width), *[w for w, _ in weight])


def passage_range(bounds_ref, row, start, size, row_len):
    first = jnp.int32(0)
    last = jnp.int32(row_len)
    for j in range(bounds_ref.shape[1]):
        bound = bounds_ref[row, j]
        first = jnp.where(bound <= start, jnp.maximum(first, bound), first)
        last = jnp.where(bound >= start + size, jnp.minimum(last, bound), last)
    return first, last


def segments_at(bounds_ref, row, positions):
    count = jnp.zeros(positions.shape, jnp.int32)
    for j in range(bounds_ref.shape[1]):
        count = count + (positions >= bounds_ref[row, j]).astype(jnp.int32)
    return count


def with_window(first, last, row_len, body):
    first_tile = first // LANES
    needed = (last + LANES - 1) // LANES - first_tile
    below = 0
    for tiles in WINDOWS:

        @pl.when((needed > below) & (needed <= tiles))
        def _(tiles=tiles):
            start = jnp.minimum(first_tile, row_len // LANES - tiles)
            body(pl.multiple_of(start * LANES, LANES), tiles * LANES)

        below = tiles


def mask_bias(bounds_ref, row, sub_start, sub_len, lane_start, lane_len):
    down = segments_at(
        bounds_ref, row, sub_start + lax.broadcasted_iota(jnp.int32, (sub_len, LANES), 0)
    )
    across = segments_at(
        bounds_ref, row, lane_start + lax.broadcasted_iota(jnp.int32, (1, lane_len), 1)
    )
    down = jnp.concatenate([down] * (lane_len // LANES), axis=1)
    return jnp.where(down == across, 0.0, MASKED).astype(f32)


def head_rows(h):
    return slice(HD * h, HD * h + HD)


def pair_lanes(h):
    return slice(PAIR * (h // 2), PAIR * (h // 2) + PAIR)


def log_row(h):
    return GROUP_ROWS * (h // GROUP) + h % GROUP


def in_pair(h, rows):
    zero = jnp.zeros_like(rows)
    return jnp.concatenate([rows, zero] if h % 2 == 0 else [zero, rows], axis=0)


def attend_kernel(bounds_ref, k_ref, qT_ref, vT_ref, outT_ref, log_ref, bias_ref):
    row = pl.program_id(0)
    row_len, width = k_ref.shape
    block = qT_ref.shape[1]
    heads = width // HD
    q_start = pl.program_id(1) * block
    first, last = passage_range(bounds_ref, row, q_start, block, row_len)

    def body(start, window):
        keys = pl.ds(start, window)
        bias_ref[:window, :] = mask_bias(bounds_ref, row, start, window, q_start, block)

        def score(h):
            return dot(k_ref[keys, pair_lanes(h)], in_pair(h, qT_ref[head_rows(h), :]))

        def weigh(scores):
            masked = scores + bias_ref[:window, :]
            best = jnp.max(masked, axis=0, keepdims=True)
            return best, jnp.exp2((masked - best) * EXP2_SCALE).astype(bf16)

        def attend(h, best, weights):
            values = jnp.concatenate(
                [vT_ref[head_rows(h), keys], jnp.ones((16, window), bf16)], axis=0
            )
            summed = dot(values, weights)
            total = summed[HD : HD + 1]
            outT_ref[head_rows(h), :] = (summed[:HD] * (1.0 / total)).astype(bf16)
            at = log_row(h)
            log_ref[at : at + 1, :] = best * EXP2_SCALE + jnp.log2(total)

        scores = [score(0), score(1)]
        held = None
        for h in range(0, heads, 2):
            now = scores
            if h + 2 < heads:
                scores = [score(h + 2), score(h + 3)]
            weighed = [weigh(s) for s in now]
            if held is not None:
                attend(h - 2, *held[0])
                attend(h - 1, *held[1])
            held = weighed
        attend(heads - 2, *held[0])
        attend(heads - 1, *held[1])

    with_window(first, last, row_len, body)


def attend_rows(bounds, qkv, qkvT, block):
    rows = bounds.shape[0]
    tokens = qkv.shape[0]
    width = qkv.shape[1] // 3
    row_len = tokens // rows
    blocks = row_len // block
    return pl.pallas_call(
        attend_kernel,
        grid_spec=pltpu.PrefetchScalarGridSpec(
            num_scalar_prefetch=1,
            grid=(rows, blocks),
            in_specs=[
                pl.BlockSpec((row_len, width), lambda r, b, s: (r, 1)),
                pl.BlockSpec((width, block), lambda r, b, s: (0, r * blocks + b)),
                pl.BlockSpec((width, row_len), lambda r, b, s: (2, r)),
            ],
            out_specs=[
                pl.BlockSpec((width, block), lambda r, b, s: (0, r * blocks + b)),
                pl.BlockSpec((H // GROUP * GROUP_ROWS, block), lambda r, b, s: (0, r * blocks + b)),
            ],
            scratch_shapes=[pltpu.VMEM((max(WINDOWS) * LANES, block), f32)],
        ),
        out_shape=[
            shape_of((width, tokens), bf16),
            shape_of((H // GROUP * GROUP_ROWS, tokens), f32),
        ],
        compiler_params=pltpu.CompilerParams(vmem_limit_bytes=VMEM_LIMIT),
        cost_estimate=cost(
            flops=16 * tokens * row_len * width // 4,
            bytes_accessed=10 * tokens * width,
            transcendentals=0,
        ),
        name="attend",
    )(bounds, qkv, qkvT, qkvT)


def attend_back_kernel(
    bounds_ref, k_ref, kT_ref, v_ref, q_ref, qT_ref, do_ref, doT_ref, outT_ref, log_ref,
    grad_ref, sum_ref, bias_ref, dqT_ref, delta_ref,
):
    row = pl.program_id(1)
    at = pl.program_id(2)
    row_len, width = q_ref.shape
    block = k_ref.shape[0]
    heads = width // HD
    k_start = at * block
    keys = pl.ds(pl.multiple_of(k_start, block), block)

    @pl.when((row == 0) & (at == 0))
    def _():
        sum_ref[...] = jnp.zeros(sum_ref.shape, f32)

    @pl.when(at == 0)
    def _():
        dqT_ref[...] = jnp.zeros(dqT_ref.shape, f32)
        for h in range(heads):
            both = doT_ref[head_rows(h), :].astype(f32) * outT_ref[head_rows(h), :].astype(f32)
            delta_ref[h : h + 1, :] = column_sum(both)

    first, last = passage_range(bounds_ref, row, k_start, block, row_len)
    low_half = lax.broadcasted_iota(jnp.int32, (block, PAIR), 1) < HD

    def body(start, window):
        queries = pl.ds(start, window)
        bias_ref[:, :window] = mask_bias(bounds_ref, row, k_start, block, start, window)
        even = {}

        def products(h):
            lanes = pair_lanes(h)
            scores = dot(k_ref[:, lanes], in_pair(h, qT_ref[head_rows(h), queries]))
            grad_prob = dot(v_ref[:, lanes], in_pair(h, doT_ref[head_rows(h), queries]))
            return scores, grad_prob

        def weigh(h, scores, grad_prob):
            shift = bias_ref[:, :window] - log_ref[h : h + 1, queries]
            probs = jnp.exp2(scores * EXP2_SCALE + shift)
            grad_score = probs * (grad_prob - delta_ref[h : h + 1, queries])
            return probs.astype(bf16), grad_score.astype(bf16)

        def gather(h, probs, grad_score):
            lanes = pair_lanes(h)
            dv = dot(probs, do_ref[queries, lanes])
            dk = dot(grad_score, q_ref[queries, lanes])
            dqT_ref[head_rows(h), queries] += dot(kT_ref[head_rows(h), :], grad_score)
            if h % 2 == 0:
                even[0] = (dv, dk)
            else:
                dk = jnp.where(low_half, even[0][1], dk) * SCORE_SCALE
                dv = jnp.where(low_half, even[0][0], dv)
                for part, value in ((1, dk), (2, dv)):
                    at_lanes = slice(part * width + lanes.start, part * width + lanes.stop)
                    grad_ref[keys, at_lanes] = value.astype(bf16)

        made = products(0)
        held = None
        for h in range(heads):
            now = made
            if h + 1 < heads:
                made = products(h + 1)
            weighed = weigh(h, *now)
            if held is not None:
                gather(h - 1, *held)
            held = weighed
        gather(heads - 1, *held)

    with_window(first, last, row_len, body)

    @pl.when(at == pl.num_programs(2) - 1)
    def _():
        grad_ref[:, :width] = (dqT_ref[...] * SCORE_SCALE).astype(bf16).T
        sum_ref[0:1, :] += column_sum(grad_ref[:, :width].astype(f32))
        sum_ref[1:2, :] += column_sum(grad_ref[:, 2 * width :].astype(f32))


def attend_rows_back(bounds, qkv, qkvT, do, doT, outT, log, first, count, block):
    rows = bounds.shape[0]
    tokens = do.shape[0]
    width = GROUP * HD
    groups = H // GROUP
    row_len = tokens // rows
    blocks = row_len // block
    whole = pl.BlockSpec((row_len, width), lambda g, r, b, s: (r, first + g))
    wholeT = pl.BlockSpec((width, row_len), lambda g, r, b, s: (first + g, r))

    def part(j):
        return lambda g, r, b, s: (r * blocks + b, j * groups + first + g)

    def partT(j):
        return lambda g, r, b, s: (j * groups + first + g, r * blocks + b)

    return pl.pallas_call(
        attend_back_kernel,
        grid_spec=pltpu.PrefetchScalarGridSpec(
            num_scalar_prefetch=1,
            grid=(count, rows, blocks),
            in_specs=[
                pl.BlockSpec((block, width), part(1)),
                pl.BlockSpec((width, block), partT(1)),
                pl.BlockSpec((block, width), part(2)),
                whole,
                wholeT,
                whole,
                wholeT,
                wholeT,
                pl.BlockSpec((GROUP_ROWS, row_len), lambda g, r, b, s: (first + g, r)),
            ],
            out_specs=[
                pl.BlockSpec((row_len, 3 * width), lambda g, r, b, s: (r, g)),
                pl.BlockSpec((8, width), lambda g, r, b, s: (0, g)),
            ],
            scratch_shapes=[
                pltpu.VMEM((block, max(WINDOWS) * LANES), f32),
                pltpu.VMEM((width, row_len), f32),
                pltpu.VMEM((GROUP_ROWS, row_len), f32),
            ],
        ),
        out_shape=[
            shape_of((tokens, 3 * width * count), bf16),
            shape_of((8, width * count), f32),
        ],
        compiler_params=pltpu.CompilerParams(vmem_limit_bytes=VMEM_LIMIT),
        cost_estimate=cost(
            flops=40 * tokens * row_len * width * count // 4,
            bytes_accessed=22 * tokens * width * count,
            transcendentals=0,
        ),
        name="attend_back",
    )(bounds, qkv, qkvT, qkv, qkv, qkvT, do, doT, outT, log)


def gelu_and_slope(x):
    share = 0.5 + 0.5 * lax.erf(x * math.sqrt(0.5))
    density = jnp.exp(x * x * -0.5) * (1.0 / math.sqrt(2.0 * math.pi))
    return x * share, share + x * density


def normalise(values):
    centred = values - jnp.mean(values, axis=-1, keepdims=True)
    scale = lax.rsqrt(jnp.mean(centred * centred, axis=-1, keepdims=True) + 1e-06)
    return centred * scale, scale


def normalise_back(grad, normed, scale):
    along = jnp.mean(grad * normed, axis=-1, keepdims=True)
    return scale * (grad - jnp.mean(grad, axis=-1, keepdims=True) - normed * along)


class Weights:
    def __init__(self, width, inner, w_out=None, w_in=None, w_ffo=None):
        self.width = width
        self.inner = inner
        self.refs = (w_out, w_in, w_ffo)

    def out(self):
        return self.refs[0][...].reshape(self.width, self.width)

    def into(self, c):
        ref = self.refs[1]
        rows = ref.shape[1] * self.width // self.inner
        return ref[:, c * rows : (c + 1) * rows, :].reshape(self.width, self.width)

    def ffo(self, c):
        ref = self.refs[2]
        if ref.shape[0] == 1:
            return ref[0, c * self.width : (c + 1) * self.width, :]
        groups = ref.shape[0] * self.width // self.inner
        return ref[c * groups : (c + 1) * groups].reshape(self.width, self.width)


def dense_kernel(
    side_ref, attn_ref, x_ref, mine_ref, other_ref, wo_ref, wi_ref, wf_ref, vec_ref, bi_ref,
    keep_ref, send_ref, act_ref, gp_ref, gs_ref, low_ref, gr1_ref, gb_ref, do_ref, doT_ref, sum_ref,
    sum_in_ref, slope_ref,
):
    width = x_ref.shape[1]
    inner = bi_ref.shape[1]
    weights = Weights(width, inner, wo_ref, wi_ref, wf_ref)
    bias_out, gain_a, shift_a, bias_ffo, gain_f, shift_f = [vec_ref[j : j + 1, :] for j in range(6)]

    @pl.when((pl.program_id(0) == 0) & (pl.program_id(1) == 0) & (pl.program_id(2) == 0))
    def _():
        sum_ref[...] = jnp.zeros(sum_ref.shape, f32)
        sum_in_ref[...] = jnp.zeros(sum_in_ref.shape, f32)

    branch = dot_tn(attn_ref[...], weights.out()) + bias_out
    normed_a, scale_a = normalise(x_ref[...].astype(f32) + branch)
    hidden = normed_a * gain_a + shift_a
    low = hidden.astype(bf16)
    low_ref[...] = low
    cuts = [slice(c * width, (c + 1) * width) for c in range(inner // width)]
    last = len(cuts) - 1

    second = None
    held = None
    made = dot(low, weights.into(0))
    for c, cut in enumerate(cuts):
        pre = made + bi_ref[0:1, cut]
        if c < last:
            made = dot(low, weights.into(c + 1))
        value, slope = gelu_and_slope(pre)
        value = value.astype(bf16)
        act_ref[:, cut] = value
        slope_ref[:, cut] = slope.astype(bf16)
        if held is not None:
            term = dot(held, weights.ffo(c - 1))
            second = term if second is None else second + term
        held = value
    term = dot(held, weights.ffo(last))
    second = term if second is None else second + term

    normed_f, scale_f = normalise(hidden + (second + bias_ffo))
    out = (normed_f * gain_f + shift_f).astype(bf16)
    own = pl.program_id(1) == side_ref[0]

    @pl.when(own)
    def _():
        keep_ref[...] = out

    @pl.when(jnp.logical_not(own))
    def _():
        send_ref[...] = out

    cot = jnp.where(own, mine_ref[...], other_ref[...]).astype(f32)
    grad_r2 = normalise_back(cot * gain_f, normed_f, scale_f)
    grad_second = grad_r2.astype(bf16)
    gs_ref[...] = grad_second
    sum_ref[0:1, :] += column_sum(cot * normed_f)
    sum_ref[1:2, :] += column_sum(cot)
    sum_ref[2:3, :] += column_sum(grad_second.astype(f32))

    grad_hidden = grad_r2
    held = None
    made = dot_nt(grad_second, weights.ffo(0))
    for c, cut in enumerate(cuts):
        grad_act = made
        if c < last:
            made = dot_nt(grad_second, weights.ffo(c + 1))
        grad_pre = (grad_act * slope_ref[:, cut].astype(f32)).astype(bf16)
        gp_ref[:, cut] = grad_pre
        sum_in_ref[0:1, cut] += column_sum(grad_pre.astype(f32))
        if held is not None:
            grad_hidden = grad_hidden + dot_nt(held, weights.into(c - 1))
        held = grad_pre
    grad_hidden = grad_hidden + dot_nt(held, weights.into(last))

    grad_r1 = normalise_back(grad_hidden * gain_a, normed_a, scale_a)
    gr1_ref[...] = grad_r1
    grad_branch = grad_r1.astype(bf16)
    gb_ref[...] = grad_branch
    sum_ref[3:4, :] += column_sum(grad_hidden * normed_a)
    sum_ref[4:5, :] += column_sum(grad_hidden)
    sum_ref[5:6, :] += column_sum(grad_branch.astype(f32))
    grad_attn = dot_nt(grad_branch, weights.out()).astype(bf16)
    do_ref[...] = grad_attn
    doT_ref[...] = grad_attn.T


def held(shape, index):
    return pl.BlockSpec(shape, lambda *_: index, pipeline_mode=pl.Buffered(1))


def dense(side, attn, x, mine, other, weights, vectors, bias_in, block):
    rows, half, width = other.shape
    tokens = 2 * rows * half
    inner = bias_in.shape[1]
    block = min(block, half)
    blocks = half // block
    mine_at, other_at = halves(mine, other, block)

    def at(r, h, b, s):
        return ((r * 2 + h) * blocks + b, 0)

    narrow = pl.BlockSpec((block, width), at)
    wide = pl.BlockSpec((block, inner), at)

    return pl.pallas_call(
        dense_kernel,
        grid_spec=pltpu.PrefetchScalarGridSpec(
            num_scalar_prefetch=1,
            grid=(rows, 2, blocks),
            in_specs=[
                pl.BlockSpec((width, block), lambda *i: (0, at(*i)[0])),
                narrow,
                pl.BlockSpec((block, width), mine_at),
                pl.BlockSpec((block, width), other_at),
            ]
            + [held(shape, index) for _, shape, index in weights]
            + [held(vectors.shape, (0, 0)), held(bias_in.shape, (0, 0))],
            out_specs=[
                pl.BlockSpec((block, width), mine_at),
                pl.BlockSpec((block, width), other_at),
                wide, wide, narrow, narrow, narrow, narrow, narrow,
                pl.BlockSpec((width, block), lambda *i: (0, at(*i)[0])),
                pl.BlockSpec((8, width), lambda *_: (0, 0)),
                pl.BlockSpec((8, inner), lambda *_: (0, 0)),
            ],
            scratch_shapes=[pltpu.VMEM((block, inner), bf16)],
        ),
        out_shape=[
            shape_of((mine.shape[0] * half, width), bf16),
            shape_of((rows * half, width), bf16),
            shape_of((tokens, inner), bf16),
            shape_of((tokens, inner), bf16),
            shape_of((tokens, width), bf16),
            shape_of((tokens, width), bf16),
            shape_of((tokens, width), f32),
            shape_of((tokens, width), bf16),
            shape_of((tokens, width), bf16),
            shape_of((width, tokens), bf16),
            shape_of((8, width), f32),
            shape_of((8, inner), f32),
        ],
        compiler_params=pltpu.CompilerParams(vmem_limit_bytes=VMEM_LIMIT),
        cost_estimate=cost(
            flops=2 * tokens * width * (2 * width + 4 * inner),
            bytes_accessed=tokens * (22 * width + 4 * inner) + 4 * width * inner,
            transcendentals=2 * tokens * inner,
        ),
        name="dense",
    )(
        side, attn, x, mine.reshape(-1, width), other.reshape(-1, width),
        *[array for array, _, _ in weights], vectors, bias_in,
    )


def share(place_ref, blocks, keep, send):
    core = lax.rem(place_ref[1], 2)

    @pl.when(core == 0)
    def _():
        keep(blocks[:, 0])
        send(blocks[:, 1])

    @pl.when(core == 1)
    def _():
        keep(blocks[:, 1])
        send(blocks[:, 0])


def store(ref, *at):
    def body(value):
        ref[at if at else ...] = value

    return body


def split_product_kernel(place_ref, a_ref, b_ref, keep_ref, send_ref):
    made = dot_tn(a_ref[...], b_ref[...]).astype(bf16)
    made = made.reshape((keep_ref.shape[0], 2) + keep_ref.shape[1:])
    share(place_ref, made, store(keep_ref), store(send_ref))


def split_product(place, a, b, shards):
    tokens, width = a.shape
    steps = b.shape[1] // width
    shard = width // shards
    out = pl.BlockSpec((shards // 2, shard, width), lambda i, s: (0, i, 0))
    return pl.pallas_call(
        split_product_kernel,
        grid_spec=pltpu.PrefetchScalarGridSpec(
            num_scalar_prefetch=1,
            grid=(steps,),
            in_specs=[
                pl.BlockSpec((tokens, width), lambda i, s: (0, 0), pipeline_mode=pl.Buffered(1)),
                pl.BlockSpec((tokens, width), lambda i, s: (0, i)),
            ],
            out_specs=[out] * 2,
        ),
        out_shape=[shape_of((shards // 2, steps * shard, width), bf16)] * 2,
        compiler_params=pltpu.CompilerParams(vmem_limit_bytes=VMEM_LIMIT),
        cost_estimate=cost(
            flops=2 * tokens * width * b.shape[1],
            bytes_accessed=2 * (a.size + b.size + width * b.shape[1]),
        ),
        name="split_product",
    )(place, a, b)


def pair_product_kernel(a_ref, b_ref, cT_ref, d_ref, out_ref):
    groups, rows, width = out_ref.shape
    first = a_ref.shape[1] // groups
    made = dot_tn(a_ref[...], b_ref[...]).astype(bf16)
    out_ref[:, :first, :] = made.reshape(groups, first, width)
    made = dot(cT_ref[...], d_ref[...]).astype(bf16)
    out_ref[:, first:, :] = made.reshape(groups, rows - first, width)


def pair_product(a, b, cT, d, shards):
    tokens, width = b.shape
    steps = a.shape[1] // width
    rows = (a.shape[1] + cT.shape[0]) // shards
    still = {"index_map": lambda i: (0, 0), "pipeline_mode": pl.Buffered(1)}
    return pl.pallas_call(
        pair_product_kernel,
        grid=(steps,),
        in_specs=[
            pl.BlockSpec((tokens, width), lambda i: (0, i)),
            pl.BlockSpec((tokens, width), **still),
            pl.BlockSpec((cT.shape[0] // steps, tokens), lambda i: (i, 0)),
            pl.BlockSpec((tokens, width), **still),
        ],
        out_specs=pl.BlockSpec((shards // steps, rows, width), lambda i: (i, 0, 0)),
        out_shape=shape_of((shards, rows, width), bf16),
        compiler_params=pltpu.CompilerParams(vmem_limit_bytes=VMEM_LIMIT),
        cost_estimate=cost(
            flops=2 * tokens * width * (a.shape[1] + cT.shape[0]),
            bytes_accessed=2 * (a.size + b.size + cT.size + d.size + shards * rows * width),
        ),
        name="pair_product",
    )(a, b, cT, d)


def input_grad_kernel(side_ref, g_ref, gr1_ref, w_ref, keep_ref, send_ref):
    width = send_ref.shape[1]
    total = gr1_ref[...] + dot_nt(g_ref[...], w_ref[:, : 3 * width])
    low = total.astype(bf16)
    own = pl.program_id(1) == side_ref[0]

    @pl.when(own)
    def _():
        keep_ref[...] = low

    @pl.when(jnp.logical_not(own))
    def _():
        send_ref[...] = low


def input_grad(side, grad_qkv, grad_r1, weight, mine, other, block):
    rows, half, width = other.shape
    block = min(block, half)
    blocks = half // block
    mine_at, other_at = halves(mine, other, block)

    def at(r, h, b, s):
        return ((r * 2 + h) * blocks + b, 0)

    keep, send = pl.pallas_call(
        input_grad_kernel,
        grid_spec=pltpu.PrefetchScalarGridSpec(
            num_scalar_prefetch=1,
            grid=(rows, 2, blocks),
            in_specs=[
                pl.BlockSpec((block, grad_qkv.shape[1]), at),
                pl.BlockSpec((block, width), at),
                pl.BlockSpec(weight.shape, lambda *_: (0, 0), pipeline_mode=pl.Buffered(1)),
            ],
            out_specs=[
                pl.BlockSpec((block, width), mine_at),
                pl.BlockSpec((block, width), other_at),
            ],
        ),
        out_shape=[shape_of((v.shape[0] * half, width), bf16) for v in (mine, other)],
        compiler_params=pltpu.CompilerParams(vmem_limit_bytes=VMEM_LIMIT),
        cost_estimate=cost(
            flops=12 * rows * half * width * width,
            bytes_accessed=24 * rows * half * width + 6 * width * width,
            transcendentals=0,
        ),
        name="input_grad",
    )(side, grad_qkv, grad_r1, weight)
    return keep.reshape(mine.shape), send.reshape(other.shape)


def vector_block(sums_ref, sums_in_ref, sums_qv_ref, shards):
    qv = jnp.concatenate([sums_qv_ref[j : j + 1, :] for j in range(2)], axis=1)
    rows = [sums_ref[j : j + 1, :] for j in range(6)]
    found = []
    for v in (qv, rows[5], rows[3], rows[4], sums_in_ref[0:1, :], rows[2], rows[0], rows[1]):
        found.extend(gather_vector(v, shards))
    return [v.astype(bf16) for v in found]


def last_product_kernel(place_ref, a_ref, b_ref, *refs, shards):
    keep_ref, send_ref = refs[-2:]
    at = pl.program_id(0)
    width = a_ref.shape[1]
    shard = width // shards
    made = dot_tn(a_ref[...], b_ref[...]).astype(bf16)
    here = (slice(None), pl.ds(pl.multiple_of(at * shard, 16), shard), slice(None))
    made = made.reshape(shards // 2, 2, shard, width)
    share(place_ref, made, store(keep_ref, *here), store(send_ref, *here))

    @pl.when(at == pl.num_programs(0) - 1)
    def _():
        end = keep_ref.shape[1] - 16
        for ref in (keep_ref, send_ref):
            ref[:, end:, :] = jnp.zeros((shards // 2, 16, width), bf16)
        for j, v in enumerate(vector_block(*refs[:3], shards)):
            here = (slice(None), slice(end + j, end + j + 1), slice(0, LANES))
            v = v.reshape(shards // 2, 2, 1, LANES)
            share(place_ref, v, store(keep_ref, *here), store(send_ref, *here))


def last_product(place, a, b, sums, shards):
    tokens, width = a.shape
    steps = b.shape[1] // width
    shard = width // shards
    out = (shards // 2, steps * shard + 16, width)
    return pl.pallas_call(
        functools.partial(last_product_kernel, shards=shards),
        grid_spec=pltpu.PrefetchScalarGridSpec(
            num_scalar_prefetch=1,
            grid=(steps,),
            in_specs=[
                pl.BlockSpec((tokens, width), lambda i, s: (0, 0), pipeline_mode=pl.Buffered(1)),
                pl.BlockSpec((tokens, width), lambda i, s: (0, i)),
            ]
            + [pl.BlockSpec(v.shape, lambda i, s: (0, 0)) for v in sums],
            out_specs=[pl.BlockSpec(out, lambda i, s: (0, 0, 0))] * 2,
        ),
        out_shape=[shape_of(out, bf16)] * 2,
        compiler_params=pltpu.CompilerParams(vmem_limit_bytes=VMEM_LIMIT),
        cost_estimate=cost(
            flops=2 * tokens * width * b.shape[1],
            bytes_accessed=2 * (a.size + b.size + width * b.shape[1]),
            transcendentals=0,
        ),
        name="last_product",
    )(place, a, b, *sums)


def split_heads(values):
    return values.reshape(values.shape[0], values.shape[1], H, HD)


def gathered_probs(queries, keys, allowed):
    scores = jnp.einsum("rqhd,rkhd->rhqk", queries, keys, preferred_element_type=f32)
    return jax.nn.softmax(jnp.where(allowed, scores * SCORE_SCALE, MASKED), axis=-1)


def attend_gathered(bounds, qkv, rows, seq_index):
    width = qkv.shape[1] // 3
    parts = qkv.reshape(rows, -1, 3 * width)
    tok_seq = parts.shape[1]
    whole = lax.all_gather(parts[:, :, width:], "seq", axis=1, tiled=True)
    row_len = whole.shape[1]
    queries = split_heads(parts[:, :, :width])
    keys = split_heads(whole[:, :, :width])
    values = split_heads(whole[:, :, width:])
    positions = jnp.arange(row_len, dtype=jnp.int32)
    segments = jnp.sum((positions[None, :, None] >= bounds[:, None, :]).astype(jnp.int32), axis=2)
    mine = lax.dynamic_slice_in_dim(segments, seq_index * tok_seq, tok_seq, 1)
    allowed = mine[:, None, :, None] == segments[:, None, None, :]
    probs = gathered_probs(queries, keys, allowed)
    attended = jnp.einsum(
        "rhqk,rkhd->rqhd", probs.astype(bf16), values, preferred_element_type=f32
    )
    return attended.astype(bf16).reshape(-1, width), (queries, keys, values, allowed)


def attend_gathered_back(saved, attn, do):
    queries, keys, values, allowed = saved
    rows, tok_seq = queries.shape[:2]
    width = attn.shape[1]
    probs = gathered_probs(queries, keys, allowed)
    do = do.reshape(rows, tok_seq, H, HD)
    delta = jnp.sum(do.astype(f32) * attn.reshape(do.shape).astype(f32), axis=-1)
    grad_prob = jnp.einsum("rqhd,rkhd->rhqk", do, values, preferred_element_type=f32)
    grad_score = (probs * (grad_prob - delta.transpose(0, 2, 1)[..., None])).astype(bf16)
    dq = jnp.einsum("rhqk,rkhd->rqhd", grad_score, keys, preferred_element_type=f32) * SCORE_SCALE
    dk = (
        jnp.einsum("rhqk,rqhd->rkhd", grad_score, queries, preferred_element_type=f32)
        * SCORE_SCALE
    )
    dv = jnp.einsum("rhqk,rqhd->rkhd", probs.astype(bf16), do, preferred_element_type=f32)
    pair = jnp.concatenate([dk.reshape(rows, -1, width), dv.reshape(rows, -1, width)], axis=-1)
    pair = lax.psum_scatter(pair.astype(bf16), "seq", scatter_dimension=1, tiled=True)
    pair = pair.reshape(-1, 2 * width)
    dq = dq.astype(bf16).reshape(-1, width)
    dk, dv = pair[:, :width], pair[:, width:]
    sums = jnp.stack([jnp.sum(dq.astype(f32), axis=0), jnp.sum(dv.astype(f32), axis=0)])
    return jnp.concatenate([dq, dk, dv], axis=1), jnp.pad(sums, ((0, 6), (0, 0)))


def swapped(values):
    return lax.ppermute(values, "seq", [(0, 1), (1, 0)])


def other_half(values, seq_index):
    rows = values.shape[0] // 2
    return swapped(lax.dynamic_slice_in_dim(values, (1 - seq_index) * rows, rows, 0))


def placed(values, came, seq_index, row=0):
    at = (1 - seq_index) * (values.shape[0] // 2) + row
    return lax.dynamic_update_slice_in_dim(values, came, at, 0)


def coordinates(count):
    return ((2, 1), (count // 8, 2), (4, count // 4))


def turned(values, axis, size, stride, step):
    perm = []
    for i in range(lax.axis_size(axis)):
        at = (i // stride) % size
        perm.append((i, i + ((at + step) % size - at) * stride))
    return lax.ppermute(values, axis, perm)


class StagedSum:
    def __init__(self, keep, send, axis):
        self.axis = axis
        self.sizes = coordinates(lax.axis_size(axis))
        self.index = lax.axis_index(axis)
        self.own = keep
        size, stride = self.sizes[0]
        self.came = [turned(send, axis, size, stride, 1)]

    def sum(self, pick):
        total = pick(self.own).astype(f32)
        for values in self.came:
            total = total + pick(values).astype(f32)
        return total.astype(bf16)

    def step(self, at):
        size, stride = self.sizes[at]
        here = (self.index // stride) % size

        def part(step):
            def pick(values):
                blocks = values.reshape((-1, size) + values.shape[1:])
                return lax.dynamic_index_in_dim(blocks, (here + step) % size, 1, False)

            return self.sum(pick)

        came = [
            turned(part(step), self.axis, size, stride, step) for step in range(1, size)
        ]
        self.own, self.came = part(0), came

    def result(self):
        return self.sum(lambda values: values[0])


def tied(*values):
    return lax.optimization_barrier(values)


def gather_pieces(values, axis):
    pieces = [(values, (0, 0, 0))]
    for at, (size, stride) in reversed(list(enumerate(coordinates(lax.axis_size(axis))))):
        more = []
        for piece, back in pieces:
            for step in range(1, size):
                came = turned(piece, axis, size, stride, step)
                more.append((came, back[:at] + (step,) + back[at + 1 :]))
        pieces = pieces + more
    return pieces


def piece_owner(index, back, count):
    owner = jnp.int32(0)
    for (size, stride), step in zip(coordinates(count), back):
        owner = owner + lax.rem(lax.rem(index // stride, size) + (size - step), size) * stride
    return owner


def per_device(
    tokens,
    weight_qkv,
    bias_qv,
    weight_out,
    bias_out,
    gain_attn,
    shift_attn,
    weight_in,
    bias_in,
    weight_ffo,
    bias_ffo,
    gain_ffn,
    shift_ffn,
    lengths,
    cotangent,
):
    rows, tok_seq, width = tokens.shape
    seq_count = lax.axis_size("seq")
    seq_index = lax.axis_index("seq")
    shards = lax.axis_size("dp")
    shard = weight_qkv.shape[0]
    by_rows = seq_count == 2 and rows % 2 == 0 and shards % 8 == 0 and shard % 16 == 0
    inner = weight_in.shape[1]
    chunks = inner // width
    token_count = rows * tok_seq

    small = (bias_qv, bias_out, gain_attn, shift_attn, bias_in, bias_ffo, gain_ffn, shift_ffn)
    first, others = lower(weight_qkv, weight_in, weight_ffo, weight_out, small)
    if by_rows:
        first = gather_pieces(first, "dp")
        backs = [back for _, back in first]
    else:
        first = [(lax.all_gather(first, "dp", axis=0, tiled=True), None)]
    others = lax.all_gather(others[None], "dp", axis=0, tiled=True)
    if shard % 16 == 0:
        weights = (
            (others, (shards, shard, width), (0, 2 * chunks, 0)),
            (others, (shards, chunks * shard, width), (0, 0, 0)),
            (others, (shards, chunks * shard, width), (0, 1, 0)),
        )
    else:
        part = chunks * shard
        w_in = others[:, :part].reshape(shards, chunks, shard, width).transpose(1, 0, 2, 3)
        w_in = w_in.reshape(1, inner, width)
        w_ffo = others[:, part : 2 * part].reshape(1, inner, width)
        w_out = others[:, 2 * part :].reshape(1, width, width)
        weights = [(w, w.shape, (0, 0, 0)) for w in (w_out, w_in, w_ffo)]

    bounds = jnp.cumsum(lengths, axis=1)
    if by_rows:
        mine = rows // 2
        bounds = lax.dynamic_slice_in_dim(bounds, seq_index * mine, mine, 0)
        side = jnp.stack([seq_index, lax.axis_index("dp")]).astype(jnp.int32)
        x_other = other_half(tokens, seq_index)
        first, x_other, held_cot = tied([w for w, _ in first], x_other, cotangent)
        x_halves = tokens, x_other
        first = list(zip(first, backs))
        cot_halves = cotangent, other_half(held_cot, seq_index)
    else:
        mine = 1
        side = jnp.zeros((2,), jnp.int32)
        x_halves = tokens.reshape(2, 1, -1, width)
        cot_halves = cotangent.reshape(2, 1, -1, width)
    half = x_halves[1].shape[1]

    x, qkv, qkvT, w_qkv, vec, in_bias = project(side, *x_halves, first, inner, TALL)
    if by_rows:
        attnT, log = attend_rows(bounds, qkv, qkvT, BLOCK)
    else:
        attn, saved = attend_gathered(bounds, qkv, rows, seq_index)
        attnT = attn.T
    out, out_other, act, gp, gs, low, gr1, gb, do, doT, sums, sums_in = dense(
        side, attnT, x, *cot_halves, weights, vec, in_bias, TALL
    )
    out = out.reshape(-1, half, width)
    out_other = out_other.reshape(-1, half, width)
    part = chunks * shard
    if by_rows:
        out_other = swapped(out_other)
        g_in = split_product(side, low, gp, shards)
        *g_in, act = tied(*g_in, act)
        in_sum = StagedSum(*g_in, "dp")
        g_ffo = pair_product(act, gs, attnT, gb, shards)
    else:
        out = jnp.concatenate([out, out_other], axis=1).reshape(rows, tok_seq, width)
        g_ffo = dot_tn(act, gs).astype(bf16).reshape(shards, part, width)
        g_in = dot_tn(low, gp).astype(bf16).reshape(shards, shard, chunks, width)
        g_in = g_in.transpose(0, 2, 1, 3).reshape(shards, part, width)
        g_out = dot_tn(attn, gb).astype(bf16).reshape(shards, shard, width)
        g_ffo = jnp.concatenate([g_ffo, g_out], axis=1)
        g_in = lax.psum_scatter(g_in, "dp", scatter_dimension=0, tiled=True)[0]
    if by_rows:
        g_ffo, do, in_sum.came = tied(g_ffo, do, in_sum.came)
    g_ffo = lax.psum_scatter(g_ffo, "dp", scatter_dimension=0, tiled=True)[0]

    if by_rows:
        in_sum.step(1)
        g_x, sums_qv = attend_rows_back(bounds, qkv, qkvT, do, doT, attnT, log, 0, 1, BLOCK)
        g_x, out_other, in_sum.came = tied(g_x, out_other, in_sum.came)
        in_sum.step(2)
        g_qkv = last_product(side, x, g_x, (sums, sums_in, sums_qv), shards)
        g_qkv, gr1 = tied(g_qkv, gr1)
        qkv_sum = StagedSum(*g_qkv, "dp")
        grad_x, grad_other = input_grad(side, g_x, gr1, w_qkv, *x_halves, TALL)
        grad_other, qkv_sum.came = tied(grad_other, qkv_sum.came)
        qkv_sum.step(1)
        grad_other = [swapped(grad_other[r : r + 1]) for r in range(mine)]
        qkv_sum.came, in_sum.came, grad_other[0] = tied(
            qkv_sum.came, in_sum.came, grad_other[0]
        )
        qkv_sum.step(2)
        g_in = in_sum.result()
        both = swapped(jnp.concatenate([g_in, g_ffo], axis=0))
        g_qkv, both, grad_other = tied(qkv_sum.result(), both, grad_other)
        for r in range(mine):
            grad_x = placed(grad_x, grad_other[r], seq_index, r)
        out = placed(out, out_other, seq_index)
        g_in = g_in.astype(f32) + both[:part].astype(f32)
        g_ffo = g_ffo.astype(f32) + both[part:].astype(f32)
        g_qkv = g_qkv.astype(f32) + swapped(g_qkv).astype(f32)
    else:
        g_x, sums_qv = attend_gathered_back(saved, attn, do)
        vectors = []
        for v in (sums_qv[:2].reshape(-1), sums[5], sums[3], sums[4], sums_in[0], sums[2], sums[0], sums[1]):
            v = v.reshape(shards, -1)
            vectors.append(jnp.pad(v, ((0, 0), (0, -v.shape[1] % LANES))).reshape(shards, -1, LANES))
        vectors = jnp.concatenate(vectors, axis=1).astype(bf16)
        vectors = jnp.pad(vectors, ((0, 0), (0, 16 - vectors.shape[1]), (0, width - LANES)))
        g_qkv = dot_tn(x, g_x).astype(bf16).reshape(shards, shard, 3, width)
        g_qkv = g_qkv.transpose(0, 2, 1, 3).reshape(shards, 3 * shard, width)
        g_qkv = jnp.concatenate([g_qkv, vectors], axis=1)
        g_qkv = lax.psum_scatter(g_qkv, "dp", scatter_dimension=0, tiled=True)[0]
        grad_x, grad_other = input_grad(side, g_x, gr1, w_qkv, *x_halves, TALL)
        grad_x = jnp.concatenate([grad_x, grad_other], axis=1).reshape(rows, tok_seq, width)
        g_ffo, g_in, g_qkv = [lax.psum(v, "seq").astype(f32) for v in (g_ffo, g_in, g_qkv)]
    vectors = g_qkv[3 * shard :, :LANES]
    d_qkv = jnp.concatenate([g_qkv[j * shard : (j + 1) * shard] for j in range(3)], axis=1)
    d_ffo, d_out = g_ffo[:part], g_ffo[part:]
    d_in = jnp.concatenate([g_in[c * shard : (c + 1) * shard] for c in range(chunks)], axis=1)
    sizes = [v.shape[0] for v in small]
    d_small = []
    for row, size in zip(vector_rows(sizes)[0], sizes):
        d_small.append(vectors[row : row - (-size // LANES)].reshape(-1)[:size])
    g_qv, g_bo, g_ga, g_sa, g_bi, g_bf, g_gf, g_sf = d_small
    return (
        out, grad_x, d_qkv, g_qv, d_out, g_bo, g_ga, g_sa, d_in, g_bi, d_ffo,
        g_bf, g_gf, g_sf,
    )


def solution(mesh):
    by_token = P("dp", "seq", None)
    weight = P("dp", None)
    vector = P("dp")
    params = (
        weight, vector, weight, vector, vector, vector, weight, vector, weight, vector, vector,
        vector,
    )
    return jax.shard_map(
        per_device,
        mesh=mesh,
        in_specs=(by_token,) + params + (weight, by_token),
        out_specs=(by_token, by_token) + params,
        check_vma=False,
    )
```
